128 devices in a mesh: ens: 4 (over y), tile: 32 (over z, x, core).
Axes of the slice: x: 4, y: 4, z: 4, core: 2. Of those that a mesh axis runs over, the one named last changes fastest.
Arguments:
- perturbations: bfloat16 [32, 64, 32768], P('ens', None, 'tile'), may hold values from -6 to 6
- control: float32 [32, 64, 32768], P('ens', None, 'tile'), may hold values from -6 to 6
- loc_vertical: float32 [64, 64], replicated, may hold values from -0.75 to 0.75
- loc_horizontal: bfloat16 [1024, 1024], replicated, may hold values from -0.1875 to 0.1875
- obs_weight: bfloat16 [32768, 128, 128], P(('ens', 'tile')), may hold values from -0.5 to 0.5
- obs_vertical: float32 [32768, 64, 128], P(('ens', 'tile')), may hold values from -0.75 to 0.75
- innovation: float32 [32768, 128], P(('ens', 'tile')), may hold values from -6 to 6
- obs_precision: float32 [32768, 128], P(('ens', 'tile')), may hold values from 0.25 to 4
- block_column: int32 [32768], P(('ens', 'tile')), may hold values from 0 to 7
- tile_count: int32 [4096], P(('ens', 'tile')), may hold values from 7 to 8, as said below
Outputs:
- gradient: float32 [32, 64, 32768], P('ens', None, 'tile')
The draws below stay inside these ranges and needn't reach their ends.
Inputs may be any that keep to these rules, and one draw needn't show every extreme that they name: For each destination tile the first tile_count entries of a device's 8 slots for that tile are live and the rest are padding; at most 8 blocks go from one device to one tile, and for every ens index some tile receives 8 from every device.
All inputs are finite; a program needn't handle non-finite values.
Results may differ from the reference program's by a relative error of at most 0.013.
Values may be sent and summed in bfloat16 or wider, within the bound.
A program may use at most 128 MiB of HBM per device.

```python
import math
import jax
import jax.numpy as jnp
from jax import lax

LEV = 64
BLK = 128
CB_DEV = 8
CAP = 8
MEMBERS = 32
COL_DEV = 1024
NCOL = 32768
OBS_SLOTS = 32768
N_ENS = 4
N_TILE = 32


def draw_tile_count(key, part):
    key = jax.random.fold_in(key, 11)
    key_forced = jax.random.fold_in(key, 2)
    key_counts = jax.random.fold_in(key, 3)
    forced = jax.random.randint(key_forced, (N_ENS, 1, 1), 0, N_TILE)
    positions = jnp.arange(N_TILE, dtype=jnp.int32).reshape(1, 1, N_TILE)
    is_forced = positions == forced
    dropped = jax.random.randint(key_counts, (N_ENS, N_TILE, N_TILE), 0, 2)
    counts = CAP - dropped
    counts = jnp.where(is_forced, CAP, counts)
    return counts.reshape(-1).astype(jnp.int32)


def with_ends(values, key, least, top_value):
    longest = values.shape.index(max(values.shape))
    spots = []
    for shift in (0, 1):
        where = [jax.random.randint(jax.random.fold_in(key, axis), (), 0, length) for axis, length in enumerate(values.shape)]
        where[longest] = (where[longest] + shift) % values.shape[longest]
        spots.append(tuple(where))
    return values.at[spots[0]].set(least).at[spots[1]].set(top_value)


def block_levels(stream_key, extent, split, low, largest):
    level = 1.0
    for axis_at, blocks in split:
        draws = jax.random.uniform(jax.random.fold_in(jax.random.fold_in(stream_key, 6), axis_at), (blocks,), jnp.float32, low / len(split), largest / len(split))
        level = level * jnp.repeat(jnp.exp(draws), extent[axis_at] // blocks).reshape((-1,) + (1,) * (len(extent) - 1 - axis_at))
    return level


def gaussian(own_key, extent, scale, most, split=(), kind=jnp.bfloat16):
    level = block_levels(own_key, extent, split, -0.22, 0.18) if split else 1.0
    values = jax.random.normal(own_key, extent, jnp.float32) * scale * level
    return jnp.minimum(jnp.maximum(values, -most), most).astype(kind)


def setup_inputs(seed: int = 0) -> dict:
    streams_of = jax.random.split(jax.random.key(seed), 11)
    return {
        "perturbations": gaussian(streams_of[0], (MEMBERS, LEV, NCOL), 1.0, 6.0, ((0, 4), (2, 32))),
        "control": gaussian(streams_of[1], (MEMBERS, LEV, NCOL), 1.0, 6.0, ((0, 4), (2, 32)), jnp.float32),
        "loc_vertical": gaussian(streams_of[2], (LEV, LEV), LEV ** -0.5, 0.75, (), jnp.float32),
        "loc_horizontal": gaussian(streams_of[3], (COL_DEV, COL_DEV), COL_DEV ** -0.5, 0.1875),
        "obs_weight": gaussian(streams_of[4], (OBS_SLOTS, BLK, BLK), BLK ** -0.5, 0.5, ((0, 128),)),
        "obs_vertical": gaussian(streams_of[5], (OBS_SLOTS, LEV, BLK), LEV ** -0.5, 0.75, ((0, 128),), jnp.float32),
        "innovation": gaussian(streams_of[6], (OBS_SLOTS, BLK), 1.0, 6.0, ((0, 128),), jnp.float32),
        "obs_precision": jnp.clip(jnp.exp(math.log(4.0) - 2.7725887 * jax.random.uniform(streams_of[7], (OBS_SLOTS, BLK), jnp.float32) ** block_levels(streams_of[7], (OBS_SLOTS, BLK), ((0, 128),), -0.2, 0.2)), 0.25, 4.0),
        "block_column": with_ends(jax.random.randint(streams_of[8], (OBS_SLOTS,), 0, CB_DEV), jax.random.fold_in(streams_of[8], 1), 0, CB_DEV - 1).astype(jnp.int32),
        "tile_count": draw_tile_count(jax.random.fold_in(streams_of[10], 71), 0),
    }


def reference(perturbations, control, loc_vertical, loc_horizontal, obs_weight, obs_vertical, innovation, obs_precision, block_column, tile_count):
    factor = 1.0 / math.sqrt(MEMBERS - 1)
    vertical = jnp.einsum('ml,klc->kmc', loc_vertical, control, precision=lax.Precision.HIGHEST).astype(jnp.bfloat16)
    spread = jnp.dot(vertical.reshape(MEMBERS * LEV * N_TILE, COL_DEV), loc_horizontal, preferred_element_type=jnp.float32).reshape(MEMBERS, LEV, NCOL)
    increment = lax.optimization_barrier(jnp.sum(perturbations.astype(jnp.float32) * spread, axis=0)) * factor
    state = increment.astype(jnp.bfloat16)
    state_blocks = state.reshape(LEV, N_TILE * CB_DEV, BLK)
    per_device = N_TILE * CAP
    slot_index = jnp.arange(per_device, dtype=jnp.int32)
    target = (slot_index // CAP).astype(jnp.int32)
    sources = N_ENS * N_TILE

    def one_device(adj_total, inputs):
        weights, vert_w, innov, precision_w, column_ids, counts = inputs
        active = slot_index % CAP < counts[target]
        chosen = (target * CB_DEV + column_ids).astype(jnp.int32)
        blocks = jnp.take(state_blocks, chosen, axis=1).astype(jnp.float32)
        wide = weights.astype(jnp.float32)
        projected = jnp.einsum('soc,lsc->slo', wide, blocks, precision=lax.Precision.HIGHEST)
        model_obs = lax.optimization_barrier(jnp.sum(vert_w * projected, axis=1))
        departure = jnp.where(active[:, None], precision_w * (model_obs - innov), jnp.float32(0.0))
        weighted = lax.optimization_barrier((vert_w * departure[:, None, :]).astype(jnp.bfloat16)).astype(jnp.float32)
        adj_blocks = jnp.einsum('soc,slo->lsc', wide, weighted, precision=lax.Precision.HIGHEST)
        adj_total = adj_total.at[:, chosen, :].add(adj_blocks)
        return (adj_total, None)
    inputs = (obs_weight.reshape(sources, per_device, BLK, BLK), obs_vertical.reshape(sources, per_device, LEV, BLK), innovation.reshape(sources, per_device, BLK), obs_precision.reshape(sources, per_device, BLK), block_column.reshape(sources, per_device), tile_count.reshape(sources, N_TILE))
    start = jnp.zeros((LEV, N_TILE * CB_DEV, BLK), jnp.float32)
    adj_total, unused = lax.scan(one_device, start, inputs)
    adjoint = adj_total.reshape(LEV, NCOL)
    product_field = perturbations.astype(jnp.float32) * adjoint[None]
    back_vertical = jnp.einsum('ml,kmc->klc', loc_vertical, product_field, precision=lax.Precision.HIGHEST).astype(jnp.bfloat16)
    spread_back = jnp.dot(back_vertical.reshape(MEMBERS * LEV * N_TILE, COL_DEV), loc_horizontal.T, preferred_element_type=jnp.float32).reshape(MEMBERS, LEV, NCOL)
    return control + factor * spread_back
```

```python
import math

import jax
import jax.numpy as jnp
from jax import lax
from jax.experimental import pallas as pl
from jax.experimental.pallas import tpu as pltpu
from jax.sharding import PartitionSpec as P

MESH = pl.DeviceIdType.MESH
F32 = jnp.float32
BF16 = jnp.bfloat16
SIDE = 4
LOADS = 8


def tile_of(z, x, c):
    return (z * SIDE + x) * 2 + c


def flat(part, c, hi, lo):
    return ((part * 2 + c) * SIDE + hi) * SIDE + lo


def exchange_kernel(
    block_ref,
    count_ref,
    prev_ref,
    last_ref,
    partial_ref,
    innov_ref,
    prec_ref,
    weight_hbm,
    vertical_hbm,
    out_ref,
    weight,
    vertical,
    sendy,
    recvy,
    state,
    chain,
    adj,
    core_in,
    total,
    half_in,
    row_in,
    plane,
    plane_in,
    unit,
    unit_b,
    unit_in,
    final,
    load_sem,
    ssem,
    rsem,
):
    e = lax.axis_index("ens")
    t = lax.axis_index("tile")
    c = t % 2
    x = (t // 2) % SIDE
    z = t // (2 * SIDE)

    slots = weight.shape[0]
    chunk = slots // LOADS
    loads = []
    for i in range(LOADS):
        at = pl.ds(i * chunk, chunk)
        for n, (src, dst) in enumerate(((weight_hbm, weight), (vertical_hbm, vertical))):
            loads.append(pltpu.make_async_copy(src.at[at], dst.at[at], load_sem.at[2 * i + n]))
    for load in loads:
        load.start()

    def along(axis, q):
        if axis == "y":
            return ((e + q) % SIDE, t)
        if axis == "x":
            return (e, tile_of(z, (x + q) % SIDE, c))
        if axis == "z":
            return (e, tile_of((z + q) % SIDE, x, c))
        return (e, tile_of(z, x, 1 - c))

    barrier = pltpu.get_barrier_semaphore()
    for axis in ("x", "y", "z"):
        for q in (1, 2, 3):
            pl.semaphore_signal(barrier, inc=1, device_id=along(axis, q), device_id_type=MESH)
    pl.semaphore_signal(barrier, inc=1, device_id=along("core", 1), device_id_type=MESH)
    pl.semaphore_wait(barrier, 10)

    used = [0]
    started = []

    def send(src, dst, axis, q=1):
        n = used[0]
        used[0] = n + 1
        copy = pltpu.make_async_remote_copy(
            src_ref=src,
            dst_ref=dst,
            send_sem=ssem.at[n],
            recv_sem=rsem.at[n],
            device_id=along(axis, q),
            device_id_type=MESH,
        )
        copy.start()
        started.append(copy)
        return copy

    hi_axis = ("z", "x")
    lo_axis = ("x", "z")
    hi = (z, x)
    lo = (x, z)

    for k in range(8):
        sendy[k] = partial_ref[:, k * 128 : (k + 1) * 128].astype(BF16)
    copies = []
    for q in (1, 2, 3):
        other = (e + q) % SIDE
        copies.append(send(sendy.at[pl.ds(2 * other, 2)], recvy.at[q - 1], "y", q))
    for copy in copies:
        copy.wait_recv()
    mine = jnp.where(e // 2 == 0, flat(0, c, z, x), flat(1, c, x, z)) * 4 + 2 * (e % 2)
    for h in range(2):
        own = partial_ref[:, pl.ds(pl.multiple_of(e * 256 + h * 128, 128), 128)]
        for q in range(3):
            own = own + recvy[q, h].astype(F32)
        state[mine + h] = own.astype(BF16)

    copies = []
    for q in (1, 2, 3):
        piece = state.at[pl.ds(mine, 2)]
        copies.append(send(piece, piece, "y", q))
    for copy in copies:
        copy.wait_recv()
    copies = []
    for p in (0, 1):
        piece = state.at[pl.ds(flat(p, c, hi[p], lo[p]) * 4, 4)]
        for q in (1, 3, 2):
            copies.append(send(piece, piece, lo_axis[p], q))
    rows = []
    cores = []

    def row_at(p, r, first=0, count=4):
        return state.at[pl.ds(flat(p, c, (hi[p] + r) % SIDE, first) * 4, count * 4)]

    for p in (0, 1):
        for q in range(3):
            copies[p * 3 + q].wait_recv()
        row = row_at(p, 0)
        rows.append([send(row, row, hi_axis[p], 1), send(row, row, hi_axis[p], 3)])
        cores.append(send(row, row, "core"))
    halves = []
    for p in (0, 1):
        rows[p][0].wait_recv()
        first = row_at(p, 3, 0, 2)
        one = send(first, first, hi_axis[p], 1)
        rows[p][1].wait_recv()
        second = row_at(p, 1, 2, 2)
        halves.append([one, send(second, second, hi_axis[p], 3)])
        for r in (3, 1):
            row = row_at(p, r)
            cores.append(send(row, row, "core"))
    for p in (0, 1):
        halves[p][0].wait_recv()
        halves[p][1].wait_recv()
        row = row_at(p, 2)
        cores.append(send(row, row, "core"))
    for copy in cores:
        copy.wait_recv()
    for load in loads:
        load.wait()

    chain[8] = jnp.zeros((64, 128), F32)

    def one_tile(j, carry):
        jc = j % 2
        jx = (j // 2) % SIDE
        jz = j // (2 * SIDE)
        f0 = flat(0, jc, jz, jx) * 4
        f1 = flat(1, jc, jx, jz) * 4 - 4
        base = pl.multiple_of(j * 8, 8)
        innov = innov_ref[pl.ds(base, 8), :]
        prec = prec_ref[pl.ds(base, 8), :]
        count = count_ref[j]
        for p in range(8):
            s = base + p
            k = block_ref[s]
            block = state[jnp.where(k < 4, f0, f1) + k]
            w = weight[s]
            v = vertical[s]
            projected = lax.dot_general(
                block, w, (((1,), (1,)), ((), ())), preferred_element_type=F32
            )
            model = jnp.sum(v * projected, axis=0, keepdims=True)
            dep = prec[p : p + 1] * (model - innov[p : p + 1])
            dep = jnp.where(p < count, dep, 0.0)
            weighted = (v * dep).astype(BF16)
            back = jnp.dot(weighted, w, preferred_element_type=F32)
            if p > 0:
                back = back + chain[prev_ref[s]]
            chain[p] = back
        for k in range(8):
            adj[(f0 if k < 4 else f1) + k] = chain[last_ref[base + k]].astype(BF16)
        return carry

    lax.fori_loop(0, 32, one_tile, 0)

    cores = []
    for r in (2, 1, 3, 0):
        for p in (0, 1):
            src = adj.at[pl.ds(flat(p, 1 - c, (hi[p] + r) % SIDE, 0) * 4, 16)]
            cores.append((p, r, send(src, core_in.at[pl.ds((p * 4 + r) * 16, 16)], "core")))
    halves = [None, None]
    for p, r, copy in cores:
        copy.wait_recv()
        src0 = flat(p, c, (hi[p] + r) % SIDE, 0) * 4
        dst0 = (p * 4 + r) * 16

        def add(i, carry):
            both = adj[src0 + i].astype(F32) + core_in[dst0 + i].astype(F32)
            total[dst0 + i] = both.astype(BF16)
            return carry

        lax.fori_loop(0, 16, add, 0)
        if r == 2:
            halves[p] = [
                send(total.at[pl.ds(dst0, 8)], half_in.at[pl.ds(p * 16, 8)], hi_axis[p], 1),
                send(total.at[pl.ds(dst0 + 8, 8)], half_in.at[pl.ds(p * 16 + 8, 8)], hi_axis[p], 3),
            ]
    rows = [None, None]
    for p in (0, 1):
        rows[p] = []
        for d, r in ((0, 1), (1, 3)):
            halves[p][d].wait_recv()
            dst0 = (p * 4 + r) * 16

            def add(i, carry):
                at = dst0 + 8 * d + i
                both = total[at].astype(F32) + half_in[p * 16 + 8 * d + i].astype(F32)
                total[at] = both.astype(BF16)
                return carry

            lax.fori_loop(0, 8, add, 0)
            rows[p].append(
                send(
                    total.at[pl.ds(dst0, 16)], row_in.at[pl.ds((p * 2 + d) * 16, 16)], hi_axis[p], r
                )
            )
    planes = [None, None]
    for p in (0, 1):
        rows[p][0].wait_recv()
        rows[p][1].wait_recv()

        def add(i, carry):
            three = (
                total[p * 64 + i].astype(F32)
                + row_in[p * 32 + i].astype(F32)
                + row_in[p * 32 + 16 + i].astype(F32)
            )
            plane[p * 16 + i] = three.astype(BF16)
            return carry

        lax.fori_loop(0, 16, add, 0)
        planes[p] = []
        for q in (1, 3, 2):
            src = plane.at[pl.ds(p * 16 + (lo[p] + q) % SIDE * 4, 4)]
            planes[p].append(
                send(src, plane_in.at[pl.ds((p * 3 + q - 1) * 4, 4)], lo_axis[p], q)
            )
    for p in (0, 1):
        for copy in planes[p]:
            copy.wait_recv()
        for i in range(4):
            both = plane[p * 16 + lo[p] * 4 + i].astype(F32)
            for q in range(3):
                both = both + plane_in[(p * 3 + q) * 4 + i].astype(F32)
            unit[p * 4 + i] = both
            unit_b[p * 4 + i] = both.astype(BF16)

    copies = []
    for q in (1, 2, 3):
        other = (e + q) % SIDE
        copies.append(send(unit_b.at[pl.ds(2 * other, 2)], unit_in.at[q - 1], "y", q))
    for copy in copies:
        copy.wait_recv()
    for h in range(2):
        both = unit[2 * e + h]
        for q in range(3):
            both = both + unit_in[q, h].astype(F32)
        final[2 * e + h] = both.astype(BF16)
    copies = []
    for q in (1, 2, 3):
        piece = final.at[pl.ds(2 * e, 2)]
        copies.append(send(piece, piece, "y", q))
    for copy in copies:
        copy.wait_recv()
    for k in range(8):
        out_ref[:, k * 128 : (k + 1) * 128] = final[k].astype(F32)
    for copy in started:
        copy.wait_send()


def exchange(partial_sum, innovation, obs_precision, obs_weight, obs_vertical, meta):
    levels, columns = partial_sum.shape
    slots, block, _ = obs_weight.shape
    smem = pl.BlockSpec(memory_space=pltpu.SMEM)
    vmem = pl.BlockSpec(memory_space=pltpu.VMEM)
    hbm = pl.BlockSpec(memory_space=pl.ANY)

    def blocks(*lead, dtype=BF16):
        return pltpu.VMEM((*lead, levels, block), dtype)

    return pl.pallas_call(
        exchange_kernel,
        out_shape=jax.ShapeDtypeStruct((levels, columns), F32),
        in_specs=[smem] * 4 + [vmem] * 3 + [hbm] * 2,
        out_specs=vmem,
        scratch_shapes=[
            pltpu.VMEM((slots, block, block), BF16),
            pltpu.VMEM((slots, levels, block), F32),
            blocks(8),
            blocks(3, 2),
            blocks(256),
            blocks(9, dtype=F32),
            blocks(256),
            blocks(128),
            blocks(128),
            blocks(32),
            blocks(64),
            blocks(32),
            blocks(24),
            blocks(8, dtype=F32),
            blocks(8),
            blocks(3, 2),
            blocks(8),
            pltpu.SemaphoreType.DMA((2 * LOADS,)),
            pltpu.SemaphoreType.DMA((64,)),
            pltpu.SemaphoreType.DMA((64,)),
        ],
        compiler_params=pltpu.CompilerParams(
            collective_id=0, has_side_effects=True, vmem_limit_bytes=48 * 1024 * 1024
        ),
    )(*meta, partial_sum, innovation, obs_precision, obs_weight, obs_vertical)


def on_device(
    perturbations,
    control,
    loc_vertical,
    loc_horizontal,
    obs_weight,
    obs_vertical,
    innovation,
    obs_precision,
    block_column,
    tile_count,
):
    members_dev, levels, columns = control.shape
    tile_total = lax.axis_size("tile")
    ens_total = lax.axis_size("ens")
    factor = 1.0 / math.sqrt(members_dev * ens_total - 1)
    vertical = jnp.einsum(
        "ml,klc->kmc", loc_vertical, control, precision=lax.Precision.HIGHEST
    ).astype(BF16)
    spread = jnp.dot(
        vertical.reshape(members_dev * levels, columns),
        loc_horizontal,
        preferred_element_type=F32,
    ).reshape(members_dev, levels, columns)
    partial_sum = jnp.sum(perturbations.astype(F32) * spread, axis=0) * factor

    slots = block_column.reshape(tile_total, 8)
    place = jnp.arange(8, dtype=jnp.int32)
    same = (slots[:, :, None] == slots[:, None, :]) & (place[:, None] > place[None, :])
    prev = jnp.max(jnp.where(same, place[None, None, :], -1), axis=2)
    prev = jnp.where(prev < 0, 8, prev).reshape(-1)
    holds = slots[:, None, :] == place[None, :, None]
    last = jnp.max(jnp.where(holds, place[None, None, :], -1), axis=2)
    last = jnp.where(last < 0, 8, last).reshape(-1)
    adjoint = exchange(
        partial_sum,
        innovation,
        obs_precision,
        obs_weight,
        obs_vertical,
        (block_column, tile_count, prev, last),
    )
    product_field = perturbations.astype(F32) * adjoint[None]
    back_vertical = jnp.einsum(
        "ml,kmc->klc", loc_vertical, product_field, precision=lax.Precision.HIGHEST
    ).astype(BF16)
    spread_back = jnp.einsum(
        "rc,dc->rd",
        back_vertical.reshape(members_dev * levels, columns),
        loc_horizontal,
        preferred_element_type=F32,
    )
    return control + factor * spread_back.reshape(members_dev, levels, columns)


def solution(mesh):
    in_specs = (
        P("ens", None, "tile"),
        P("ens", None, "tile"),
        P(),
        P(),
        P(("ens", "tile"), None, None),
        P(("ens", "tile"), None, None),
        P(("ens", "tile"), None),
        P(("ens", "tile"), None),
        P(("ens", "tile")),
        P(("ens", "tile")),
    )
    out_specs = P("ens", None, "tile")
    return jax.shard_map(
        on_device, mesh=mesh, in_specs=in_specs, out_specs=out_specs, check_vma=False
    )
```

```python
import math

import jax
import jax.numpy as jnp
from jax import lax
from jax.experimental import pallas as pl
from jax.experimental.pallas import tpu as pltpu
from jax.sharding import PartitionSpec as P

MESH = pl.DeviceIdType.MESH
F32 = jnp.float32
BF16 = jnp.bfloat16
SIDE = 4
LOADS = 8


def tile_of(z, x, c):
    return (z * SIDE + x) * 2 + c


def flat(part, c, hi, lo):
    return ((part * 2 + c) * SIDE + hi) * SIDE + lo


def exchange_kernel(
    block_ref,
    count_ref,
    prev_ref,
    last_ref,
    partial_ref,
    innov_ref,
    prec_ref,
    weight_hbm,
    vertical_hbm,
    out_ref,
    weight,
    vertical,
    sendy,
    recvy,
    state,
    chain,
    adj,
    core_in,
    total,
    half_in,
    row_in,
    plane,
    plane_in,
    unit,
    unit_b,
    unit_in,
    final,
    load_sem,
    ssem,
    rsem,
):
    e = lax.axis_index("ens")
    t = lax.axis_index("tile")
    c = t % 2
    x = (t // 2) % SIDE
    z = t // (2 * SIDE)

    slots = weight.shape[0]
    chunk = slots // LOADS
    loads = []
    for i in range(LOADS):
        at = pl.ds(i * chunk, chunk)
        for n, (src, dst) in enumerate(((weight_hbm, weight), (vertical_hbm, vertical))):
            loads.append(pltpu.make_async_copy(src.at[at], dst.at[at], load_sem.at[2 * i + n]))
    for load in loads:
        load.start()

    def along(axis, q):
        if axis == "y":
            return ((e + q) % SIDE, t)
        if axis == "x":
            return (e, tile_of(z, (x + q) % SIDE, c))
        if axis == "z":
            return (e, tile_of((z + q) % SIDE, x, c))
        return (e, tile_of(z, x, 1 - c))

    barrier = pltpu.get_barrier_semaphore()
    for axis in ("x", "y", "z"):
        for q in (1, 2, 3):
            pl.semaphore_signal(barrier, inc=1, device_id=along(axis, q), device_id_type=MESH)
    pl.semaphore_signal(barrier, inc=1, device_id=along("core", 1), device_id_type=MESH)
    pl.semaphore_wait(barrier, 10)

    used = [0]
    started = []

    def send(src, dst, axis, q=1):
        n = used[0]
        used[0] = n + 1
        copy = pltpu.make_async_remote_copy(
            src_ref=src,
            dst_ref=dst,
            send_sem=ssem.at[n],
            recv_sem=rsem.at[n],
            device_id=along(axis, q),
            device_id_type=MESH,
        )
        copy.start()
        started.append(copy)
        return copy

    hi_axis = ("z", "x")
    lo_axis = ("x", "z")
    hi = (z, x)
    lo = (x, z)

    for k in range(8):
        sendy[k] = partial_ref[:, k * 128 : (k + 1) * 128].astype(BF16)
    copies = []
    for q in (1, 2, 3):
        other = (e + q) % SIDE
        copies.append(send(sendy.at[pl.ds(2 * other, 2)], recvy.at[q - 1], "y", q))
    for copy in copies:
        copy.wait_recv()
    mine = jnp.where(e // 2 == 0, flat(0, c, z, x), flat(1, c, x, z)) * 4 + 2 * (e % 2)
    for h in range(2):
        own = partial_ref[:, pl.ds(pl.multiple_of(e * 256 + h * 128, 128), 128)]
        for q in range(3):
            own = own + recvy[q, h].astype(F32)
        state[mine + h] = own.astype(BF16)

    copies = []
    for q in (1, 2, 3):
        piece = state.at[pl.ds(mine, 2)]
        copies.append(send(piece, piece, "y", q))
    for copy in copies:
        copy.wait_recv()
    copies = []
    for p in (0, 1):
        piece = state.at[pl.ds(flat(p, c, hi[p], lo[p]) * 4, 4)]
        for q in (1, 3, 2):
            copies.append(send(piece, piece, lo_axis[p], q))
    rows = []
    cores = []

    def row_at(p, r, first=0, count=4):
        return state.at[pl.ds(flat(p, c, (hi[p] + r) % SIDE, first) * 4, count * 4)]

    for p in (0, 1):
        for q in range(3):
            copies[p * 3 + q].wait_recv()
        row = row_at(p, 0)
        rows.append([send(row, row, hi_axis[p], 1), send(row, row, hi_axis[p], 3)])
        cores.append(send(row, row, "core"))
    halves = []
    for p in (0, 1):
        rows[p][0].wait_recv()
        first = row_at(p, 3, 0, 2)
        one = send(first, first, hi_axis[p], 1)
        rows[p][1].wait_recv()
        second = row_at(p, 1, 2, 2)
        halves.append([one, send(second, second, hi_axis[p], 3)])
        for r in (3, 1):
            row = row_at(p, r)
            cores.append(send(row, row, "core"))
    for p in (0, 1):
        halves[p][0].wait_recv()
        halves[p][1].wait_recv()
        row = row_at(p, 2)
        cores.append(send(row, row, "core"))
    for copy in cores:
        copy.wait_recv()
    for load in loads:
        load.wait()

    chain[8] = jnp.zeros((64, 128), F32)

    def one_tile(j, carry):
        jc = j % 2
        jx = (j // 2) % SIDE
        jz = j // (2 * SIDE)
        f0 = flat(0, jc, jz, jx) * 4
        f1 = flat(1, jc, jx, jz) * 4 - 4
        base = pl.multiple_of(j * 8, 8)
        innov = innov_ref[pl.ds(base, 8), :]
        prec = prec_ref[pl.ds(base, 8), :]
        count = count_ref[j]
        projs = []
        for p in range(8):
            s = base + p
            k = block_ref[s]
            block = state[jnp.where(k < 4, f0, f1) + k]
            projs.append(lax.dot_general(
                block, weight[s], (((1,), (1,)), ((), ())), preferred_element_type=F32
            ))
        models = [jnp.sum(vertical[base + p] * projs[p], axis=0, keepdims=True) for p in range(8)]
        deps = []
        for p in range(8):
            dep = prec[p : p + 1] * (models[p] - innov[p : p + 1])
            deps.append(jnp.where(p < count, dep, 0.0))
        backs = []
        for p in range(8):
            weighted = (vertical[base + p] * deps[p]).astype(BF16)
            backs.append(jnp.dot(weighted, weight[base + p], preferred_element_type=F32))
        for p in range(8):
            back = backs[p]
            if p > 0:
                back = back + chain[prev_ref[base + p]]
            chain[p] = back
        for k in range(8):
            adj[(f0 if k < 4 else f1) + k] = chain[last_ref[base + k]].astype(BF16)
        return carry

    lax.fori_loop(0, 32, one_tile, 0)

    cores = []
    for r in (2, 1, 3, 0):
        for p in (0, 1):
            src = adj.at[pl.ds(flat(p, 1 - c, (hi[p] + r) % SIDE, 0) * 4, 16)]
            cores.append((p, r, send(src, core_in.at[pl.ds((p * 4 + r) * 16, 16)], "core")))
    halves = [None, None]
    for p, r, copy in cores:
        copy.wait_recv()
        src0 = flat(p, c, (hi[p] + r) % SIDE, 0) * 4
        dst0 = (p * 4 + r) * 16

        def add(i, carry):
            both = adj[src0 + i].astype(F32) + core_in[dst0 + i].astype(F32)
            total[dst0 + i] = both.astype(BF16)
            return carry

        lax.fori_loop(0, 16, add, 0)
        if r == 2:
            halves[p] = [
                send(total.at[pl.ds(dst0, 8)], half_in.at[pl.ds(p * 16, 8)], hi_axis[p], 1),
                send(total.at[pl.ds(dst0 + 8, 8)], half_in.at[pl.ds(p * 16 + 8, 8)], hi_axis[p], 3),
            ]
    rows = [None, None]
    for p in (0, 1):
        rows[p] = []
        for d, r in ((0, 1), (1, 3)):
            halves[p][d].wait_recv()
            dst0 = (p * 4 + r) * 16

            def add(i, carry):
                at = dst0 + 8 * d + i
                both = total[at].astype(F32) + half_in[p * 16 + 8 * d + i].astype(F32)
                total[at] = both.astype(BF16)
                return carry

            lax.fori_loop(0, 8, add, 0)
            rows[p].append(
                send(
                    total.at[pl.ds(dst0, 16)], row_in.at[pl.ds((p * 2 + d) * 16, 16)], hi_axis[p], r
                )
            )
    planes = [None, None]
    for p in (0, 1):
        rows[p][0].wait_recv()
        rows[p][1].wait_recv()

        def add(i, carry):
            three = (
                total[p * 64 + i].astype(F32)
                + row_in[p * 32 + i].astype(F32)
                + row_in[p * 32 + 16 + i].astype(F32)
            )
            plane[p * 16 + i] = three.astype(BF16)
            return carry

        lax.fori_loop(0, 16, add, 0)
        planes[p] = []
        for q in (1, 3, 2):
            src = plane.at[pl.ds(p * 16 + (lo[p] + q) % SIDE * 4, 4)]
            planes[p].append(
                send(src, plane_in.at[pl.ds((p * 3 + q - 1) * 4, 4)], lo_axis[p], q)
            )
    for p in (0, 1):
        for copy in planes[p]:
            copy.wait_recv()
        for i in range(4):
            both = plane[p * 16 + lo[p] * 4 + i].astype(F32)
            for q in range(3):
                both = both + plane_in[(p * 3 + q) * 4 + i].astype(F32)
            unit[p * 4 + i] = both
            unit_b[p * 4 + i] = both.astype(BF16)

    copies = []
    for q in (1, 2, 3):
        other = (e + q) % SIDE
        copies.append(send(unit_b.at[pl.ds(2 * other, 2)], unit_in.at[q - 1], "y", q))
    for copy in copies:
        copy.wait_recv()
    for h in range(2):
        both = unit[2 * e + h]
        for q in range(3):
            both = both + unit_in[q, h].astype(F32)
        final[2 * e + h] = both.astype(BF16)
    copies = []
    for q in (1, 2, 3):
        piece = final.at[pl.ds(2 * e, 2)]
        copies.append(send(piece, piece, "y", q))
    for copy in copies:
        copy.wait_recv()
    for k in range(8):
        out_ref[:, k * 128 : (k + 1) * 128] = final[k].astype(F32)
    for copy in started:
        copy.wait_send()


def exchange(partial_sum, innovation, obs_precision, obs_weight, obs_vertical, meta):
    levels, columns = partial_sum.shape
    slots, block, _ = obs_weight.shape
    smem = pl.BlockSpec(memory_space=pltpu.SMEM)
    vmem = pl.BlockSpec(memory_space=pltpu.VMEM)
    hbm = pl.BlockSpec(memory_space=pl.ANY)

    def blocks(*lead, dtype=BF16):
        return pltpu.VMEM((*lead, levels, block), dtype)

    return pl.pallas_call(
        exchange_kernel,
        out_shape=jax.ShapeDtypeStruct((levels, columns), F32),
        in_specs=[smem] * 4 + [vmem] * 3 + [hbm] * 2,
        out_specs=vmem,
        scratch_shapes=[
            pltpu.VMEM((slots, block, block), BF16),
            pltpu.VMEM((slots, levels, block), F32),
            blocks(8),
            blocks(3, 2),
            blocks(256),
            blocks(9, dtype=F32),
            blocks(256),
            blocks(128),
            blocks(128),
            blocks(32),
            blocks(64),
            blocks(32),
            blocks(24),
            blocks(8, dtype=F32),
            blocks(8),
            blocks(3, 2),
            blocks(8),
            pltpu.SemaphoreType.DMA((2 * LOADS,)),
            pltpu.SemaphoreType.DMA((64,)),
            pltpu.SemaphoreType.DMA((64,)),
        ],
        compiler_params=pltpu.CompilerParams(
            collective_id=0, has_side_effects=True, vmem_limit_bytes=48 * 1024 * 1024
        ),
    )(*meta, partial_sum, innovation, obs_precision, obs_weight, obs_vertical)


def on_device(
    perturbations,
    control,
    loc_vertical,
    loc_horizontal,
    obs_weight,
    obs_vertical,
    innovation,
    obs_precision,
    block_column,
    tile_count,
):
    members_dev, levels, columns = control.shape
    tile_total = lax.axis_size("tile")
    ens_total = lax.axis_size("ens")
    factor = 1.0 / math.sqrt(members_dev * ens_total - 1)
    vertical = jnp.einsum(
        "ml,klc->kmc", loc_vertical, control, precision=lax.Precision.HIGHEST
    ).astype(BF16)
    spread = jnp.dot(
        vertical.reshape(members_dev * levels, columns),
        loc_horizontal,
        preferred_element_type=F32,
    ).reshape(members_dev, levels, columns)
    partial_sum = jnp.sum(perturbations.astype(F32) * spread, axis=0) * factor

    slots = block_column.reshape(tile_total, 8)
    place = jnp.arange(8, dtype=jnp.int32)
    same = (slots[:, :, None] == slots[:, None, :]) & (place[:, None] > place[None, :])
    prev = jnp.max(jnp.where(same, place[None, None, :], -1), axis=2)
    prev = jnp.where(prev < 0, 8, prev).reshape(-1)
    holds = slots[:, None, :] == place[None, :, None]
    last = jnp.max(jnp.where(holds, place[None, None, :], -1), axis=2)
    last = jnp.where(last < 0, 8, last).reshape(-1)
    adjoint = exchange(
        partial_sum,
        innovation,
        obs_precision,
        obs_weight,
        obs_vertical,
        (block_column, tile_count, prev, last),
    )
    product_field = perturbations.astype(F32) * adjoint[None]
    back_vertical = jnp.einsum(
        "ml,kmc->klc", loc_vertical, product_field, precision=lax.Precision.HIGHEST
    ).astype(BF16)
    spread_back = jnp.einsum(
        "rc,dc->rd",
        back_vertical.reshape(members_dev * levels, columns),
        loc_horizontal,
        preferred_element_type=F32,
    )
    return control + factor * spread_back.reshape(members_dev, levels, columns)


def solution(mesh):
    in_specs = (
        P("ens", None, "tile"),
        P("ens", None, "tile"),
        P(),
        P(),
        P(("ens", "tile"), None, None),
        P(("ens", "tile"), None, None),
        P(("ens", "tile"), None),
        P(("ens", "tile"), None),
        P(("ens", "tile")),
        P(("ens", "tile")),
    )
    out_specs = P("ens", None, "tile")
    return jax.shard_map(
        on_device, mesh=mesh, in_specs=in_specs, out_specs=out_specs, check_vma=False
    )
```

```python
import math

import jax
import jax.numpy as jnp
from jax import lax
from jax.experimental import pallas as pl
from jax.experimental.pallas import tpu as pltpu
from jax.sharding import PartitionSpec as P

MESH = pl.DeviceIdType.MESH
F32 = jnp.float32
BF16 = jnp.bfloat16
SIDE = 4
LOADS = 4


def tile_of(z, x, c):
    return (z * SIDE + x) * 2 + c


ORDER = (
    (0, 0), (0, 1), (0, 3), (3, 0), (1, 0), (0, 2), (3, 1), (1, 1),
    (3, 3), (1, 3), (3, 2), (1, 2), (2, 0), (2, 1), (2, 3), (2, 2),
)
ARRIVE = {
    1: ((0, 3), (0, 1), (3, 0), (1, 0)),
    3: ((0, 2),),
    5: ((3, 1), (1, 1)),
    7: ((3, 3), (1, 3)),
    9: ((3, 2), (1, 2)),
    11: ((2, 0),),
    12: ((2, 1),),
    13: ((2, 3),),
    14: ((2, 2),),
}
STEP_OF = {place: i for i, place in enumerate(ORDER)}
STEPS = len(ORDER)
LATE = (0, 1, 3, 2)


def exchange_kernel(
    block_ref,
    count_ref,
    prev_ref,
    last_ref,
    partial_ref,
    innov_ref,
    prec_ref,
    weight_hbm,
    vertical_hbm,
    out_ref,
    *scratch,
):
    rest = list(scratch)
    own = [[rest.pop(0) for _ in range(4)] for _ in range(4)]
    other = [[rest.pop(0) for _ in range(4)] for _ in range(4)]
    (
        weight,
        turned,
        vertical,
        sendy,
        recvy,
        picked,
        chain,
        adj_own,
        adj_other,
        core_in,
        total,
        half_in,
        row_in,
        plane,
        plane_in,
        unit,
        unit_b,
        unit_in,
        final,
        load_sem,
        ssem,
        rsem,
    ) = rest

    e = lax.axis_index("ens")
    t = lax.axis_index("tile")
    c = t % 2
    x = (t // 2) % SIDE
    z = t // (2 * SIDE)

    slots = weight.shape[0]
    chunk = slots // LOADS
    loads = []
    for n, (src, dst) in enumerate(((weight_hbm, weight), (vertical_hbm, vertical))):
        for i in range(LOADS):
            at = pl.ds(i * chunk, chunk)
            copy = pltpu.make_async_copy(src.at[at], dst.at[at], load_sem.at[n * LOADS + i])
            copy.start()
            loads.append(copy)

    def beside(zq, xq):
        return tile_of((z + zq) % SIDE, (x + xq) % SIDE, c)

    y_dev = {q: ((e + q) % SIDE, t) for q in (1, 2, 3)}
    hi_dev = {q: (e, jnp.where(c == 0, beside(q, 0), beside(0, q))) for q in (1, 3)}
    lo_dev = {q: (e, jnp.where(c == 0, beside(0, q), beside(q, 0))) for q in (1, 2, 3)}
    core_dev = (e, tile_of(z, x, 1 - c))

    def slot_tile(core, r, rho):
        hi = (jnp.where(core == 0, z, x) + r) % SIDE
        lo = (jnp.where(core == 0, x, z) + rho) % SIDE
        return jnp.where(core == 0, tile_of(hi, lo, 0), tile_of(lo, hi, 1))

    barrier = pltpu.get_barrier_semaphore()
    greet = [*y_dev.values(), *hi_dev.values(), *lo_dev.values(), core_dev]
    for dev in greet:
        pl.semaphore_signal(barrier, inc=1, device_id=dev, device_id_type=MESH)
    pl.semaphore_wait(barrier, len(greet))

    ways = {}

    def way(name, src, dst, dev):
        ways[name] = (len(ways), src, dst, dev)

    def copy_of(name):
        n, src, dst, dev = ways[name]
        return pltpu.make_async_remote_copy(
            src_ref=src,
            dst_ref=dst,
            send_sem=ssem.at[n],
            recv_sem=rsem.at[n],
            device_id=dev,
            device_id_type=MESH,
        )

    def go(*names):
        for name in names:
            copy_of(name).start()

    def got(*names):
        for name in names:
            copy_of(name).wait_recv()

    low, high = pl.ds(0, 4), pl.ds(4, 4)
    for i, (r, rho) in enumerate(ORDER):
        at = pl.ds(i * 8, 8)
        way(("D", i), adj_other.at[at], core_in.at[at], core_dev)
    mine = own[0][0].at[pl.ds(2 * e, 2)]
    for q in (1, 2, 3):
        way(("yr", q), sendy.at[pl.ds(2 * ((e + q) % SIDE), 2)], recvy.at[q - 1], y_dev[q])
        way(("yg", q), mine, mine, y_dev[q])
    way("A3", own[0][0], own[0][3], lo_dev[1])
    way("A1", own[0][0], own[0][1], lo_dev[3])
    way("A2a", own[0][3].at[low], own[0][2].at[low], lo_dev[1])
    way("A2b", own[0][1].at[high], own[0][2].at[high], lo_dev[3])
    for rho in range(4):
        way(("B", 3, rho), own[0][rho], own[3][rho], hi_dev[1])
        way(("B", 1, rho), own[0][rho], own[1][rho], hi_dev[3])
        way(("F", 0, rho), own[3][rho].at[low], own[2][rho].at[low], hi_dev[1])
        way(("F", 1, rho), own[1][rho].at[high], own[2][rho].at[high], hi_dev[3])
        for r in range(4):
            way(("C", r, rho), own[r][rho], other[r][rho], core_dev)

    def total_at(r, rho, first, count):
        return total.at[pl.ds(STEP_OF[r, rho] * 8 + first, count)]

    for rho in range(4):
        to_next, to_back = row_in.at[pl.ds(rho * 8, 8)], row_in.at[pl.ds(32 + rho * 8, 8)]
        way(("H", 0, rho), total_at(2, rho, 0, 4), half_in.at[pl.ds(rho * 4, 4)], hi_dev[1])
        way(("H", 1, rho), total_at(2, rho, 4, 4), half_in.at[pl.ds(16 + rho * 4, 4)], hi_dev[3])
        way(("R0u", rho), total_at(1, rho, 4, 4), row_in.at[pl.ds(rho * 8 + 4, 4)], hi_dev[1])
        way(("R0a", rho), total_at(1, rho, 0, 4), row_in.at[pl.ds(rho * 8, 4)], hi_dev[1])
        way(("R1u", rho), total_at(3, rho, 0, 4), row_in.at[pl.ds(32 + rho * 8, 4)], hi_dev[3])
        way(("R1a", rho), total_at(3, rho, 4, 4), row_in.at[pl.ds(32 + rho * 8 + 4, 4)], hi_dev[3])
    for rho in (1, 2, 3):
        way(("L", rho), plane.at[pl.ds(rho * 8, 8)], plane_in.at[pl.ds((rho - 1) * 8, 8)], lo_dev[rho])
    done = final.at[pl.ds(2 * e, 2)]
    for q in (1, 2, 3):
        way(("ur", q), unit_b.at[pl.ds(2 * ((e + q) % SIDE), 2)], unit_in.at[q - 1], y_dev[q])
        way(("ug", q), done, done, y_dev[q])

    def turn(first, count):
        def some(i, carry):
            for u in range(4):
                turned[i * 4 + u] = weight[i * 4 + u].T
            return carry

        lax.fori_loop(first // 4, (first + count) // 4, some, 0)

    for k in range(8):
        sendy[k] = partial_ref[:, k * 128 : (k + 1) * 128].astype(BF16)
    go(("yr", 1), ("yr", 3), ("yr", 2))
    for load in loads[:LOADS]:
        load.wait()
    turn(0, slots // 2)
    got(("yr", 1), ("yr", 3), ("yr", 2))
    for h in range(2):
        whole = partial_ref[:, pl.ds(pl.multiple_of(e * 256 + h * 128, 128), 128)]
        for q in range(3):
            whole = whole + recvy[q, h].astype(F32)
        own[0][0][2 * e + h] = whole.astype(BF16)
    go(("yg", 1), ("yg", 3), ("yg", 2))
    turn(slots // 2, slots // 2)
    got(("yg", 1), ("yg", 3), ("yg", 2))
    go("A3", "A1", ("B", 3, 0), ("B", 1, 0), ("C", 0, 0))
    for load in loads[LOADS:]:
        load.wait()
    for f in range(2):
        chain[f * 9 + 8] = jnp.zeros((64, 128), F32)

    def arrived(r, rho):
        if r == 0 and rho == 2:
            got("A2a", "A2b")
        elif r == 0:
            got("A%d" % rho)
            go("A2a" if rho == 3 else "A2b")
        elif r == 2:
            got(("F", 0, rho), ("F", 1, rho))
        else:
            got(("B", r, rho))
            go(("F", 0 if r == 3 else 1, rho))
        if r == 0:
            go(("B", 3, rho), ("B", 1, rho))
        go(("C", r, rho))

    def event(i):
        for place in ARRIVE.get(i, ()):
            arrived(*place)
        if i == 13:
            for rho in LATE:
                go(("R0u", rho), ("R1u", rho))
        if i >= 2 and ORDER[i - 2][0] == 2:
            rho = ORDER[i - 2][1]
            go(("H", 0, rho), ("H", 1, rho))
        if i < STEPS:
            r, rho = ORDER[i]
            got(("C", r, rho))
            for f, refs in ((0, own), (1, other)):
                base = slot_tile(c if f == 0 else 1 - c, r, rho) * 8
                for p in range(8):
                    picked[f * 8 + p] = refs[r][rho][block_ref[base + p]]

    def dispatch(i, first, last):
        if last - first == 1:
            event(first)
            return
        middle = (first + last) // 2

        @pl.when(i < middle)
        def _():
            dispatch(i, first, middle)

        @pl.when(i >= middle)
        def _():
            dispatch(i, middle, last)

    def add_core(i):
        pltpu.make_async_remote_copy(
            src_ref=adj_other.at[pl.ds(i * 8, 8)],
            dst_ref=core_in.at[pl.ds(i * 8, 8)],
            send_sem=ssem.at[i],
            recv_sem=rsem.at[i],
            device_id=core_dev,
            device_id_type=MESH,
        ).wait_recv()
        for k in range(8):
            both = adj_own[i * 8 + k].astype(F32) + core_in[i * 8 + k].astype(F32)
            total[i * 8 + k] = both.astype(BF16)

    def step(i, carry):
        @pl.when(i >= 2)
        def _():
            add_core(i - 2)

        dispatch(i, 0, STEPS)
        r, rho = jnp.int32(0), jnp.int32(0)
        for n, (rn, rhon) in enumerate(ORDER):
            r = jnp.where(i == n, rn, r)
            rho = jnp.where(i == n, rhon, rho)
        pairs = []
        for f in range(2):
            tile = slot_tile(c if f == 0 else 1 - c, r, rho)
            pairs.append((f, tile, pl.multiple_of(tile * 8, 8)))
        both = [(f, tile, base, p) for f, tile, base in pairs for p in range(8)]
        innov = [innov_ref[pl.ds(base, 8), :] for _, _, base in pairs]
        prec = [prec_ref[pl.ds(base, 8), :] for _, _, base in pairs]
        projs = [
            jnp.dot(picked[f * 8 + p], turned[base + p], preferred_element_type=F32)
            for f, tile, base, p in both
        ]
        deps = []
        for f, tile, base, p in both:
            model = jnp.sum(vertical[base + p] * projs[f * 8 + p], axis=0, keepdims=True)
            dep = prec[f][p : p + 1] * (model - innov[f][p : p + 1])
            deps.append(jnp.where(p < count_ref[tile], dep, 0.0))
        backs = []
        for f, tile, base, p in both:
            weighted = (vertical[base + p] * deps[f * 8 + p]).astype(BF16)
            backs.append(jnp.dot(weighted, weight[base + p], preferred_element_type=F32))
        for f, tile, base, p in both:
            back = backs[f * 8 + p]
            if p > 0:
                back = back + chain[f * 9 + prev_ref[base + p]]
            chain[f * 9 + p] = back
        for f, tile, base in pairs:
            into = adj_own if f == 0 else adj_other
            for k in range(8):
                into[i * 8 + k] = chain[f * 9 + last_ref[base + k]].astype(BF16)
        pltpu.make_async_remote_copy(
            src_ref=adj_other.at[pl.ds(i * 8, 8)],
            dst_ref=core_in.at[pl.ds(i * 8, 8)],
            send_sem=ssem.at[i],
            recv_sem=rsem.at[i],
            device_id=core_dev,
            device_id_type=MESH,
        ).start()
        return carry

    lax.fori_loop(0, STEPS, step, 0)

    for i in (STEPS, STEPS + 1):
        add_core(i - 2)
        event(i)
    for rho in LATE:
        for d, r, first, name in ((0, 1, 0, "R0a"), (1, 3, 4, "R1a")):
            got(("H", d, rho))
            for b in range(4):
                at = STEP_OF[r, rho] * 8 + first + b
                sum_ = total[at].astype(F32) + half_in[d * 16 + rho * 4 + b].astype(F32)
                total[at] = sum_.astype(BF16)
            go((name, rho))
    for rho in (1, 3, 2, 0):
        got(("R0u", rho), ("R0a", rho), ("R1u", rho), ("R1a", rho))
        for k in range(8):
            sum_ = (
                total[STEP_OF[0, rho] * 8 + k].astype(F32)
                + row_in[rho * 8 + k].astype(F32)
                + row_in[32 + rho * 8 + k].astype(F32)
            )
            if rho == 0:
                unit[k] = sum_
            else:
                plane[rho * 8 + k] = sum_.astype(BF16)
        if rho != 0:
            go(("L", rho))
    got(("L", 1), ("L", 3), ("L", 2))
    for k in range(8):
        sum_ = unit[k]
        for q in range(3):
            sum_ = sum_ + plane_in[q * 8 + k].astype(F32)
        unit[k] = sum_
        unit_b[k] = sum_.astype(BF16)

    go(("ur", 1), ("ur", 3), ("ur", 2))
    got(("ur", 1), ("ur", 3), ("ur", 2))
    for h in range(2):
        sum_ = unit[2 * e + h]
        for q in range(3):
            sum_ = sum_ + unit_in[q, h].astype(F32)
        final[2 * e + h] = sum_.astype(BF16)
    go(("ug", 1), ("ug", 3), ("ug", 2))
    got(("ug", 1), ("ug", 3), ("ug", 2))
    for k in range(8):
        out_ref[:, k * 128 : (k + 1) * 128] = final[k].astype(F32)
    for name in ways:
        copy_of(name).wait_send()


def exchange(partial_sum, innovation, obs_precision, obs_weight, obs_vertical, meta):
    levels, columns = partial_sum.shape
    slots, block, _ = obs_weight.shape
    smem = pl.BlockSpec(memory_space=pltpu.SMEM)
    vmem = pl.BlockSpec(memory_space=pltpu.VMEM)
    hbm = pl.BlockSpec(memory_space=pl.ANY)

    def blocks(*lead, dtype=BF16):
        return pltpu.VMEM((*lead, levels, block), dtype)

    return pl.pallas_call(
        exchange_kernel,
        out_shape=jax.ShapeDtypeStruct((levels, columns), F32),
        in_specs=[smem] * 4 + [vmem] * 3 + [hbm] * 2,
        out_specs=vmem,
        scratch_shapes=[blocks(8) for _ in range(32)]
        + [
            pltpu.VMEM((slots, block, block), BF16),
            pltpu.VMEM((slots, block, block), BF16),
            pltpu.VMEM((slots, levels, block), F32),
            blocks(8),
            blocks(3, 2),
            blocks(16),
            blocks(18, dtype=F32),
            blocks(128),
            blocks(128),
            blocks(128),
            blocks(128),
            blocks(32),
            blocks(64),
            blocks(32),
            blocks(24),
            blocks(8, dtype=F32),
            blocks(8),
            blocks(3, 2),
            blocks(8),
            pltpu.SemaphoreType.DMA((2 * LOADS,)),
            pltpu.SemaphoreType.DMA((112,)),
            pltpu.SemaphoreType.DMA((112,)),
        ],
        compiler_params=pltpu.CompilerParams(
            collective_id=0, has_side_effects=True, vmem_limit_bytes=52 * 1024 * 1024
        ),
    )(*meta, partial_sum, innovation, obs_precision, obs_weight, obs_vertical)


def on_device(
    perturbations,
    control,
    loc_vertical,
    loc_horizontal,
    obs_weight,
    obs_vertical,
    innovation,
    obs_precision,
    block_column,
    tile_count,
):
    members_dev, levels, columns = control.shape
    tile_total = lax.axis_size("tile")
    ens_total = lax.axis_size("ens")
    factor = 1.0 / math.sqrt(members_dev * ens_total - 1)
    vertical = jnp.einsum(
        "ml,klc->kmc", loc_vertical, control, precision=lax.Precision.HIGHEST
    ).astype(BF16)
    spread = jnp.dot(
        vertical.reshape(members_dev * levels, columns),
        loc_horizontal,
        preferred_element_type=F32,
    ).reshape(members_dev, levels, columns)
    partial_sum = jnp.sum(perturbations.astype(F32) * spread, axis=0) * factor

    slots = block_column.reshape(tile_total, 8)
    place = jnp.arange(8, dtype=jnp.int32)
    same = (slots[:, :, None] == slots[:, None, :]) & (place[:, None] > place[None, :])
    prev = jnp.max(jnp.where(same, place[None, None, :], -1), axis=2)
    prev = jnp.where(prev < 0, 8, prev).reshape(-1)
    holds = slots[:, None, :] == place[None, :, None]
    last = jnp.max(jnp.where(holds, place[None, None, :], -1), axis=2)
    last = jnp.where(last < 0, 8, last).reshape(-1)
    adjoint = exchange(
        partial_sum,
        innovation,
        obs_precision,
        obs_weight,
        obs_vertical,
        (block_column, tile_count, prev, last),
    )
    product_field = perturbations.astype(F32) * adjoint[None]
    back_vertical = jnp.einsum(
        "ml,kmc->klc", loc_vertical, product_field, precision=lax.Precision.HIGHEST
    ).astype(BF16)
    spread_back = jnp.einsum(
        "rc,dc->rd",
        back_vertical.reshape(members_dev * levels, columns),
        loc_horizontal,
        preferred_element_type=F32,
    )
    return control + factor * spread_back.reshape(members_dev, levels, columns)


def solution(mesh):
    in_specs = (
        P("ens", None, "tile"),
        P("ens", None, "tile"),
        P(),
        P(),
        P(("ens", "tile"), None, None),
        P(("ens", "tile"), None, None),
        P(("ens", "tile"), None),
        P(("ens", "tile"), None),
        P(("ens", "tile")),
        P(("ens", "tile")),
    )
    out_specs = P("ens", None, "tile")
    return jax.shard_map(
        on_device, mesh=mesh, in_specs=in_specs, out_specs=out_specs, check_vma=False
    )
```

```python
import functools
import math

import jax
import jax.numpy as jnp
from jax import lax
from jax.experimental import pallas as pl
from jax.experimental.pallas import tpu as pltpu
from jax.sharding import PartitionSpec as P

MESH = pl.DeviceIdType.MESH
F32 = jnp.float32
BF16 = jnp.bfloat16
SIDE = 4
LOADS = 4


def tile_of(z, x, c):
    return (z * SIDE + x) * 2 + c


ORDER = (
    (0, 0), (0, 1), (0, 3), (3, 0), (1, 0), (0, 2), (3, 1), (1, 1),
    (3, 3), (1, 3), (3, 2), (1, 2), (2, 0), (2, 1), (2, 3), (2, 2),
)
ARRIVE = {
    1: ((0, 3), (0, 1), (3, 0), (1, 0)),
    3: ((0, 2),),
    5: ((3, 1), (1, 1)),
    7: ((3, 3), (1, 3)),
    9: ((3, 2), (1, 2)),
    11: ((2, 0),),
    12: ((2, 1),),
    13: ((2, 3),),
    14: ((2, 2),),
}
STEP_OF = {place: i for i, place in enumerate(ORDER)}
STEPS = len(ORDER)
LATE = (0, 1, 3, 2)


def exchange_kernel(
    factor,
    block_ref,
    count_ref,
    loc_vertical_ref,
    innov_ref,
    prec_ref,
    pert_hbm,
    control_hbm,
    horizontal_hbm,
    weight_hbm,
    vertical_hbm,
    out_ref,
    *scratch,
):
    rest = list(scratch)
    own = [[rest.pop(0) for _ in range(4)] for _ in range(4)]
    other = [[rest.pop(0) for _ in range(4)] for _ in range(4)]
    (
        pert,
        control,
        horizontal,
        localized,
        prev_ref,
        last_ref,
        weight,
        turned,
        vertical,
        sendy,
        recvy,
        picked,
        chain,
        adj_own,
        adj_other,
        core_in,
        total,
        half_in,
        row_in,
        plane,
        plane_in,
        unit,
        unit_b,
        unit_in,
        final,
        load_sem,
        ssem,
        rsem,
    ) = rest

    e = lax.axis_index("ens")
    t = lax.axis_index("tile")
    c = t % 2
    x = (t // 2) % SIDE
    z = t // (2 * SIDE)

    first_loads = []
    for n, (src, dst) in enumerate(
        ((control_hbm, control), (horizontal_hbm, horizontal), (pert_hbm, pert))
    ):
        copy = pltpu.make_async_copy(src, dst, load_sem.at[2 * LOADS + n])
        copy.start()
        first_loads.append(copy)
    slots = weight.shape[0]
    chunk = slots // LOADS
    loads = []
    for n, (src, dst) in enumerate(((weight_hbm, weight), (vertical_hbm, vertical))):
        for i in range(LOADS):
            at = pl.ds(i * chunk, chunk)
            copy = pltpu.make_async_copy(src.at[at], dst.at[at], load_sem.at[n * LOADS + i])
            copy.start()
            loads.append(copy)

    def beside(zq, xq):
        return tile_of((z + zq) % SIDE, (x + xq) % SIDE, c)

    y_dev = {q: ((e + q) % SIDE, t) for q in (1, 2, 3)}
    hi_dev = {q: (e, jnp.where(c == 0, beside(q, 0), beside(0, q))) for q in (1, 3)}
    lo_dev = {q: (e, jnp.where(c == 0, beside(0, q), beside(q, 0))) for q in (1, 2, 3)}
    core_dev = (e, tile_of(z, x, 1 - c))

    def slot_tile(core, r, rho):
        hi = (jnp.where(core == 0, z, x) + r) % SIDE
        lo = (jnp.where(core == 0, x, z) + rho) % SIDE
        return jnp.where(core == 0, tile_of(hi, lo, 0), tile_of(lo, hi, 1))

    barrier = pltpu.get_barrier_semaphore()
    greet = [*y_dev.values(), *hi_dev.values(), *lo_dev.values(), core_dev]
    for dev in greet:
        pl.semaphore_signal(barrier, inc=1, device_id=dev, device_id_type=MESH)
    ways = {}

    def way(name, src, dst, dev):
        ways[name] = (len(ways), src, dst, dev)

    def copy_of(name):
        n, src, dst, dev = ways[name]
        return pltpu.make_async_remote_copy(
            src_ref=src,
            dst_ref=dst,
            send_sem=ssem.at[n],
            recv_sem=rsem.at[n],
            device_id=dev,
            device_id_type=MESH,
        )

    def go(*names):
        for name in names:
            copy_of(name).start()

    def got(*names):
        for name in names:
            copy_of(name).wait_recv()

    low, high = pl.ds(0, 4), pl.ds(4, 4)
    for i, (r, rho) in enumerate(ORDER):
        at = pl.ds(i * 8, 8)
        way(("D", i), adj_other.at[at], core_in.at[at], core_dev)
    mine = own[0][0].at[pl.ds(2 * e, 2)]
    for q in (1, 2, 3):
        way(("yr", q), sendy.at[q - 1], recvy.at[q - 1], y_dev[q])
        way(("yg", q), mine, mine, y_dev[q])
    way("A3", own[0][0], own[0][3], lo_dev[1])
    way("A1", own[0][0], own[0][1], lo_dev[3])
    way("A2a", own[0][3].at[low], own[0][2].at[low], lo_dev[1])
    way("A2b", own[0][1].at[high], own[0][2].at[high], lo_dev[3])
    for rho in range(4):
        way(("B", 3, rho), own[0][rho], own[3][rho], hi_dev[1])
        way(("B", 1, rho), own[0][rho], own[1][rho], hi_dev[3])
        way(("F", 0, rho), own[3][rho].at[low], own[2][rho].at[low], hi_dev[1])
        way(("F", 1, rho), own[1][rho].at[high], own[2][rho].at[high], hi_dev[3])
        for r in range(4):
            way(("C", r, rho), own[r][rho], other[r][rho], core_dev)

    def total_at(r, rho, first, count):
        return total.at[pl.ds(STEP_OF[r, rho] * 8 + first, count)]

    for rho in range(4):
        to_next, to_back = row_in.at[pl.ds(rho * 8, 8)], row_in.at[pl.ds(32 + rho * 8, 8)]
        way(("H", 0, rho), total_at(2, rho, 0, 4), half_in.at[pl.ds(rho * 4, 4)], hi_dev[1])
        way(("H", 1, rho), total_at(2, rho, 4, 4), half_in.at[pl.ds(16 + rho * 4, 4)], hi_dev[3])
        way(("R0u", rho), total_at(1, rho, 4, 4), row_in.at[pl.ds(rho * 8 + 4, 4)], hi_dev[1])
        way(("R0a", rho), total_at(1, rho, 0, 4), row_in.at[pl.ds(rho * 8, 4)], hi_dev[1])
        way(("R1u", rho), total_at(3, rho, 0, 4), row_in.at[pl.ds(32 + rho * 8, 4)], hi_dev[3])
        way(("R1a", rho), total_at(3, rho, 4, 4), row_in.at[pl.ds(32 + rho * 8 + 4, 4)], hi_dev[3])
    for rho in (1, 2, 3):
        way(("L", rho), plane.at[pl.ds(rho * 8, 8)], plane_in.at[pl.ds((rho - 1) * 8, 8)], lo_dev[rho])
    done = final.at[pl.ds(2 * e, 2)]
    for q in (1, 2, 3):
        way(("ur", q), unit_b.at[pl.ds(2 * ((e + q) % SIDE), 2)], unit_in.at[q - 1], y_dev[q])
        way(("ug", q), done, done, y_dev[q])

    def turn(first, count):
        def some(i, carry):
            for u in range(4):
                turned[i * 4 + u] = weight[i * 4 + u].T
            return carry

        lax.fori_loop(first // 4, (first + count) // 4, some, 0)

    def tables(j, carry):
        base = j * 8
        columns = [block_ref[base + p] for p in range(8)]
        for p in range(8):
            before = jnp.int32(8)
            for n in range(p):
                before = jnp.where(columns[n] == columns[p], n, before)
            prev_ref[base + p] = before
        for k in range(8):
            latest = jnp.int32(8)
            for n in range(8):
                latest = jnp.where(columns[n] == k, n, latest)
            last_ref[base + k] = latest
        return carry

    lv = loc_vertical_ref[...]
    head = lv.astype(BF16)
    heads = jnp.concatenate([head, (lv - head.astype(F32)).astype(BF16)], axis=0)
    first_loads[0].wait()

    def one_member(k, carry):
        field = control[k]
        field_head = field.astype(BF16)
        field_rest = (field - field_head.astype(F32)).astype(BF16)
        two = jnp.dot(heads, field_head, preferred_element_type=F32)
        sum_ = two[:64] + two[64:] + jnp.dot(head, field_rest, preferred_element_type=F32)
        localized[pl.ds(pl.multiple_of(k * 64, 64), 64), :] = sum_.astype(BF16)
        return carry

    lax.fori_loop(0, 8, one_member, 0)
    for load in first_loads[1:]:
        load.wait()

    def increment(q):
        at = pl.ds(pl.multiple_of((e + q) % SIDE * 256, 256), 256)
        spread = jnp.dot(localized[...], horizontal[:, at], preferred_element_type=F32)
        sum_ = pert[0, :, at].astype(F32) * spread[:64]
        for k in range(1, 8):
            sum_ = sum_ + pert[k, :, at].astype(F32) * spread[k * 64 : (k + 1) * 64]
        return sum_ * factor

    for n, q in enumerate((2, 1, 3)):
        sum_ = increment(q)
        for h in range(2):
            sendy[q - 1, h] = sum_[:, h * 128 : (h + 1) * 128].astype(BF16)
        if n == 0:
            pl.semaphore_wait(barrier, len(greet))
        go(("yr", q))
    whole = increment(0)
    for load in loads[:LOADS]:
        load.wait()
    got(("yr", 1), ("yr", 3), ("yr", 2))
    for h in range(2):
        half = whole[:, h * 128 : (h + 1) * 128]
        for q in range(3):
            half = half + recvy[q, h].astype(F32)
        own[0][0][2 * e + h] = half.astype(BF16)
    go(("yg", 2), ("yg", 1), ("yg", 3))
    turn(0, slots // 2)
    got(("yg", 1), ("yg", 3), ("yg", 2))
    go("A3", "A1", ("C", 0, 0))
    turn(slots // 2, slots // 4)
    go(("B", 3, 0), ("B", 1, 0))
    turn(slots // 4 * 3, slots // 4)
    lax.fori_loop(0, slots // 8, tables, 0)
    for load in loads[LOADS:]:
        load.wait()
    for f in range(2):
        chain[f * 9 + 8] = jnp.zeros((64, 128), F32)

    def arrived(r, rho):
        if r == 0 and rho == 2:
            got("A2a", "A2b")
        elif r == 0:
            got("A%d" % rho)
            go("A2a" if rho == 3 else "A2b")
        elif r == 2:
            got(("F", 0, rho), ("F", 1, rho))
        else:
            got(("B", r, rho))
            go(("F", 0 if r == 3 else 1, rho))
        if r == 0:
            go(("B", 3, rho), ("B", 1, rho))
        go(("C", r, rho))

    def event(i):
        for place in ARRIVE.get(i, ()):
            arrived(*place)
        if i == 13:
            for rho in LATE:
                go(("R0u", rho), ("R1u", rho))
        if i >= 2 and ORDER[i - 2][0] == 2:
            rho = ORDER[i - 2][1]
            go(("H", 0, rho), ("H", 1, rho))
        if i < STEPS:
            r, rho = ORDER[i]
            got(("C", r, rho))
            for f, refs in ((0, own), (1, other)):
                base = slot_tile(c if f == 0 else 1 - c, r, rho) * 8
                for p in range(8):
                    picked[f * 8 + p] = refs[r][rho][block_ref[base + p]]

    def dispatch(i, first, last):
        if last - first == 1:
            event(first)
            return
        middle = (first + last) // 2

        @pl.when(i < middle)
        def _():
            dispatch(i, first, middle)

        @pl.when(i >= middle)
        def _():
            dispatch(i, middle, last)

    def add_core(i):
        pltpu.make_async_remote_copy(
            src_ref=adj_other.at[pl.ds(i * 8, 8)],
            dst_ref=core_in.at[pl.ds(i * 8, 8)],
            send_sem=ssem.at[i],
            recv_sem=rsem.at[i],
            device_id=core_dev,
            device_id_type=MESH,
        ).wait_recv()
        for k in range(8):
            both = adj_own[i * 8 + k].astype(F32) + core_in[i * 8 + k].astype(F32)
            total[i * 8 + k] = both.astype(BF16)

    def step(i, carry):
        @pl.when(i >= 2)
        def _():
            add_core(i - 2)

        dispatch(i, 0, STEPS)
        r, rho = jnp.int32(0), jnp.int32(0)
        for n, (rn, rhon) in enumerate(ORDER):
            r = jnp.where(i == n, rn, r)
            rho = jnp.where(i == n, rhon, rho)
        pairs = []
        for f in range(2):
            tile = slot_tile(c if f == 0 else 1 - c, r, rho)
            pairs.append((f, tile, pl.multiple_of(tile * 8, 8)))
        both = [(f, tile, base, p) for f, tile, base in pairs for p in range(8)]
        innov = [innov_ref[pl.ds(base, 8), :] for _, _, base in pairs]
        prec = [prec_ref[pl.ds(base, 8), :] for _, _, base in pairs]
        projs = [
            jnp.dot(picked[f * 8 + p], turned[base + p], preferred_element_type=F32)
            for f, tile, base, p in both
        ]
        deps = []
        for f, tile, base, p in both:
            model = jnp.sum(vertical[base + p] * projs[f * 8 + p], axis=0, keepdims=True)
            dep = prec[f][p : p + 1] * (model - innov[f][p : p + 1])
            deps.append(jnp.where(p < count_ref[tile], dep, 0.0))
        backs = []
        for f, tile, base, p in both:
            weighted = (vertical[base + p] * deps[f * 8 + p]).astype(BF16)
            backs.append(jnp.dot(weighted, weight[base + p], preferred_element_type=F32))
        for f, tile, base, p in both:
            back = backs[f * 8 + p]
            if p > 0:
                back = back + chain[f * 9 + prev_ref[base + p]]
            chain[f * 9 + p] = back
        for f, tile, base in pairs:
            into = adj_own if f == 0 else adj_other
            for k in range(8):
                into[i * 8 + k] = chain[f * 9 + last_ref[base + k]].astype(BF16)
        pltpu.make_async_remote_copy(
            src_ref=adj_other.at[pl.ds(i * 8, 8)],
            dst_ref=core_in.at[pl.ds(i * 8, 8)],
            send_sem=ssem.at[i],
            recv_sem=rsem.at[i],
            device_id=core_dev,
            device_id_type=MESH,
        ).start()
        return carry

    lax.fori_loop(0, STEPS, step, 0)

    for i in (STEPS, STEPS + 1):
        add_core(i - 2)
        event(i)
    for rho in LATE:
        for d, r, first, name in ((0, 1, 0, "R0a"), (1, 3, 4, "R1a")):
            got(("H", d, rho))
            for b in range(4):
                at = STEP_OF[r, rho] * 8 + first + b
                sum_ = total[at].astype(F32) + half_in[d * 16 + rho * 4 + b].astype(F32)
                total[at] = sum_.astype(BF16)
            go((name, rho))
    for rho in (1, 3, 2, 0):
        got(("R0u", rho), ("R0a", rho), ("R1u", rho), ("R1a", rho))
        for k in range(8):
            sum_ = (
                total[STEP_OF[0, rho] * 8 + k].astype(F32)
                + row_in[rho * 8 + k].astype(F32)
                + row_in[32 + rho * 8 + k].astype(F32)
            )
            if rho == 0:
                unit[k] = sum_
            else:
                plane[rho * 8 + k] = sum_.astype(BF16)
        if rho != 0:
            go(("L", rho))
    got(("L", 1), ("L", 3), ("L", 2))
    for k in range(8):
        sum_ = unit[k]
        for q in range(3):
            sum_ = sum_ + plane_in[q * 8 + k].astype(F32)
        unit[k] = sum_
        unit_b[k] = sum_.astype(BF16)

    go(("ur", 1), ("ur", 3), ("ur", 2))
    got(("ur", 1), ("ur", 3), ("ur", 2))
    for h in range(2):
        sum_ = unit[2 * e + h]
        for q in range(3):
            sum_ = sum_ + unit_in[q, h].astype(F32)
        final[2 * e + h] = sum_.astype(BF16)
    go(("ug", 1), ("ug", 3), ("ug", 2))
    got(("ug", 1), ("ug", 3), ("ug", 2))
    for k in range(8):
        out_ref[:, k * 128 : (k + 1) * 128] = final[k].astype(F32)
    for name in ways:
        copy_of(name).wait_send()


def exchange(
    factor,
    block_column,
    tile_count,
    loc_vertical,
    innovation,
    obs_precision,
    perturbations,
    control,
    loc_horizontal,
    obs_weight,
    obs_vertical,
):
    members, levels, columns = control.shape
    slots, block, _ = obs_weight.shape
    smem = pl.BlockSpec(memory_space=pltpu.SMEM)
    vmem = pl.BlockSpec(memory_space=pltpu.VMEM)
    hbm = pl.BlockSpec(memory_space=pl.ANY)

    def blocks(*lead, dtype=BF16):
        return pltpu.VMEM((*lead, levels, block), dtype)

    return pl.pallas_call(
        functools.partial(exchange_kernel, factor),
        out_shape=jax.ShapeDtypeStruct((levels, columns), F32),
        in_specs=[smem] * 2 + [vmem] * 3 + [hbm] * 5,
        out_specs=vmem,
        scratch_shapes=[blocks(8) for _ in range(32)]
        + [
            pltpu.VMEM((members, levels, columns), BF16),
            pltpu.VMEM((members, levels, columns), F32),
            pltpu.VMEM((columns, columns), BF16),
            pltpu.VMEM((members * levels, columns), BF16),
            pltpu.SMEM((slots,), jnp.int32),
            pltpu.SMEM((slots,), jnp.int32),
            pltpu.VMEM((slots, block, block), BF16),
            pltpu.VMEM((slots, block, block), BF16),
            pltpu.VMEM((slots, levels, block), F32),
            blocks(3, 2),
            blocks(3, 2),
            blocks(16),
            blocks(18, dtype=F32),
            blocks(128),
            blocks(128),
            blocks(128),
            blocks(128),
            blocks(32),
            blocks(64),
            blocks(32),
            blocks(24),
            blocks(8, dtype=F32),
            blocks(8),
            blocks(3, 2),
            blocks(8),
            pltpu.SemaphoreType.DMA((2 * LOADS + 3,)),
            pltpu.SemaphoreType.DMA((112,)),
            pltpu.SemaphoreType.DMA((112,)),
        ],
        compiler_params=pltpu.CompilerParams(
            collective_id=0, has_side_effects=True, vmem_limit_bytes=56 * 1024 * 1024
        ),
    )(
        block_column,
        tile_count,
        loc_vertical,
        innovation,
        obs_precision,
        perturbations,
        control,
        loc_horizontal,
        obs_weight,
        obs_vertical,
    )


def on_device(
    perturbations,
    control,
    loc_vertical,
    loc_horizontal,
    obs_weight,
    obs_vertical,
    innovation,
    obs_precision,
    block_column,
    tile_count,
):
    members_dev, levels, columns = control.shape
    ens_total = lax.axis_size("ens")
    factor = 1.0 / math.sqrt(members_dev * ens_total - 1)
    adjoint = exchange(
        factor,
        block_column,
        tile_count,
        loc_vertical,
        innovation,
        obs_precision,
        perturbations,
        control,
        loc_horizontal,
        obs_weight,
        obs_vertical,
    )
    product_field = perturbations.astype(F32) * adjoint[None]
    back_vertical = jnp.einsum(
        "ml,kmc->klc", loc_vertical, product_field, precision=lax.Precision.HIGHEST
    ).astype(BF16)
    spread_back = jnp.einsum(
        "rc,dc->rd",
        back_vertical.reshape(members_dev * levels, columns),
        loc_horizontal,
        preferred_element_type=F32,
    )
    return control + factor * spread_back.reshape(members_dev, levels, columns)


def solution(mesh):
    in_specs = (
        P("ens", None, "tile"),
        P("ens", None, "tile"),
        P(),
        P(),
        P(("ens", "tile"), None, None),
        P(("ens", "tile"), None, None),
        P(("ens", "tile"), None),
        P(("ens", "tile"), None),
        P(("ens", "tile")),
        P(("ens", "tile")),
    )
    out_specs = P("ens", None, "tile")
    return jax.shard_map(
        on_device, mesh=mesh, in_specs=in_specs, out_specs=out_specs, check_vma=False
    )
```

```python
import functools
import math

import jax
import jax.numpy as jnp
from jax import lax
from jax.experimental import pallas as pl
from jax.experimental.pallas import tpu as pltpu
from jax.sharding import PartitionSpec as P

MESH = pl.DeviceIdType.MESH
F32 = jnp.float32
BF16 = jnp.bfloat16
SIDE = 4
LOADS = 4


def tile_of(z, x, c):
    return (z * SIDE + x) * 2 + c


ORDER = (
    (0, 0), (0, 1), (0, 3), (3, 0), (1, 0), (0, 2), (3, 1), (1, 1),
    (3, 3), (1, 3), (3, 2), (1, 2), (2, 0), (2, 1), (2, 3), (2, 2),
)
ARRIVE = {
    1: ((0, 3), (0, 1), (3, 0), (1, 0)),
    3: ((0, 2),),
    5: ((3, 1), (1, 1)),
    7: ((3, 3), (1, 3)),
    9: ((3, 2), (1, 2)),
    11: ((2, 0),),
    12: ((2, 1),),
    13: ((2, 3),),
    14: ((2, 2),),
}
STEP_OF = {place: i for i, place in enumerate(ORDER)}
STEPS = len(ORDER)
LATE = (0, 1, 3, 2)


def exchange_kernel(
    factor,
    block_ref,
    count_ref,
    loc_vertical_ref,
    innov_ref,
    prec_ref,
    pert_hbm,
    control_hbm,
    horizontal_hbm,
    weight_hbm,
    vertical_hbm,
    out_ref,
    *scratch,
):
    rest = list(scratch)
    own = [[rest.pop(0) for _ in range(4)] for _ in range(4)]
    other = [[rest.pop(0) for _ in range(4)] for _ in range(4)]
    (
        pert,
        control,
        horizontal,
        localized,
        prev_ref,
        last_ref,
        weight,
        vertical,
        sendy,
        recvy,
        picked,
        chain,
        adj_own,
        adj_other,
        core_in,
        total,
        half_in,
        row_in,
        plane,
        plane_in,
        unit,
        unit_b,
        unit_in,
        final,
        load_sem,
        ssem,
        rsem,
    ) = rest

    e = lax.axis_index("ens")
    t = lax.axis_index("tile")
    c = t % 2
    x = (t // 2) % SIDE
    z = t // (2 * SIDE)

    first_loads = []
    for n, (src, dst) in enumerate(
        ((control_hbm, control), (horizontal_hbm, horizontal), (pert_hbm, pert))
    ):
        copy = pltpu.make_async_copy(src, dst, load_sem.at[2 * LOADS + n])
        copy.start()
        first_loads.append(copy)
    slots = weight.shape[0]
    chunk = slots // LOADS
    loads = []
    for n, (src, dst) in enumerate(((weight_hbm, weight), (vertical_hbm, vertical))):
        for i in range(LOADS):
            at = pl.ds(i * chunk, chunk)
            copy = pltpu.make_async_copy(src.at[at], dst.at[at], load_sem.at[n * LOADS + i])
            copy.start()
            loads.append(copy)

    def beside(zq, xq):
        return tile_of((z + zq) % SIDE, (x + xq) % SIDE, c)

    y_dev = {q: ((e + q) % SIDE, t) for q in (1, 2, 3)}
    hi_dev = {q: (e, jnp.where(c == 0, beside(q, 0), beside(0, q))) for q in (1, 3)}
    lo_dev = {q: (e, jnp.where(c == 0, beside(0, q), beside(q, 0))) for q in (1, 2, 3)}
    core_dev = (e, tile_of(z, x, 1 - c))

    def slot_tile(core, r, rho):
        hi = (jnp.where(core == 0, z, x) + r) % SIDE
        lo = (jnp.where(core == 0, x, z) + rho) % SIDE
        return jnp.where(core == 0, tile_of(hi, lo, 0), tile_of(lo, hi, 1))

    barrier = pltpu.get_barrier_semaphore()
    greet = [*y_dev.values(), *hi_dev.values(), *lo_dev.values(), core_dev]
    for dev in greet:
        pl.semaphore_signal(barrier, inc=1, device_id=dev, device_id_type=MESH)
    ways = {}

    def way(name, src, dst, dev):
        ways[name] = (len(ways), src, dst, dev)

    def copy_of(name):
        n, src, dst, dev = ways[name]
        return pltpu.make_async_remote_copy(
            src_ref=src,
            dst_ref=dst,
            send_sem=ssem.at[n],
            recv_sem=rsem.at[n],
            device_id=dev,
            device_id_type=MESH,
        )

    def go(*names):
        for name in names:
            copy_of(name).start()

    def got(*names):
        for name in names:
            copy_of(name).wait_recv()

    low, high = pl.ds(0, 4), pl.ds(4, 4)
    for i, (r, rho) in enumerate(ORDER):
        at = pl.ds(i * 8, 8)
        way(("D", i), adj_other.at[at], core_in.at[at], core_dev)
    mine = own[0][0].at[pl.ds(2 * e, 2)]
    for q in (1, 2, 3):
        way(("yr", q), sendy.at[q - 1], recvy.at[q - 1], y_dev[q])
        way(("yg", q), mine, mine, y_dev[q])
    way("A3", own[0][0], own[0][3], lo_dev[1])
    way("A1", own[0][0], own[0][1], lo_dev[3])
    way("A2a", own[0][3].at[low], own[0][2].at[low], lo_dev[1])
    way("A2b", own[0][1].at[high], own[0][2].at[high], lo_dev[3])
    for rho in range(4):
        way(("B", 3, rho), own[0][rho], own[3][rho], hi_dev[1])
        way(("B", 1, rho), own[0][rho], own[1][rho], hi_dev[3])
        way(("F", 0, rho), own[3][rho].at[low], own[2][rho].at[low], hi_dev[1])
        way(("F", 1, rho), own[1][rho].at[high], own[2][rho].at[high], hi_dev[3])
        for r in range(4):
            way(("C", r, rho), own[r][rho], other[r][rho], core_dev)

    def total_at(r, rho, first, count):
        return total.at[pl.ds(STEP_OF[r, rho] * 8 + first, count)]

    for rho in range(4):
        to_next, to_back = row_in.at[pl.ds(rho * 8, 8)], row_in.at[pl.ds(32 + rho * 8, 8)]
        way(("H", 0, rho), total_at(2, rho, 0, 4), half_in.at[pl.ds(rho * 4, 4)], hi_dev[1])
        way(("H", 1, rho), total_at(2, rho, 4, 4), half_in.at[pl.ds(16 + rho * 4, 4)], hi_dev[3])
        way(("R0u", rho), total_at(1, rho, 4, 4), row_in.at[pl.ds(rho * 8 + 4, 4)], hi_dev[1])
        way(("R0a", rho), total_at(1, rho, 0, 4), row_in.at[pl.ds(rho * 8, 4)], hi_dev[1])
        way(("R1u", rho), total_at(3, rho, 0, 4), row_in.at[pl.ds(32 + rho * 8, 4)], hi_dev[3])
        way(("R1a", rho), total_at(3, rho, 4, 4), row_in.at[pl.ds(32 + rho * 8 + 4, 4)], hi_dev[3])
    for rho in (1, 2, 3):
        way(("L", rho), plane.at[pl.ds(rho * 8, 8)], plane_in.at[pl.ds((rho - 1) * 8, 8)], lo_dev[rho])
    done = final.at[pl.ds(2 * e, 2)]
    for q in (1, 2, 3):
        way(("ur", q), unit_b.at[pl.ds(2 * ((e + q) % SIDE), 2)], unit_in.at[q - 1], y_dev[q])
        way(("ug", q), done, done, y_dev[q])

    def tables(j, carry):
        base = j * 8
        columns = [block_ref[base + p] for p in range(8)]
        for p in range(8):
            before = jnp.int32(8)
            for n in range(p):
                before = jnp.where(columns[n] == columns[p], n, before)
            prev_ref[base + p] = before
        for k in range(8):
            latest = jnp.int32(8)
            for n in range(8):
                latest = jnp.where(columns[n] == k, n, latest)
            last_ref[base + k] = latest
        return carry

    lv = loc_vertical_ref[...]
    head = lv.astype(BF16)
    heads = jnp.concatenate([head, (lv - head.astype(F32)).astype(BF16)], axis=0)
    first_loads[0].wait()

    def one_member(k, carry):
        field = control[k]
        field_head = field.astype(BF16)
        field_rest = (field - field_head.astype(F32)).astype(BF16)
        two = jnp.dot(heads, field_head, preferred_element_type=F32)
        sum_ = two[:64] + two[64:] + jnp.dot(head, field_rest, preferred_element_type=F32)
        localized[pl.ds(pl.multiple_of(k * 64, 64), 64), :] = sum_.astype(BF16)
        return carry

    lax.fori_loop(0, 8, one_member, 0)
    for load in first_loads[1:]:
        load.wait()

    def increment(q):
        at = pl.ds(pl.multiple_of((e + q) % SIDE * 256, 256), 256)
        spread = jnp.dot(localized[...], horizontal[:, at], preferred_element_type=F32)
        sum_ = pert[0, :, at].astype(F32) * spread[:64]
        for k in range(1, 8):
            sum_ = sum_ + pert[k, :, at].astype(F32) * spread[k * 64 : (k + 1) * 64]
        return sum_ * factor

    for n, q in enumerate((2, 1, 3)):
        sum_ = increment(q)
        for h in range(2):
            sendy[q - 1, h] = sum_[:, h * 128 : (h + 1) * 128].astype(BF16)
        if n == 0:
            pl.semaphore_wait(barrier, len(greet))
        go(("yr", q))
    whole = increment(0)
    got(("yr", 1), ("yr", 3), ("yr", 2))
    for h in range(2):
        half = whole[:, h * 128 : (h + 1) * 128]
        for q in range(3):
            half = half + recvy[q, h].astype(F32)
        own[0][0][2 * e + h] = half.astype(BF16)
    go(("yg", 2), ("yg", 1), ("yg", 3))
    lax.fori_loop(0, slots // 8, tables, 0)
    got(("yg", 1), ("yg", 3), ("yg", 2))
    go("A3", "A1", ("C", 0, 0))
    go(("B", 3, 0), ("B", 1, 0))
    for load in loads:
        load.wait()
    for f in range(2):
        chain[f * 9 + 8] = jnp.zeros((64, 128), F32)

    def arrived(r, rho):
        if r == 0 and rho == 2:
            got("A2a", "A2b")
        elif r == 0:
            got("A%d" % rho)
            go("A2a" if rho == 3 else "A2b")
        elif r == 2:
            got(("F", 0, rho), ("F", 1, rho))
        else:
            got(("B", r, rho))
            go(("F", 0 if r == 3 else 1, rho))
        if r == 0:
            go(("B", 3, rho), ("B", 1, rho))
        go(("C", r, rho))

    def event(i):
        for place in ARRIVE.get(i, ()):
            arrived(*place)
        if i == 13:
            for rho in LATE:
                go(("R0u", rho), ("R1u", rho))
        if i >= 2 and ORDER[i - 2][0] == 2:
            rho = ORDER[i - 2][1]
            go(("H", 0, rho), ("H", 1, rho))
        if i < STEPS:
            r, rho = ORDER[i]
            got(("C", r, rho))
            for f, refs in ((0, own), (1, other)):
                base = slot_tile(c if f == 0 else 1 - c, r, rho) * 8
                for p in range(8):
                    picked[f * 8 + p] = refs[r][rho][block_ref[base + p]]

    def dispatch(i, first, last):
        if last - first == 1:
            event(first)
            return
        middle = (first + last) // 2

        @pl.when(i < middle)
        def _():
            dispatch(i, first, middle)

        @pl.when(i >= middle)
        def _():
            dispatch(i, middle, last)

    def add_core(i):
        pltpu.make_async_remote_copy(
            src_ref=adj_other.at[pl.ds(i * 8, 8)],
            dst_ref=core_in.at[pl.ds(i * 8, 8)],
            send_sem=ssem.at[i],
            recv_sem=rsem.at[i],
            device_id=core_dev,
            device_id_type=MESH,
        ).wait_recv()
        for k in range(8):
            both = adj_own[i * 8 + k].astype(F32) + core_in[i * 8 + k].astype(F32)
            total[i * 8 + k] = both.astype(BF16)

    def step(i, carry):
        @pl.when(i >= 2)
        def _():
            add_core(i - 2)

        dispatch(i, 0, STEPS)
        r, rho = jnp.int32(0), jnp.int32(0)
        for n, (rn, rhon) in enumerate(ORDER):
            r = jnp.where(i == n, rn, r)
            rho = jnp.where(i == n, rhon, rho)
        pairs = []
        for f in range(2):
            tile = slot_tile(c if f == 0 else 1 - c, r, rho)
            pairs.append((f, tile, pl.multiple_of(tile * 8, 8)))
        both = [(f, tile, base, p) for f, tile, base in pairs for p in range(8)]
        innov = [innov_ref[pl.ds(base, 8), :] for _, _, base in pairs]
        prec = [prec_ref[pl.ds(base, 8), :] for _, _, base in pairs]
        projs = [
            lax.dot_general(
                picked[f * 8 + p],
                weight[base + p],
                (((1,), (1,)), ((), ())),
                preferred_element_type=F32,
            )
            for f, tile, base, p in both
        ]
        deps = []
        for f, tile, base, p in both:
            model = jnp.sum(vertical[base + p] * projs[f * 8 + p], axis=0, keepdims=True)
            dep = prec[f][p : p + 1] * (model - innov[f][p : p + 1])
            deps.append(jnp.where(p < count_ref[tile], dep, 0.0))
        backs = []
        for f, tile, base, p in both:
            weighted = (vertical[base + p] * deps[f * 8 + p]).astype(BF16)
            backs.append(jnp.dot(weighted, weight[base + p], preferred_element_type=F32))
        for f, tile, base, p in both:
            back = backs[f * 8 + p]
            if p > 0:
                back = back + chain[f * 9 + prev_ref[base + p]]
            chain[f * 9 + p] = back
        for f, tile, base in pairs:
            into = adj_own if f == 0 else adj_other
            for k in range(8):
                into[i * 8 + k] = chain[f * 9 + last_ref[base + k]].astype(BF16)
        pltpu.make_async_remote_copy(
            src_ref=adj_other.at[pl.ds(i * 8, 8)],
            dst_ref=core_in.at[pl.ds(i * 8, 8)],
            send_sem=ssem.at[i],
            recv_sem=rsem.at[i],
            device_id=core_dev,
            device_id_type=MESH,
        ).start()
        return carry

    lax.fori_loop(0, STEPS, step, 0)

    for i in (STEPS, STEPS + 1):
        add_core(i - 2)
        event(i)
    for rho in LATE:
        for d, r, first, name in ((0, 1, 0, "R0a"), (1, 3, 4, "R1a")):
            got(("H", d, rho))
            for b in range(4):
                at = STEP_OF[r, rho] * 8 + first + b
                sum_ = total[at].astype(F32) + half_in[d * 16 + rho * 4 + b].astype(F32)
                total[at] = sum_.astype(BF16)
            go((name, rho))
    for rho in (1, 3, 2, 0):
        got(("R0u", rho), ("R0a", rho), ("R1u", rho), ("R1a", rho))
        for k in range(8):
            sum_ = (
                total[STEP_OF[0, rho] * 8 + k].astype(F32)
                + row_in[rho * 8 + k].astype(F32)
                + row_in[32 + rho * 8 + k].astype(F32)
            )
            if rho == 0:
                unit[k] = sum_
            else:
                plane[rho * 8 + k] = sum_.astype(BF16)
        if rho != 0:
            go(("L", rho))
    got(("L", 1), ("L", 3), ("L", 2))
    for k in range(8):
        sum_ = unit[k]
        for q in range(3):
            sum_ = sum_ + plane_in[q * 8 + k].astype(F32)
        unit[k] = sum_
        unit_b[k] = sum_.astype(BF16)

    go(("ur", 1), ("ur", 3), ("ur", 2))
    got(("ur", 1), ("ur", 3), ("ur", 2))
    for h in range(2):
        sum_ = unit[2 * e + h]
        for q in range(3):
            sum_ = sum_ + unit_in[q, h].astype(F32)
        final[2 * e + h] = sum_.astype(BF16)
    go(("ug", 1), ("ug", 3), ("ug", 2))
    lv_t = loc_vertical_ref[...].T
    head_t = lv_t.astype(BF16)
    heads_t = jnp.concatenate([head_t, (lv_t - head_t.astype(F32)).astype(BF16)], axis=0)
    for q in (0, 1, 3, 2):
        if q > 0:
            got(("ug", (4 - q)))
        chunk_at = (e + q) % SIDE
        at = pl.ds(pl.multiple_of(chunk_at * 256, 256), 256)
        adjoint = jnp.concatenate(
            [final[2 * chunk_at].astype(F32), final[2 * chunk_at + 1].astype(F32)], axis=1
        )
        for k in range(8):
            field = pert[k, :, at].astype(F32) * adjoint
            field_head = field.astype(BF16)
            field_rest = (field - field_head.astype(F32)).astype(BF16)
            two = jnp.dot(heads_t, field_head, preferred_element_type=F32)
            sum_ = two[:64] + two[64:] + jnp.dot(head_t, field_rest, preferred_element_type=F32)
            out_ref[k * 64 : (k + 1) * 64, at] = sum_.astype(BF16)
    for name in ways:
        copy_of(name).wait_send()


def exchange(
    factor,
    block_column,
    tile_count,
    loc_vertical,
    innovation,
    obs_precision,
    perturbations,
    control,
    loc_horizontal,
    obs_weight,
    obs_vertical,
):
    members, levels, columns = control.shape
    slots, block, _ = obs_weight.shape
    smem = pl.BlockSpec(memory_space=pltpu.SMEM)
    vmem = pl.BlockSpec(memory_space=pltpu.VMEM)
    hbm = pl.BlockSpec(memory_space=pl.ANY)

    def blocks(*lead, dtype=BF16):
        return pltpu.VMEM((*lead, levels, block), dtype)

    return pl.pallas_call(
        functools.partial(exchange_kernel, factor),
        out_shape=jax.ShapeDtypeStruct((members * levels, columns), BF16),
        in_specs=[smem] * 2 + [vmem] * 3 + [hbm] * 5,
        out_specs=vmem,
        scratch_shapes=[blocks(8) for _ in range(32)]
        + [
            pltpu.VMEM((members, levels, columns), BF16),
            pltpu.VMEM((members, levels, columns), F32),
            pltpu.VMEM((columns, columns), BF16),
            pltpu.VMEM((members * levels, columns), BF16),
            pltpu.SMEM((slots,), jnp.int32),
            pltpu.SMEM((slots,), jnp.int32),
            pltpu.VMEM((slots, block, block), BF16),
            pltpu.VMEM((slots, levels, block), F32),
            blocks(3, 2),
            blocks(3, 2),
            blocks(16),
            blocks(18, dtype=F32),
            blocks(128),
            blocks(128),
            blocks(128),
            blocks(128),
            blocks(32),
            blocks(64),
            blocks(32),
            blocks(24),
            blocks(8, dtype=F32),
            blocks(8),
            blocks(3, 2),
            blocks(8),
            pltpu.SemaphoreType.DMA((2 * LOADS + 3,)),
            pltpu.SemaphoreType.DMA((112,)),
            pltpu.SemaphoreType.DMA((112,)),
        ],
        compiler_params=pltpu.CompilerParams(
            collective_id=0, has_side_effects=True, vmem_limit_bytes=56 * 1024 * 1024
        ),
    )(
        block_column,
        tile_count,
        loc_vertical,
        innovation,
        obs_precision,
        perturbations,
        control,
        loc_horizontal,
        obs_weight,
        obs_vertical,
    )


def on_device(
    perturbations,
    control,
    loc_vertical,
    loc_horizontal,
    obs_weight,
    obs_vertical,
    innovation,
    obs_precision,
    block_column,
    tile_count,
):
    members_dev, levels, columns = control.shape
    ens_total = lax.axis_size("ens")
    factor = 1.0 / math.sqrt(members_dev * ens_total - 1)
    back_vertical = exchange(
        factor,
        block_column,
        tile_count,
        loc_vertical,
        innovation,
        obs_precision,
        perturbations,
        control,
        loc_horizontal,
        obs_weight,
        obs_vertical,
    )
    spread_back = jnp.einsum(
        "rc,dc->rd",
        back_vertical,
        loc_horizontal,
        preferred_element_type=F32,
    )
    return control + factor * spread_back.reshape(members_dev, levels, columns)


def solution(mesh):
    in_specs = (
        P("ens", None, "tile"),
        P("ens", None, "tile"),
        P(),
        P(),
        P(("ens", "tile"), None, None),
        P(("ens", "tile"), None, None),
        P(("ens", "tile"), None),
        P(("ens", "tile"), None),
        P(("ens", "tile")),
        P(("ens", "tile")),
    )
    out_specs = P("ens", None, "tile")
    return jax.shard_map(
        on_device, mesh=mesh, in_specs=in_specs, out_specs=out_specs, check_vma=False
    )
```

```python
import functools
import math

import jax
import jax.numpy as jnp
from jax import lax
from jax.experimental import pallas as pl
from jax.experimental.pallas import tpu as pltpu
from jax.sharding import PartitionSpec as P

MESH = pl.DeviceIdType.MESH
F32 = jnp.float32
BF16 = jnp.bfloat16
SIDE = 4
LOADS = 4


def tile_of(z, x, c):
    return (z * SIDE + x) * 2 + c


ORDER = (
    (0, 0), (0, 1), (0, 3), (3, 0), (1, 0), (0, 2), (3, 1), (1, 1),
    (3, 3), (1, 3), (3, 2), (1, 2), (2, 0), (2, 1), (2, 3), (2, 2),
)
ARRIVE = {
    1: (
        (0, 0, 3), (0, 0, 1), (1, 0, 3), (1, 0, 1),
        (0, 3, 0), (0, 1, 0), (1, 3, 0), (1, 1, 0),
    ),
    3: ((1, 0, 2),),
    5: ((0, 3, 3), (0, 1, 1), (0, 3, 1), (0, 1, 3), (1, 3, 1), (1, 1, 1)),
    7: ((1, 3, 3), (1, 1, 3)),
    8: ((0, 3, 2), (0, 1, 2)),
    9: ((1, 3, 2), (1, 1, 2)),
    10: ((1, 2, 0),),
    12: ((1, 2, 1),),
    13: ((1, 2, 3),),
    14: ((1, 2, 2),),
}
STEP_OF = {place: i for i, place in enumerate(ORDER)}
STEPS = len(ORDER)
LATE = (0, 1, 3, 2)


def exchange_kernel(
    factor,
    block_ref,
    count_ref,
    loc_vertical_ref,
    innov_ref,
    prec_ref,
    pert_hbm,
    control_hbm,
    horizontal_hbm,
    weight_hbm,
    vertical_hbm,
    out_ref,
    *scratch,
):
    rest = list(scratch)
    own = [[rest.pop(0) for _ in range(4)] for _ in range(4)]
    other = [[rest.pop(0) for _ in range(4)] for _ in range(4)]
    (
        pert,
        control,
        horizontal,
        localized,
        prev_ref,
        last_ref,
        weight,
        turned,
        vertical,
        sendy,
        recvy,
        picked,
        chain,
        adj_own,
        adj_other,
        core_in,
        total,
        half_in,
        row_in,
        plane,
        plane_in,
        unit,
        unit_b,
        unit_in,
        final,
        load_sem,
        ssem,
        rsem,
    ) = rest

    e = lax.axis_index("ens")
    t = lax.axis_index("tile")
    c = t % 2
    x = (t // 2) % SIDE
    z = t // (2 * SIDE)

    first_loads = []
    for n, (src, dst) in enumerate(
        ((control_hbm, control), (horizontal_hbm, horizontal), (pert_hbm, pert))
    ):
        copy = pltpu.make_async_copy(src, dst, load_sem.at[2 * LOADS + n])
        copy.start()
        first_loads.append(copy)
    slots = weight.shape[0]
    chunk = slots // LOADS
    loads = []
    for n, (src, dst) in enumerate(((weight_hbm, weight), (vertical_hbm, vertical))):
        for i in range(LOADS):
            at = pl.ds(i * chunk, chunk)
            copy = pltpu.make_async_copy(src.at[at], dst.at[at], load_sem.at[n * LOADS + i])
            copy.start()
            loads.append(copy)

    def beside(zq, xq):
        return tile_of((z + zq) % SIDE, (x + xq) % SIDE, c)

    y_dev = {q: ((e + q) % SIDE, t) for q in (1, 2, 3)}
    hi_dev = {q: (e, jnp.where(c == 0, beside(q, 0), beside(0, q))) for q in (1, 3)}
    lo_dev = {q: (e, jnp.where(c == 0, beside(0, q), beside(q, 0))) for q in (1, 2, 3)}
    core_dev = (e, tile_of(z, x, 1 - c))

    def slot_tile(core, r, rho):
        hi = (jnp.where(core == 0, z, x) + r) % SIDE
        lo = (jnp.where(core == 0, x, z) + rho) % SIDE
        return jnp.where(core == 0, tile_of(hi, lo, 0), tile_of(lo, hi, 1))

    barrier = pltpu.get_barrier_semaphore()
    greet = [*y_dev.values(), *hi_dev.values(), *lo_dev.values(), core_dev]
    for dev in greet:
        pl.semaphore_signal(barrier, inc=1, device_id=dev, device_id_type=MESH)
    ways = {}

    def way(name, src, dst, dev):
        ways[name] = (len(ways), src, dst, dev)

    def copy_of(name):
        n, src, dst, dev = ways[name]
        return pltpu.make_async_remote_copy(
            src_ref=src,
            dst_ref=dst,
            send_sem=ssem.at[n],
            recv_sem=rsem.at[n],
            device_id=dev,
            device_id_type=MESH,
        )

    def go(*names):
        for name in names:
            copy_of(name).start()

    def got(*names):
        for name in names:
            copy_of(name).wait_recv()

    low, high = pl.ds(0, 4), pl.ds(4, 4)
    for i, (r, rho) in enumerate(ORDER):
        at = pl.ds(i * 8, 8)
        way(("D", i), adj_other.at[at], core_in.at[at], core_dev)
    mine = own[0][0].at[pl.ds(2 * e, 2)]
    for q in (1, 2, 3):
        way(("yr", q), sendy.at[q - 1], recvy.at[q - 1], y_dev[q])
        way(("yg", q), mine, mine, y_dev[q])
    for part, at in (("l", low), ("h", high)):
        way(("A", 3, part), own[0][0].at[at], own[0][3].at[at], lo_dev[1])
        way(("A", 1, part), own[0][0].at[at], own[0][1].at[at], lo_dev[3])
    way("A2a", own[0][3].at[low], own[0][2].at[low], lo_dev[1])
    way("A2b", own[0][1].at[high], own[0][2].at[high], lo_dev[3])
    for rho in range(4):
        for part, at in (("l", low), ("h", high)):
            way(("B", 3, rho, part), own[0][rho].at[at], own[3][rho].at[at], hi_dev[1])
            way(("B", 1, rho, part), own[0][rho].at[at], own[1][rho].at[at], hi_dev[3])
        way(("F", 0, rho), own[3][rho].at[low], own[2][rho].at[low], hi_dev[1])
        way(("F", 1, rho), own[1][rho].at[high], own[2][rho].at[high], hi_dev[3])
        for r in range(4):
            way(("C", r, rho), own[r][rho], other[r][rho], core_dev)

    def total_at(r, rho, first, count):
        return total.at[pl.ds(STEP_OF[r, rho] * 8 + first, count)]

    for rho in range(4):
        to_next, to_back = row_in.at[pl.ds(rho * 8, 8)], row_in.at[pl.ds(32 + rho * 8, 8)]
        way(("H", 0, rho), total_at(2, rho, 0, 4), half_in.at[pl.ds(rho * 4, 4)], hi_dev[1])
        way(("H", 1, rho), total_at(2, rho, 4, 4), half_in.at[pl.ds(16 + rho * 4, 4)], hi_dev[3])
        way(("R0u", rho), total_at(1, rho, 4, 4), row_in.at[pl.ds(rho * 8 + 4, 4)], hi_dev[1])
        way(("R0a", rho), total_at(1, rho, 0, 4), row_in.at[pl.ds(rho * 8, 4)], hi_dev[1])
        way(("R1u", rho), total_at(3, rho, 0, 4), row_in.at[pl.ds(32 + rho * 8, 4)], hi_dev[3])
        way(("R1a", rho), total_at(3, rho, 4, 4), row_in.at[pl.ds(32 + rho * 8 + 4, 4)], hi_dev[3])
    for q in range(4):
        at = 2 * ((e + q) % SIDE)
        way(("L2", q), plane.at[pl.ds(16 + at, 2)], plane_in.at[pl.ds(8 + at, 2)], lo_dev[2])
    for rho in (1, 3):
        way(("L", rho), plane.at[pl.ds(rho * 8, 8)], plane_in.at[pl.ds((rho - 1) * 8, 8)], lo_dev[rho])
    done = final.at[pl.ds(2 * e, 2)]
    for q in (1, 2, 3):
        way(("ur", q), unit_b.at[pl.ds(2 * ((e + q) % SIDE), 2)], unit_in.at[q - 1], y_dev[q])
        way(("ug", q), done, done, y_dev[q])

    def turn(first, count):
        def some(i, carry):
            for u in range(8):
                turned[i * 8 + u] = weight[i * 8 + u].T
            return carry

        lax.fori_loop(first // 8, (first + count) // 8, some, 0)

    def tables(j, carry):
        base = j * 8
        columns = [block_ref[base + p] for p in range(8)]
        for p in range(8):
            before = jnp.int32(8)
            for n in range(p):
                before = jnp.where(columns[n] == columns[p], n, before)
            prev_ref[base + p] = before
        for k in range(8):
            latest = jnp.int32(8)
            for n in range(8):
                latest = jnp.where(columns[n] == k, n, latest)
            last_ref[base + k] = latest
        return carry

    lv = loc_vertical_ref[...]
    head = lv.astype(BF16)
    heads = jnp.concatenate([head, (lv - head.astype(F32)).astype(BF16)], axis=0)
    first_loads[0].wait()

    def one_member(k, carry):
        field = control[k]
        field_head = field.astype(BF16)
        field_rest = (field - field_head.astype(F32)).astype(BF16)
        two = jnp.dot(heads, field_head, preferred_element_type=F32)
        sum_ = two[:64] + two[64:] + jnp.dot(head, field_rest, preferred_element_type=F32)
        localized[pl.ds(pl.multiple_of(k * 64, 64), 64), :] = sum_.astype(BF16)
        return carry

    lax.fori_loop(0, 8, one_member, 0)
    for load in first_loads[1:]:
        load.wait()

    def increment(q):
        at = pl.ds(pl.multiple_of((e + q) % SIDE * 256, 256), 256)
        spread = jnp.dot(localized[...], horizontal[:, at], preferred_element_type=F32)
        sum_ = pert[0, :, at].astype(F32) * spread[:64]
        for k in range(1, 8):
            sum_ = sum_ + pert[k, :, at].astype(F32) * spread[k * 64 : (k + 1) * 64]
        return sum_ * factor

    for n, q in enumerate((2, 1, 3)):
        sum_ = increment(q)
        for h in range(2):
            sendy[q - 1, h] = sum_[:, h * 128 : (h + 1) * 128].astype(BF16)
        if n == 0:
            pl.semaphore_wait(barrier, len(greet))
        go(("yr", q))
    whole = increment(0)
    got(("yr", 1), ("yr", 3), ("yr", 2))
    for h in range(2):
        half = whole[:, h * 128 : (h + 1) * 128]
        for q in range(3):
            half = half + recvy[q, h].astype(F32)
        own[0][0][2 * e + h] = half.astype(BF16)
    go(("yg", 2), ("yg", 1), ("yg", 3))
    lax.fori_loop(0, slots // 8, tables, 0)
    for load in loads[:LOADS]:
        load.wait()
    turn(0, slots // 2)
    got(("yg", 1), ("yg", 3), ("yg", 2))
    go(("A", 3, "l"), ("A", 1, "h"), ("A", 3, "h"), ("A", 1, "l"))
    go(("B", 3, 0, "l"), ("B", 1, 0, "h"), ("C", 0, 0), ("B", 3, 0, "h"), ("B", 1, 0, "l"))
    turn(slots // 2, slots // 2)
    for load in loads[LOADS:]:
        load.wait()
    for f in range(2):
        chain[f * 9 + 8] = jnp.zeros((64, 128), F32)

    def forward(r, rho):
        if r == 0:
            if rho == 3:
                got(("A", 3, "l"))
                go("A2a", ("B", 3, 3, "l"))
            else:
                got(("A", 1, "h"))
                go("A2b", ("B", 1, 1, "h"))
        else:
            got(("B", r, rho, "l" if r == 3 else "h"))
            go(("F", 0 if r == 3 else 1, rho))

    def complete(r, rho):
        if r == 0 and rho == 2:
            got("A2a")
            go(("B", 3, 2, "l"))
            got("A2b")
            go(("B", 1, 2, "h"), ("B", 1, 2, "l"), ("B", 3, 2, "h"))
        elif r == 0 and rho == 3:
            got(("A", 3, "h"))
            go(("B", 1, 3, "h"), ("B", 3, 3, "h"), ("B", 1, 3, "l"))
        elif r == 0:
            got(("A", 1, "l"))
            go(("B", 3, 1, "l"), ("B", 1, 1, "l"), ("B", 3, 1, "h"))
        elif r == 2:
            got(("F", 0, rho), ("F", 1, rho))
        else:
            got(("B", r, rho, "h" if r == 3 else "l"))
        go(("C", r, rho))

    def event(i):
        for whole_tile, r, rho in ARRIVE.get(i, ()):
            (complete if whole_tile else forward)(r, rho)
        if i == 13:
            for rho in LATE:
                go(("R0u", rho), ("R1u", rho))
        if i >= 2 and ORDER[i - 2][0] == 2:
            rho = ORDER[i - 2][1]
            go(("H", 0, rho), ("H", 1, rho))
        if i < STEPS:
            r, rho = ORDER[i]
            got(("C", r, rho))
            for f, refs in ((0, own), (1, other)):
                base = slot_tile(c if f == 0 else 1 - c, r, rho) * 8
                for p in range(8):
                    picked[f * 8 + p] = refs[r][rho][block_ref[base + p]]

    def dispatch(i, first, last):
        if last - first == 1:
            event(first)
            return
        middle = (first + last) // 2

        @pl.when(i < middle)
        def _():
            dispatch(i, first, middle)

        @pl.when(i >= middle)
        def _():
            dispatch(i, middle, last)

    def add_core(i):
        pltpu.make_async_remote_copy(
            src_ref=adj_other.at[pl.ds(i * 8, 8)],
            dst_ref=core_in.at[pl.ds(i * 8, 8)],
            send_sem=ssem.at[i],
            recv_sem=rsem.at[i],
            device_id=core_dev,
            device_id_type=MESH,
        ).wait_recv()
        for k in range(8):
            both = adj_own[i * 8 + k].astype(F32) + core_in[i * 8 + k].astype(F32)
            total[i * 8 + k] = both.astype(BF16)

    def step(i, carry):
        @pl.when(i >= 2)
        def _():
            add_core(i - 2)

        dispatch(i, 0, STEPS)
        r, rho = jnp.int32(0), jnp.int32(0)
        for n, (rn, rhon) in enumerate(ORDER):
            r = jnp.where(i == n, rn, r)
            rho = jnp.where(i == n, rhon, rho)
        pairs = []
        for f in range(2):
            tile = slot_tile(c if f == 0 else 1 - c, r, rho)
            pairs.append((f, tile, pl.multiple_of(tile * 8, 8)))
        both = [(f, tile, base, p) for f, tile, base in pairs for p in range(8)]
        innov = [innov_ref[pl.ds(base, 8), :] for _, _, base in pairs]
        prec = [prec_ref[pl.ds(base, 8), :] for _, _, base in pairs]
        projs = [
            jnp.dot(picked[f * 8 + p], turned[base + p], preferred_element_type=F32)
            for f, tile, base, p in both
        ]
        deps = []
        for f, tile, base, p in both:
            model = jnp.sum(vertical[base + p] * projs[f * 8 + p], axis=0, keepdims=True)
            dep = prec[f][p : p + 1] * (model - innov[f][p : p + 1])
            deps.append(jnp.where(p < count_ref[tile], dep, 0.0))
        backs = []
        for f, tile, base, p in both:
            weighted = (vertical[base + p] * deps[f * 8 + p]).astype(BF16)
            backs.append(jnp.dot(weighted, weight[base + p], preferred_element_type=F32))
        for f, tile, base, p in both:
            back = backs[f * 8 + p]
            if p > 0:
                back = back + chain[f * 9 + prev_ref[base + p]]
            chain[f * 9 + p] = back
        for f, tile, base in pairs:
            into = adj_own if f == 0 else adj_other
            for k in range(8):
                into[i * 8 + k] = chain[f * 9 + last_ref[base + k]].astype(BF16)
        pltpu.make_async_remote_copy(
            src_ref=adj_other.at[pl.ds(i * 8, 8)],
            dst_ref=core_in.at[pl.ds(i * 8, 8)],
            send_sem=ssem.at[i],
            recv_sem=rsem.at[i],
            device_id=core_dev,
            device_id_type=MESH,
        ).start()
        return carry

    lax.fori_loop(0, STEPS, step, 0)

    for i in (STEPS, STEPS + 1):
        add_core(i - 2)
        event(i)
    for rho in LATE:
        for d, r, first, name in ((0, 1, 0, "R0a"), (1, 3, 4, "R1a")):
            got(("H", d, rho))
            for b in range(4):
                at = STEP_OF[r, rho] * 8 + first + b
                sum_ = total[at].astype(F32) + half_in[d * 16 + rho * 4 + b].astype(F32)
                total[at] = sum_.astype(BF16)
            go((name, rho))
    for rho in (1, 3, 2, 0):
        got(("R0u", rho), ("R0a", rho), ("R1u", rho), ("R1a", rho))
        for k in range(8):
            sum_ = (
                total[STEP_OF[0, rho] * 8 + k].astype(F32)
                + row_in[rho * 8 + k].astype(F32)
                + row_in[32 + rho * 8 + k].astype(F32)
            )
            if rho == 0:
                unit[k] = sum_
            else:
                plane[rho * 8 + k] = sum_.astype(BF16)
        if rho == 2:
            go(*[("L2", q) for q in (2, 1, 3, 0)])
        elif rho != 0:
            go(("L", rho))
    got(("L", 1), ("L", 3))

    kept = []
    for q in (2, 1, 3, 0):
        got(("L2", q))
        for h in range(2):
            k = 2 * ((e + q) % SIDE) + h
            sum_ = unit[k]
            for n in range(3):
                sum_ = sum_ + plane_in[n * 8 + k].astype(F32)
            if q == 0:
                kept.append(sum_)
            else:
                unit_b[k] = sum_.astype(BF16)
        if q != 0:
            go(("ur", q))
    got(("ur", 1), ("ur", 3), ("ur", 2))
    for h in range(2):
        sum_ = kept[h]
        for q in range(3):
            sum_ = sum_ + unit_in[q, h].astype(F32)
        final[2 * e + h] = sum_.astype(BF16)
    go(("ug", 1), ("ug", 3), ("ug", 2))
    lv_t = loc_vertical_ref[...].T
    head_t = lv_t.astype(BF16)
    heads_t = jnp.concatenate([head_t, (lv_t - head_t.astype(F32)).astype(BF16)], axis=0)
    for q in (0, 1, 3, 2):
        if q > 0:
            got(("ug", (4 - q)))
        chunk_at = (e + q) % SIDE
        at = pl.ds(pl.multiple_of(chunk_at * 256, 256), 256)
        adjoint = jnp.concatenate(
            [final[2 * chunk_at].astype(F32), final[2 * chunk_at + 1].astype(F32)], axis=1
        )
        for k in range(8):
            field = pert[k, :, at].astype(F32) * adjoint
            field_head = field.astype(BF16)
            field_rest = (field - field_head.astype(F32)).astype(BF16)
            two = jnp.dot(heads_t, field_head, preferred_element_type=F32)
            sum_ = two[:64] + two[64:] + jnp.dot(head_t, field_rest, preferred_element_type=F32)
            out_ref[k * 64 : (k + 1) * 64, at] = sum_.astype(BF16)
    for name in ways:
        copy_of(name).wait_send()


def exchange(
    factor,
    block_column,
    tile_count,
    loc_vertical,
    innovation,
    obs_precision,
    perturbations,
    control,
    loc_horizontal,
    obs_weight,
    obs_vertical,
):
    members, levels, columns = control.shape
    slots, block, _ = obs_weight.shape
    smem = pl.BlockSpec(memory_space=pltpu.SMEM)
    vmem = pl.BlockSpec(memory_space=pltpu.VMEM)
    hbm = pl.BlockSpec(memory_space=pl.ANY)

    def blocks(*lead, dtype=BF16):
        return pltpu.VMEM((*lead, levels, block), dtype)

    return pl.pallas_call(
        functools.partial(exchange_kernel, factor),
        out_shape=jax.ShapeDtypeStruct((members * levels, columns), BF16),
        in_specs=[smem] * 2 + [vmem] * 3 + [hbm] * 5,
        out_specs=vmem,
        scratch_shapes=[blocks(8) for _ in range(32)]
        + [
            pltpu.VMEM((members, levels, columns), BF16),
            pltpu.VMEM((members, levels, columns), F32),
            pltpu.VMEM((columns, columns), BF16),
            pltpu.VMEM((members * levels, columns), BF16),
            pltpu.SMEM((slots,), jnp.int32),
            pltpu.SMEM((slots,), jnp.int32),
            pltpu.VMEM((slots, block, block), BF16),
            pltpu.VMEM((slots, block, block), BF16),
            pltpu.VMEM((slots, levels, block), F32),
            blocks(3, 2),
            blocks(3, 2),
            blocks(16),
            blocks(18, dtype=F32),
            blocks(128),
            blocks(128),
            blocks(128),
            blocks(128),
            blocks(32),
            blocks(64),
            blocks(32),
            blocks(24),
            blocks(8, dtype=F32),
            blocks(8),
            blocks(3, 2),
            blocks(8),
            pltpu.SemaphoreType.DMA((2 * LOADS + 3,)),
            pltpu.SemaphoreType.DMA((128,)),
            pltpu.SemaphoreType.DMA((128,)),
        ],
        compiler_params=pltpu.CompilerParams(
            collective_id=0, has_side_effects=True, vmem_limit_bytes=56 * 1024 * 1024
        ),
    )(
        block_column,
        tile_count,
        loc_vertical,
        innovation,
        obs_precision,
        perturbations,
        control,
        loc_horizontal,
        obs_weight,
        obs_vertical,
    )


def on_device(
    perturbations,
    control,
    loc_vertical,
    loc_horizontal,
    obs_weight,
    obs_vertical,
    innovation,
    obs_precision,
    block_column,
    tile_count,
):
    members_dev, levels, columns = control.shape
    ens_total = lax.axis_size("ens")
    factor = 1.0 / math.sqrt(members_dev * ens_total - 1)
    back_vertical = exchange(
        factor,
        block_column,
        tile_count,
        loc_vertical,
        innovation,
        obs_precision,
        perturbations,
        control,
        loc_horizontal,
        obs_weight,
        obs_vertical,
    )
    spread_back = jnp.einsum(
        "rc,dc->rd", back_vertical, loc_horizontal, preferred_element_type=F32
    )
    flat_control = control.reshape(members_dev * levels, columns)
    return (flat_control + factor * spread_back).reshape(control.shape)


def solution(mesh):
    in_specs = (
        P("ens", None, "tile"),
        P("ens", None, "tile"),
        P(),
        P(),
        P(("ens", "tile"), None, None),
        P(("ens", "tile"), None, None),
        P(("ens", "tile"), None),
        P(("ens", "tile"), None),
        P(("ens", "tile")),
        P(("ens", "tile")),
    )
    out_specs = P("ens", None, "tile")
    return jax.shard_map(
        on_device, mesh=mesh, in_specs=in_specs, out_specs=out_specs, check_vma=False
    )
```

```python
import functools
import math

import jax
import jax.numpy as jnp
from jax import lax
from jax.experimental import pallas as pl
from jax.experimental.pallas import tpu as pltpu
from jax.sharding import PartitionSpec as P

MESH = pl.DeviceIdType.MESH
F32 = jnp.float32
BF16 = jnp.bfloat16
SIDE = 4
LOADS = 4


def tile_of(z, x, c):
    return (z * SIDE + x) * 2 + c


ORDER = (
    (0, 0), (0, 1), (0, 3), (3, 0), (1, 0), (0, 2), (3, 1), (1, 1),
    (3, 3), (1, 3), (3, 2), (1, 2), (2, 0), (2, 1), (2, 3), (2, 2),
)
ARRIVE = {
    1: (
        (0, 0, 3), (0, 0, 1), (1, 0, 3), (1, 0, 1),
        (0, 3, 0), (0, 1, 0), (1, 3, 0), (1, 1, 0),
    ),
    3: ((1, 0, 2),),
    5: ((0, 3, 3), (0, 1, 1), (0, 3, 1), (0, 1, 3), (1, 3, 1), (1, 1, 1)),
    7: ((1, 3, 3), (1, 1, 3)),
    8: ((0, 3, 2), (0, 1, 2)),
    9: ((1, 3, 2), (1, 1, 2)),
    10: ((1, 2, 0),),
    12: ((1, 2, 1),),
    13: ((1, 2, 3),),
    14: ((1, 2, 2),),
}
STEP_OF = {place: i for i, place in enumerate(ORDER)}
STEPS = len(ORDER)
STRAIGHT = STEPS - 2
LATE = (0, 1, 3, 2)


def exchange_kernel(
    factor,
    block_ref,
    count_ref,
    loc_vertical_ref,
    innov_ref,
    prec_ref,
    pert_hbm,
    control_hbm,
    horizontal_hbm,
    weight_hbm,
    vertical_hbm,
    out_ref,
    *scratch,
):
    rest = list(scratch)
    own = [[rest.pop(0) for _ in range(4)] for _ in range(4)]
    other = [[rest.pop(0) for _ in range(4)] for _ in range(4)]
    (
        pert,
        control,
        horizontal,
        localized,
        prev_ref,
        last_ref,
        weight,
        turned,
        vertical,
        sendy,
        recvy,
        picked,
        chain,
        adj_own,
        adj_other,
        core_in,
        total,
        half_in,
        half_other,
        row_in,
        plane,
        plane_in,
        unit,
        unit_b,
        unit_in,
        final,
        load_sem,
        ssem,
        rsem,
    ) = rest

    e = lax.axis_index("ens")
    t = lax.axis_index("tile")
    c = t % 2
    x = (t // 2) % SIDE
    z = t // (2 * SIDE)

    first_loads = []
    for n, (src, dst) in enumerate(
        ((control_hbm, control), (horizontal_hbm, horizontal), (pert_hbm, pert))
    ):
        copy = pltpu.make_async_copy(src, dst, load_sem.at[2 * LOADS + n])
        copy.start()
        first_loads.append(copy)
    slots = weight.shape[0]
    chunk = slots // LOADS
    loads = []
    for n, (src, dst) in enumerate(((weight_hbm, weight), (vertical_hbm, vertical))):
        for i in range(LOADS):
            at = pl.ds(i * chunk, chunk)
            copy = pltpu.make_async_copy(src.at[at], dst.at[at], load_sem.at[n * LOADS + i])
            loads.append(copy)

    def beside(zq, xq):
        return tile_of((z + zq) % SIDE, (x + xq) % SIDE, c)

    y_dev = {q: ((e + q) % SIDE, t) for q in (1, 2, 3)}
    hi_dev = {q: (e, jnp.where(c == 0, beside(q, 0), beside(0, q))) for q in (1, 3)}
    lo_dev = {q: (e, jnp.where(c == 0, beside(0, q), beside(q, 0))) for q in (1, 2, 3)}
    core_dev = (e, tile_of(z, x, 1 - c))
    swap = 1 - 2 * c
    hi_cross = {q: (e, hi_dev[q][1] + swap) for q in (1, 3)}
    lo_cross = {q: (e, lo_dev[q][1] + swap) for q in (1, 3)}

    def slot_tile(core, r, rho):
        hi = (jnp.where(core == 0, z, x) + r) % SIDE
        lo = (jnp.where(core == 0, x, z) + rho) % SIDE
        return jnp.where(core == 0, tile_of(hi, lo, 0), tile_of(lo, hi, 1))

    barrier = pltpu.get_barrier_semaphore()
    greet = [*y_dev.values(), *hi_dev.values(), *lo_dev.values(), core_dev]
    greet += [*hi_cross.values(), *lo_cross.values()]
    for dev in greet:
        pl.semaphore_signal(barrier, inc=1, device_id=dev, device_id_type=MESH)
    ways = {}

    def way(name, src, dst, dev):
        ways[name] = (len(ways), src, dst, dev)

    def copy_of(name):
        n, src, dst, dev = ways[name]
        return pltpu.make_async_remote_copy(
            src_ref=src,
            dst_ref=dst,
            send_sem=ssem.at[n],
            recv_sem=rsem.at[n],
            device_id=dev,
            device_id_type=MESH,
        )

    def go(*names):
        for name in names:
            copy_of(name).start()

    def got(*names):
        for name in names:
            copy_of(name).wait_recv()

    low, high = pl.ds(0, 4), pl.ds(4, 4)
    for i in range(STRAIGHT):
        at = pl.ds(i * 8, 8)
        way(("D", i), adj_other.at[at], core_in.at[at], core_dev)
    mine = own[0][0].at[pl.ds(2 * e, 2)]
    for q in (1, 2, 3):
        way(("yr", q), sendy.at[q - 1], recvy.at[q - 1], y_dev[q])
        way(("yg", q), mine, mine, y_dev[q])
    for part, at in (("l", low), ("h", high)):
        way(("A", 3, part), own[0][0].at[at], own[0][3].at[at], lo_dev[1])
        way(("A", 1, part), own[0][0].at[at], own[0][1].at[at], lo_dev[3])
    way("A2a", own[0][3].at[low], own[0][2].at[low], lo_dev[1])
    way("A2b", own[0][1].at[high], own[0][2].at[high], lo_dev[3])
    for rho in range(4):
        for part, at in (("l", low), ("h", high)):
            way(("B", 3, rho, part), own[0][rho].at[at], own[3][rho].at[at], hi_dev[1])
            way(("B", 1, rho, part), own[0][rho].at[at], own[1][rho].at[at], hi_dev[3])
        way(("F", 0, rho), own[3][rho].at[low], own[2][rho].at[low], hi_dev[1])
        way(("F", 1, rho), own[1][rho].at[high], own[2][rho].at[high], hi_dev[3])
        for r in range(4):
            if (r, rho) != (2, 2):
                way(("C", r, rho), own[r][rho], other[r][rho], core_dev)

    def total_at(r, rho, first, count):
        return total.at[pl.ds(STEP_OF[r, rho] * 8 + first, count)]

    way(("FC", 0), own[3][2].at[low], other[2][2].at[low], hi_cross[1])
    way(("FC", 1), own[1][2].at[high], other[2][2].at[high], hi_cross[3])
    for i in range(STRAIGHT, STEPS):
        for d, q in ((0, 1), (1, 3)):
            src = adj_other.at[pl.ds(i * 8 + d * 4, 4)]
            dst = half_other.at[pl.ds((i - STRAIGHT) * 8 + d * 4, 4)]
            way(("HD", d, i), src, dst, lo_cross[q])
    for rho in range(4):
        i = STEP_OF[2, rho]
        src = total if i < STRAIGHT else adj_own
        for d, q in ((0, 1), (1, 3)):
            dst = half_in.at[pl.ds(d * 16 + rho * 4, 4)]
            way(("H", d, rho), src.at[pl.ds(i * 8 + d * 4, 4)], dst, hi_dev[q])
        way(("R0u", rho), total_at(1, rho, 4, 4), row_in.at[pl.ds(rho * 8 + 4, 4)], hi_dev[1])
        way(("R0a", rho), total_at(1, rho, 0, 4), row_in.at[pl.ds(rho * 8, 4)], hi_dev[1])
        way(("R1u", rho), total_at(3, rho, 0, 4), row_in.at[pl.ds(32 + rho * 8, 4)], hi_dev[3])
        way(("R1a", rho), total_at(3, rho, 4, 4), row_in.at[pl.ds(32 + rho * 8 + 4, 4)], hi_dev[3])
    for q in range(4):
        at = 2 * ((e + q) % SIDE)
        way(("L2", q), plane.at[pl.ds(16 + at, 2)], plane_in.at[pl.ds(8 + at, 2)], lo_dev[2])
    for rho in (1, 3):
        way(("L", rho), plane.at[pl.ds(rho * 8, 8)], plane_in.at[pl.ds((rho - 1) * 8, 8)], lo_dev[rho])
    done = final.at[pl.ds(2 * e, 2)]
    for q in (1, 2, 3):
        way(("ur", q), unit_b.at[pl.ds(2 * ((e + q) % SIDE), 2)], unit_in.at[q - 1], y_dev[q])
        way(("ug", q), done, done, y_dev[q])

    def turn(first, count):
        def some(i, carry):
            for u in range(8):
                turned[i * 8 + u] = weight[i * 8 + u].T
            return carry

        lax.fori_loop(first // 8, (first + count) // 8, some, 0)

    def tables(j, carry):
        base = j * 8
        columns = [block_ref[base + p] for p in range(8)]
        for p in range(8):
            before = jnp.int32(8)
            for n in range(p):
                before = jnp.where(columns[n] == columns[p], n, before)
            prev_ref[base + p] = before
        for k in range(8):
            latest = jnp.int32(8)
            for n in range(8):
                latest = jnp.where(columns[n] == k, n, latest)
            last_ref[base + k] = latest
        return carry

    lv = loc_vertical_ref[...]
    head = lv.astype(BF16)
    heads = jnp.concatenate([head, (lv - head.astype(F32)).astype(BF16)], axis=0)
    first_loads[0].wait()

    def one_member(k, carry):
        field = control[k]
        field_head = field.astype(BF16)
        field_rest = (field - field_head.astype(F32)).astype(BF16)
        two = jnp.dot(heads, field_head, preferred_element_type=F32)
        sum_ = two[:64] + two[64:] + jnp.dot(head, field_rest, preferred_element_type=F32)
        localized[pl.ds(pl.multiple_of(k * 64, 64), 64), :] = sum_.astype(BF16)
        return carry

    lax.fori_loop(0, 8, one_member, 0)
    for load in first_loads[1:]:
        load.wait()
    for load in loads:
        load.start()

    def increment(q):
        at = pl.ds(pl.multiple_of((e + q) % SIDE * 256, 256), 256)
        spread = jnp.dot(localized[...], horizontal[:, at], preferred_element_type=F32)
        sum_ = pert[0, :, at].astype(F32) * spread[:64]
        for k in range(1, 8):
            sum_ = sum_ + pert[k, :, at].astype(F32) * spread[k * 64 : (k + 1) * 64]
        return sum_ * factor

    for n, q in enumerate((2, 1, 3)):
        sum_ = increment(q)
        for h in range(2):
            sendy[q - 1, h] = sum_[:, h * 128 : (h + 1) * 128].astype(BF16)
        if n == 0:
            pl.semaphore_wait(barrier, len(greet))
        go(("yr", q))
    whole = increment(0)
    got(("yr", 1), ("yr", 3), ("yr", 2))
    for h in range(2):
        half = whole[:, h * 128 : (h + 1) * 128]
        for q in range(3):
            half = half + recvy[q, h].astype(F32)
        own[0][0][2 * e + h] = half.astype(BF16)
    go(("yg", 2), ("yg", 1), ("yg", 3))
    lax.fori_loop(0, slots // 8, tables, 0)
    for load in loads[:LOADS]:
        load.wait()
    turn(0, slots // 2)
    got(("yg", 1), ("yg", 3), ("yg", 2))
    go(("A", 3, "l"), ("A", 1, "h"), ("A", 3, "h"), ("A", 1, "l"))
    go(("B", 3, 0, "l"), ("B", 1, 0, "h"), ("C", 0, 0), ("B", 3, 0, "h"), ("B", 1, 0, "l"))
    turn(slots // 2, slots // 2)
    for load in loads[LOADS:]:
        load.wait()
    for f in range(2):
        chain[f * 9 + 8] = jnp.zeros((64, 128), F32)

    def forward(r, rho):
        if r == 0:
            if rho == 3:
                got(("A", 3, "l"))
                go("A2a", ("B", 3, 3, "l"))
            else:
                got(("A", 1, "h"))
                go("A2b", ("B", 1, 1, "h"))
        else:
            got(("B", r, rho, "l" if r == 3 else "h"))
            d = 0 if r == 3 else 1
            go(("F", d, rho))
            if rho == 2:
                go(("FC", d))

    def complete(r, rho):
        if r == 0 and rho == 2:
            got("A2a")
            go(("B", 3, 2, "l"))
            got("A2b")
            go(("B", 1, 2, "h"), ("B", 1, 2, "l"), ("B", 3, 2, "h"))
        elif r == 0 and rho == 3:
            got(("A", 3, "h"))
            go(("B", 1, 3, "h"), ("B", 3, 3, "h"), ("B", 1, 3, "l"))
        elif r == 0:
            got(("A", 1, "l"))
            go(("B", 3, 1, "l"), ("B", 1, 1, "l"), ("B", 3, 1, "h"))
        elif r == 2:
            got(("F", 0, rho), ("F", 1, rho))
        else:
            got(("B", r, rho, "h" if r == 3 else "l"))
        if (r, rho) != (2, 2):
            go(("C", r, rho))

    def event(i):
        if i == 13:
            for rho in LATE:
                go(("R0u", rho), ("R1u", rho))
        if i - 2 in range(STEP_OF[2, 0], STRAIGHT):
            rho = ORDER[i - 2][1]
            go(("H", 0, rho), ("H", 1, rho))
        for whole_tile, r, rho in ARRIVE.get(i, ()):
            (complete if whole_tile else forward)(r, rho)
        if i < STEPS:
            r, rho = ORDER[i]
            if (r, rho) == (2, 2):
                got(("FC", 0), ("FC", 1))
            else:
                got(("C", r, rho))
            for f, refs in ((0, own), (1, other)):
                base = slot_tile(c if f == 0 else 1 - c, r, rho) * 8
                for p in range(8):
                    picked[f * 8 + p] = refs[r][rho][block_ref[base + p]]

    def dispatch(i, first, last):
        if last - first == 1:
            event(first)
            return
        middle = (first + last) // 2

        @pl.when(i < middle)
        def _():
            dispatch(i, first, middle)

        @pl.when(i >= middle)
        def _():
            dispatch(i, middle, last)

    def core_copy(i):
        return pltpu.make_async_remote_copy(
            src_ref=adj_other.at[pl.ds(i * 8, 8)],
            dst_ref=core_in.at[pl.ds(i * 8, 8)],
            send_sem=ssem.at[i],
            recv_sem=rsem.at[i],
            device_id=core_dev,
            device_id_type=MESH,
        )

    def add_core(i):
        core_copy(i).wait_recv()
        for k in range(8):
            both = adj_own[i * 8 + k].astype(F32) + core_in[i * 8 + k].astype(F32)
            total[i * 8 + k] = both.astype(BF16)

    def step(i, carry):
        @pl.when(i >= 2)
        def _():
            add_core(i - 2)

        dispatch(i, 0, STEPS)
        r, rho = jnp.int32(0), jnp.int32(0)
        for n, (rn, rhon) in enumerate(ORDER):
            r = jnp.where(i == n, rn, r)
            rho = jnp.where(i == n, rhon, rho)
        pairs = []
        for f in range(2):
            tile = slot_tile(c if f == 0 else 1 - c, r, rho)
            pairs.append((f, tile, pl.multiple_of(tile * 8, 8)))
        both = [(f, tile, base, p) for f, tile, base in pairs for p in range(8)]
        innov = [innov_ref[pl.ds(base, 8), :] for _, _, base in pairs]
        prec = [prec_ref[pl.ds(base, 8), :] for _, _, base in pairs]
        projs = [
            jnp.dot(picked[f * 8 + p], turned[base + p], preferred_element_type=F32)
            for f, tile, base, p in both
        ]
        deps = []
        for f, tile, base, p in both:
            model = jnp.sum(vertical[base + p] * projs[f * 8 + p], axis=0, keepdims=True)
            dep = prec[f][p : p + 1] * (model - innov[f][p : p + 1])
            deps.append(jnp.where(p < count_ref[tile], dep, 0.0))
        backs = []
        for f, tile, base, p in both:
            weighted = (vertical[base + p] * deps[f * 8 + p]).astype(BF16)
            backs.append(jnp.dot(weighted, weight[base + p], preferred_element_type=F32))
        for f, tile, base, p in both:
            back = backs[f * 8 + p]
            if p > 0:
                back = back + chain[f * 9 + prev_ref[base + p]]
            chain[f * 9 + p] = back
        for f, tile, base in pairs:
            into = adj_own if f == 0 else adj_other
            for k in range(8):
                into[i * 8 + k] = chain[f * 9 + last_ref[base + k]].astype(BF16)

        @pl.when(i < STRAIGHT)
        def _():
            core_copy(i).start()

        for last in range(STRAIGHT, STEPS):

            @pl.when(i == last)
            def _():
                for d in range(2):
                    go(("H", d, ORDER[last][1]), ("HD", d, last))

        return carry

    lax.fori_loop(0, STEPS, step, 0)

    for rho in LATE:
        for d, r, first, name in ((0, 1, 0, "R0a"), (1, 3, 4, "R1a")):
            got(("H", d, rho))
            straight = STEP_OF[2, rho] - STRAIGHT
            if straight >= 0:
                got(("HD", d, STEP_OF[2, rho]))
            for b in range(4):
                at = STEP_OF[r, rho] * 8 + first + b
                sum_ = total[at].astype(F32) + half_in[d * 16 + rho * 4 + b].astype(F32)
                if straight >= 0:
                    sum_ = sum_ + half_other[straight * 8 + d * 4 + b].astype(F32)
                total[at] = sum_.astype(BF16)
            go((name, rho))
    for rho in (1, 3, 2, 0):
        got(("R0u", rho), ("R0a", rho), ("R1u", rho), ("R1a", rho))
        for k in range(8):
            sum_ = (
                total[STEP_OF[0, rho] * 8 + k].astype(F32)
                + row_in[rho * 8 + k].astype(F32)
                + row_in[32 + rho * 8 + k].astype(F32)
            )
            if rho == 0:
                unit[k] = sum_
            else:
                plane[rho * 8 + k] = sum_.astype(BF16)
        if rho == 2:
            go(*[("L2", q) for q in (2, 1, 3, 0)])
        elif rho != 0:
            go(("L", rho))
    got(("L", 1), ("L", 3))

    kept = []
    for q in (2, 1, 3, 0):
        got(("L2", q))
        for h in range(2):
            k = 2 * ((e + q) % SIDE) + h
            sum_ = unit[k]
            for n in range(3):
                sum_ = sum_ + plane_in[n * 8 + k].astype(F32)
            if q == 0:
                kept.append(sum_)
            else:
                unit_b[k] = sum_.astype(BF16)
        if q != 0:
            go(("ur", q))
    got(("ur", 1), ("ur", 3), ("ur", 2))
    for h in range(2):
        sum_ = kept[h]
        for q in range(3):
            sum_ = sum_ + unit_in[q, h].astype(F32)
        final[2 * e + h] = sum_.astype(BF16)
    go(("ug", 1), ("ug", 3), ("ug", 2))
    lv_t = loc_vertical_ref[...].T
    head_t = lv_t.astype(BF16)
    heads_t = jnp.concatenate([head_t, (lv_t - head_t.astype(F32)).astype(BF16)], axis=0)
    for q in (0, 1, 3, 2):
        if q > 0:
            got(("ug", (4 - q)))
        chunk_at = (e + q) % SIDE
        at = pl.ds(pl.multiple_of(chunk_at * 256, 256), 256)
        adjoint = jnp.concatenate(
            [final[2 * chunk_at].astype(F32), final[2 * chunk_at + 1].astype(F32)], axis=1
        )
        for k in range(8):
            field = pert[k, :, at].astype(F32) * adjoint
            field_head = field.astype(BF16)
            field_rest = (field - field_head.astype(F32)).astype(BF16)
            two = jnp.dot(heads_t, field_head, preferred_element_type=F32)
            sum_ = two[:64] + two[64:] + jnp.dot(head_t, field_rest, preferred_element_type=F32)
            out_ref[k * 64 : (k + 1) * 64, at] = sum_.astype(BF16)
    for name in ways:
        copy_of(name).wait_send()


def exchange(
    factor,
    block_column,
    tile_count,
    loc_vertical,
    innovation,
    obs_precision,
    perturbations,
    control,
    loc_horizontal,
    obs_weight,
    obs_vertical,
):
    members, levels, columns = control.shape
    slots, block, _ = obs_weight.shape
    smem = pl.BlockSpec(memory_space=pltpu.SMEM)
    vmem = pl.BlockSpec(memory_space=pltpu.VMEM)
    hbm = pl.BlockSpec(memory_space=pl.ANY)

    def blocks(*lead, dtype=BF16):
        return pltpu.VMEM((*lead, levels, block), dtype)

    return pl.pallas_call(
        functools.partial(exchange_kernel, factor),
        out_shape=jax.ShapeDtypeStruct((members * levels, columns), BF16),
        in_specs=[smem] * 2 + [vmem] * 3 + [hbm] * 5,
        out_specs=vmem,
        scratch_shapes=[blocks(8) for _ in range(32)]
        + [
            pltpu.VMEM((members, levels, columns), BF16),
            pltpu.VMEM((members, levels, columns), F32),
            pltpu.VMEM((columns, columns), BF16),
            pltpu.VMEM((members * levels, columns), BF16),
            pltpu.SMEM((slots,), jnp.int32),
            pltpu.SMEM((slots,), jnp.int32),
            pltpu.VMEM((slots, block, block), BF16),
            pltpu.VMEM((slots, block, block), BF16),
            pltpu.VMEM((slots, levels, block), F32),
            blocks(3, 2),
            blocks(3, 2),
            blocks(16),
            blocks(18, dtype=F32),
            blocks(128),
            blocks(128),
            blocks(128),
            blocks(128),
            blocks(32),
            blocks(16),
            blocks(64),
            blocks(32),
            blocks(24),
            blocks(8, dtype=F32),
            blocks(8),
            blocks(3, 2),
            blocks(8),
            pltpu.SemaphoreType.DMA((2 * LOADS + 3,)),
            pltpu.SemaphoreType.DMA((128,)),
            pltpu.SemaphoreType.DMA((128,)),
        ],
        compiler_params=pltpu.CompilerParams(
            collective_id=0, has_side_effects=True, vmem_limit_bytes=56 * 1024 * 1024
        ),
    )(
        block_column,
        tile_count,
        loc_vertical,
        innovation,
        obs_precision,
        perturbations,
        control,
        loc_horizontal,
        obs_weight,
        obs_vertical,
    )


def on_device(
    perturbations,
    control,
    loc_vertical,
    loc_horizontal,
    obs_weight,
    obs_vertical,
    innovation,
    obs_precision,
    block_column,
    tile_count,
):
    members_dev, levels, columns = control.shape
    ens_total = lax.axis_size("ens")
    factor = 1.0 / math.sqrt(members_dev * ens_total - 1)
    back_vertical = exchange(
        factor,
        block_column,
        tile_count,
        loc_vertical,
        innovation,
        obs_precision,
        perturbations,
        control,
        loc_horizontal,
        obs_weight,
        obs_vertical,
    )
    spread_back = jnp.einsum(
        "rc,dc->rd", back_vertical, loc_horizontal, preferred_element_type=F32
    )
    flat_control = control.reshape(members_dev * levels, columns)
    return (flat_control + factor * spread_back).reshape(control.shape)


def solution(mesh):
    in_specs = (
        P("ens", None, "tile"),
        P("ens", None, "tile"),
        P(),
        P(),
        P(("ens", "tile"), None, None),
        P(("ens", "tile"), None, None),
        P(("ens", "tile"), None),
        P(("ens", "tile"), None),
        P(("ens", "tile")),
        P(("ens", "tile")),
    )
    out_specs = P("ens", None, "tile")
    return jax.shard_map(
        on_device, mesh=mesh, in_specs=in_specs, out_specs=out_specs, check_vma=False
    )
```

```python
import functools
import math

import jax
import jax.numpy as jnp
from jax import lax
from jax.experimental import pallas as pl
from jax.experimental.pallas import tpu as pltpu
from jax.sharding import PartitionSpec as P

MESH = pl.DeviceIdType.MESH
F32 = jnp.float32
BF16 = jnp.bfloat16
SIDE = 4
LOADS = 4


def tile_of(z, x, c):
    return (z * SIDE + x) * 2 + c


ORDER = (
    (0, 0), (0, 1), (0, 3), (3, 0), (1, 0), (0, 2), (3, 1), (1, 1),
    (3, 3), (1, 3), (3, 2), (1, 2), (2, 0), (2, 1), (2, 3), (2, 2),
)
ARRIVE = {
    1: (
        (0, 0, 3), (0, 0, 1), (1, 0, 3), (1, 0, 1),
        (0, 3, 0), (0, 1, 0), (1, 3, 0), (1, 1, 0),
    ),
    3: ((1, 0, 2),),
    5: ((0, 3, 3), (0, 1, 1), (0, 3, 1), (0, 1, 3), (1, 3, 1), (1, 1, 1)),
    7: ((1, 3, 3), (1, 1, 3)),
    8: ((0, 3, 2), (0, 1, 2)),
    9: ((1, 3, 2), (1, 1, 2)),
    10: ((1, 2, 0),),
    12: ((1, 2, 1),),
    13: ((1, 2, 3),),
    14: ((1, 2, 2),),
}
STEP_OF = {place: i for i, place in enumerate(ORDER)}
STEPS = len(ORDER)
LATE = (0, 1, 3, 2)


def exchange_kernel(
    factor,
    block_ref,
    count_ref,
    loc_vertical_ref,
    innov_ref,
    prec_ref,
    pert_hbm,
    control_hbm,
    horizontal_hbm,
    weight_hbm,
    vertical_hbm,
    out_ref,
    *scratch,
):
    rest = list(scratch)
    own = [[rest.pop(0) for _ in range(4)] for _ in range(4)]
    other = [[rest.pop(0) for _ in range(4)] for _ in range(4)]
    (
        pert,
        control,
        horizontal,
        localized,
        prev_ref,
        last_ref,
        weight,
        turned,
        vertical,
        sendy,
        recvy,
        picked,
        chain,
        adj_own,
        adj_other,
        core_in,
        total,
        half_in,
        row_in,
        plane,
        plane_in,
        unit,
        unit_b,
        unit_in,
        final,
        load_sem,
        ssem,
        rsem,
    ) = rest

    e = lax.axis_index("ens")
    t = lax.axis_index("tile")
    c = t % 2
    x = (t // 2) % SIDE
    z = t // (2 * SIDE)

    first_loads = []
    for n, (src, dst) in enumerate(
        ((control_hbm, control), (horizontal_hbm, horizontal), (pert_hbm, pert))
    ):
        copy = pltpu.make_async_copy(src, dst, load_sem.at[2 * LOADS + n])
        copy.start()
        first_loads.append(copy)
    slots = weight.shape[0]
    chunk = slots // LOADS
    loads = []
    for n, (src, dst) in enumerate(((weight_hbm, weight), (vertical_hbm, vertical))):
        for i in range(LOADS):
            at = pl.ds(i * chunk, chunk)
            copy = pltpu.make_async_copy(src.at[at], dst.at[at], load_sem.at[n * LOADS + i])
            copy.start()
            loads.append(copy)

    def beside(zq, xq):
        return tile_of((z + zq) % SIDE, (x + xq) % SIDE, c)

    y_dev = {q: ((e + q) % SIDE, t) for q in (1, 2, 3)}
    hi_dev = {q: (e, jnp.where(c == 0, beside(q, 0), beside(0, q))) for q in (1, 3)}
    lo_dev = {q: (e, jnp.where(c == 0, beside(0, q), beside(q, 0))) for q in (1, 2, 3)}
    core_dev = (e, tile_of(z, x, 1 - c))

    def slot_tile(core, r, rho):
        hi = (jnp.where(core == 0, z, x) + r) % SIDE
        lo = (jnp.where(core == 0, x, z) + rho) % SIDE
        return jnp.where(core == 0, tile_of(hi, lo, 0), tile_of(lo, hi, 1))

    barrier = pltpu.get_barrier_semaphore()
    greet = [*y_dev.values(), *hi_dev.values(), *lo_dev.values(), core_dev]
    for dev in greet:
        pl.semaphore_signal(barrier, inc=1, device_id=dev, device_id_type=MESH)
    ways = {}

    def way(name, src, dst, dev):
        ways[name] = (len(ways), src, dst, dev)

    def copy_of(name):
        n, src, dst, dev = ways[name]
        return pltpu.make_async_remote_copy(
            src_ref=src,
            dst_ref=dst,
            send_sem=ssem.at[n],
            recv_sem=rsem.at[n],
            device_id=dev,
            device_id_type=MESH,
        )

    def go(*names):
        for name in names:
            copy_of(name).start()

    def got(*names):
        for name in names:
            copy_of(name).wait_recv()

    low, high = pl.ds(0, 4), pl.ds(4, 4)
    for i, (r, rho) in enumerate(ORDER):
        at = pl.ds(i * 8, 8)
        way(("D", i), adj_other.at[at], core_in.at[at], core_dev)
    mine = own[0][0].at[pl.ds(2 * e, 2)]
    for q in (1, 2, 3):
        way(("yr", q), sendy.at[q - 1], recvy.at[q - 1], y_dev[q])
        way(("yg", q), mine, mine, y_dev[q])
    for part, at in (("l", low), ("h", high)):
        way(("A", 3, part), own[0][0].at[at], own[0][3].at[at], lo_dev[1])
        way(("A", 1, part), own[0][0].at[at], own[0][1].at[at], lo_dev[3])
    way("A2a", own[0][3].at[low], own[0][2].at[low], lo_dev[1])
    way("A2b", own[0][1].at[high], own[0][2].at[high], lo_dev[3])
    for rho in range(4):
        for part, at in (("l", low), ("h", high)):
            way(("B", 3, rho, part), own[0][rho].at[at], own[3][rho].at[at], hi_dev[1])
            way(("B", 1, rho, part), own[0][rho].at[at], own[1][rho].at[at], hi_dev[3])
        way(("F", 0, rho), own[3][rho].at[low], own[2][rho].at[low], hi_dev[1])
        way(("F", 1, rho), own[1][rho].at[high], own[2][rho].at[high], hi_dev[3])
        for r in range(4):
            way(("C", r, rho), own[r][rho], other[r][rho], core_dev)

    def total_at(r, rho, first, count):
        return total.at[pl.ds(STEP_OF[r, rho] * 8 + first, count)]

    for rho in range(4):
        to_next, to_back = row_in.at[pl.ds(rho * 8, 8)], row_in.at[pl.ds(32 + rho * 8, 8)]
        way(("H", 0, rho), total_at(2, rho, 0, 4), half_in.at[pl.ds(rho * 4, 4)], hi_dev[1])
        way(("H", 1, rho), total_at(2, rho, 4, 4), half_in.at[pl.ds(16 + rho * 4, 4)], hi_dev[3])
        way(("R0u", rho), total_at(1, rho, 4, 4), row_in.at[pl.ds(rho * 8 + 4, 4)], hi_dev[1])
        way(("R0a", rho), total_at(1, rho, 0, 4), row_in.at[pl.ds(rho * 8, 4)], hi_dev[1])
        way(("R1u", rho), total_at(3, rho, 0, 4), row_in.at[pl.ds(32 + rho * 8, 4)], hi_dev[3])
        way(("R1a", rho), total_at(3, rho, 4, 4), row_in.at[pl.ds(32 + rho * 8 + 4, 4)], hi_dev[3])
    for q in range(4):
        at = 2 * ((e + q) % SIDE)
        way(("L2", q), plane.at[pl.ds(16 + at, 2)], plane_in.at[pl.ds(8 + at, 2)], lo_dev[2])
    for rho in (1, 3):
        way(("L", rho), plane.at[pl.ds(rho * 8, 8)], plane_in.at[pl.ds((rho - 1) * 8, 8)], lo_dev[rho])
    done = final.at[pl.ds(2 * e, 2)]
    for q in (1, 2, 3):
        way(("ur", q), unit_b.at[pl.ds(2 * ((e + q) % SIDE), 2)], unit_in.at[q - 1], y_dev[q])
        way(("ug", q), done, done, y_dev[q])

    def turn(first, count):
        def some(i, carry):
            for u in range(8):
                turned[i * 8 + u] = weight[i * 8 + u].T
            return carry

        lax.fori_loop(first // 8, (first + count) // 8, some, 0)

    def tables(j, carry):
        base = j * 8
        columns = [block_ref[base + p] for p in range(8)]
        for p in range(8):
            before = jnp.int32(8)
            for n in range(p):
                before = jnp.where(columns[n] == columns[p], n, before)
            prev_ref[base + p] = before
        for k in range(8):
            latest = jnp.int32(8)
            for n in range(8):
                latest = jnp.where(columns[n] == k, n, latest)
            last_ref[base + k] = latest
        return carry

    lv = loc_vertical_ref[...]
    head = lv.astype(BF16)
    heads = jnp.concatenate([head, (lv - head.astype(F32)).astype(BF16)], axis=0)
    first_loads[0].wait()

    def one_member(k, carry):
        field = control[k]
        field_head = field.astype(BF16)
        field_rest = (field - field_head.astype(F32)).astype(BF16)
        two = jnp.dot(heads, field_head, preferred_element_type=F32)
        sum_ = two[:64] + two[64:] + jnp.dot(head, field_rest, preferred_element_type=F32)
        localized[pl.ds(pl.multiple_of(k * 64, 64), 64), :] = sum_.astype(BF16)
        return carry

    lax.fori_loop(0, 8, one_member, 0)
    for load in first_loads[1:]:
        load.wait()

    def increment(q):
        at = pl.ds(pl.multiple_of((e + q) % SIDE * 256, 256), 256)
        spread = jnp.dot(localized[...], horizontal[:, at], preferred_element_type=F32)
        sum_ = pert[0, :, at].astype(F32) * spread[:64]
        for k in range(1, 8):
            sum_ = sum_ + pert[k, :, at].astype(F32) * spread[k * 64 : (k + 1) * 64]
        return sum_ * factor

    for n, q in enumerate((2, 1, 3)):
        sum_ = increment(q)
        for h in range(2):
            sendy[q - 1, h] = sum_[:, h * 128 : (h + 1) * 128].astype(BF16)
        if n == 0:
            pl.semaphore_wait(barrier, len(greet))
        go(("yr", q))
    whole = increment(0)
    got(("yr", 1), ("yr", 3), ("yr", 2))
    for h in range(2):
        half = whole[:, h * 128 : (h + 1) * 128]
        for q in range(3):
            half = half + recvy[q, h].astype(F32)
        own[0][0][2 * e + h] = half.astype(BF16)
    go(("yg", 2), ("yg", 1), ("yg", 3))
    lax.fori_loop(0, slots // 8, tables, 0)
    for load in loads[:LOADS]:
        load.wait()
    turn(0, slots // 2)
    got(("yg", 1), ("yg", 3), ("yg", 2))
    go(("A", 3, "l"), ("A", 1, "h"), ("A", 3, "h"), ("A", 1, "l"))
    go(("B", 3, 0, "l"), ("B", 1, 0, "h"), ("C", 0, 0), ("B", 3, 0, "h"), ("B", 1, 0, "l"))
    turn(slots // 2, slots // 2)
    for load in loads[LOADS:]:
        load.wait()
    for f in range(2):
        chain[f * 9 + 8] = jnp.zeros((64, 128), F32)

    def forward(r, rho):
        if r == 0:
            if rho == 3:
                got(("A", 3, "l"))
                go("A2a", ("B", 3, 3, "l"))
            else:
                got(("A", 1, "h"))
                go("A2b", ("B", 1, 1, "h"))
        else:
            got(("B", r, rho, "l" if r == 3 else "h"))
            go(("F", 0 if r == 3 else 1, rho))

    def complete(r, rho):
        if r == 0 and rho == 2:
            got("A2a")
            go(("B", 3, 2, "l"))
            got("A2b")
            go(("B", 1, 2, "h"), ("B", 1, 2, "l"), ("B", 3, 2, "h"))
        elif r == 0 and rho == 3:
            got(("A", 3, "h"))
            go(("B", 1, 3, "h"), ("B", 3, 3, "h"), ("B", 1, 3, "l"))
        elif r == 0:
            got(("A", 1, "l"))
            go(("B", 3, 1, "l"), ("B", 1, 1, "l"), ("B", 3, 1, "h"))
        elif r == 2:
            got(("F", 0, rho), ("F", 1, rho))
        else:
            got(("B", r, rho, "h" if r == 3 else "l"))
        go(("C", r, rho))

    def event(i):
        if i >= 2 and ORDER[i - 2][0] == 2:
            rho = ORDER[i - 2][1]
            go(("H", 0, rho), ("H", 1, rho))
        for whole_tile, r, rho in ARRIVE.get(i, ()):
            (complete if whole_tile else forward)(r, rho)
        if i >= 2 and ORDER[i - 2][0] in (1, 3):
            go(("R0u" if ORDER[i - 2][0] == 1 else "R1u", ORDER[i - 2][1]))
        if i < STEPS:
            r, rho = ORDER[i]
            got(("C", r, rho))
            for f, refs in ((0, own), (1, other)):
                base = slot_tile(c if f == 0 else 1 - c, r, rho) * 8
                for p in range(8):
                    picked[f * 8 + p] = refs[r][rho][block_ref[base + p]]

    def dispatch(i, first, last):
        if last - first == 1:
            event(first)
            return
        middle = (first + last) // 2

        @pl.when(i < middle)
        def _():
            dispatch(i, first, middle)

        @pl.when(i >= middle)
        def _():
            dispatch(i, middle, last)

    def add_core(i):
        pltpu.make_async_remote_copy(
            src_ref=adj_other.at[pl.ds(i * 8, 8)],
            dst_ref=core_in.at[pl.ds(i * 8, 8)],
            send_sem=ssem.at[i],
            recv_sem=rsem.at[i],
            device_id=core_dev,
            device_id_type=MESH,
        ).wait_recv()
        for k in range(8):
            both = adj_own[i * 8 + k].astype(F32) + core_in[i * 8 + k].astype(F32)
            total[i * 8 + k] = both.astype(BF16)

    def step(i, carry):
        @pl.when(i >= 2)
        def _():
            add_core(i - 2)

        dispatch(i, 0, STEPS)
        r, rho = jnp.int32(0), jnp.int32(0)
        for n, (rn, rhon) in enumerate(ORDER):
            r = jnp.where(i == n, rn, r)
            rho = jnp.where(i == n, rhon, rho)
        pairs = []
        for f in range(2):
            tile = slot_tile(c if f == 0 else 1 - c, r, rho)
            pairs.append((f, tile, pl.multiple_of(tile * 8, 8)))
        both = [(f, tile, base, p) for f, tile, base in pairs for p in range(8)]
        innov = [innov_ref[pl.ds(base, 8), :] for _, _, base in pairs]
        prec = [prec_ref[pl.ds(base, 8), :] for _, _, base in pairs]
        projs = [
            jnp.dot(picked[f * 8 + p], turned[base + p], preferred_element_type=F32)
            for f, tile, base, p in both
        ]
        deps = []
        for f, tile, base, p in both:
            model = jnp.sum(vertical[base + p] * projs[f * 8 + p], axis=0, keepdims=True)
            dep = prec[f][p : p + 1] * (model - innov[f][p : p + 1])
            deps.append(jnp.where(p < count_ref[tile], dep, 0.0))
        backs = []
        for f, tile, base, p in both:
            weighted = (vertical[base + p] * deps[f * 8 + p]).astype(BF16)
            backs.append(jnp.dot(weighted, weight[base + p], preferred_element_type=F32))
        for f, tile, base, p in both:
            back = backs[f * 8 + p]
            if p > 0:
                back = back + chain[f * 9 + prev_ref[base + p]]
            chain[f * 9 + p] = back
        for f, tile, base in pairs:
            into = adj_own if f == 0 else adj_other
            for k in range(8):
                into[i * 8 + k] = chain[f * 9 + last_ref[base + k]].astype(BF16)
        pltpu.make_async_remote_copy(
            src_ref=adj_other.at[pl.ds(i * 8, 8)],
            dst_ref=core_in.at[pl.ds(i * 8, 8)],
            send_sem=ssem.at[i],
            recv_sem=rsem.at[i],
            device_id=core_dev,
            device_id_type=MESH,
        ).start()
        return carry

    lax.fori_loop(0, STEPS, step, 0)

    for i in (STEPS, STEPS + 1):
        add_core(i - 2)
        event(i)
    for rho in LATE:
        for d, r, first, name in ((0, 1, 0, "R0a"), (1, 3, 4, "R1a")):
            got(("H", d, rho))
            for b in range(4):
                at = STEP_OF[r, rho] * 8 + first + b
                sum_ = total[at].astype(F32) + half_in[d * 16 + rho * 4 + b].astype(F32)
                total[at] = sum_.astype(BF16)
            go((name, rho))
    for rho in (1, 3, 2, 0):
        got(("R0u", rho), ("R0a", rho), ("R1u", rho), ("R1a", rho))
        for k in range(8):
            sum_ = (
                total[STEP_OF[0, rho] * 8 + k].astype(F32)
                + row_in[rho * 8 + k].astype(F32)
                + row_in[32 + rho * 8 + k].astype(F32)
            )
            if rho == 0:
                unit[k] = sum_
            else:
                plane[rho * 8 + k] = sum_.astype(BF16)
        if rho == 2:
            go(*[("L2", q) for q in (2, 1, 3, 0)])
        elif rho != 0:
            go(("L", rho))
    got(("L", 1), ("L", 3))

    kept = []
    for q in (2, 1, 3, 0):
        got(("L2", q))
        for h in range(2):
            k = 2 * ((e + q) % SIDE) + h
            sum_ = unit[k]
            for n in range(3):
                sum_ = sum_ + plane_in[n * 8 + k].astype(F32)
            if q == 0:
                kept.append(sum_)
            else:
                unit_b[k] = sum_.astype(BF16)
        if q != 0:
            go(("ur", q))
    got(("ur", 1), ("ur", 3), ("ur", 2))
    for h in range(2):
        sum_ = kept[h]
        for q in range(3):
            sum_ = sum_ + unit_in[q, h].astype(F32)
        final[2 * e + h] = sum_.astype(BF16)
    go(("ug", 1), ("ug", 3), ("ug", 2))
    lv_t = loc_vertical_ref[...].T
    head_t = lv_t.astype(BF16)
    heads_t = jnp.concatenate([head_t, (lv_t - head_t.astype(F32)).astype(BF16)], axis=0)
    for q in (0, 1, 3, 2):
        if q > 0:
            got(("ug", (4 - q)))
        chunk_at = (e + q) % SIDE
        at = pl.ds(pl.multiple_of(chunk_at * 256, 256), 256)
        adjoint = jnp.concatenate(
            [final[2 * chunk_at].astype(F32), final[2 * chunk_at + 1].astype(F32)], axis=1
        )
        for k in range(8):
            field = pert[k, :, at].astype(F32) * adjoint
            field_head = field.astype(BF16)
            field_rest = (field - field_head.astype(F32)).astype(BF16)
            two = jnp.dot(heads_t, field_head, preferred_element_type=F32)
            sum_ = two[:64] + two[64:] + jnp.dot(head_t, field_rest, preferred_element_type=F32)
            out_ref[k * 64 : (k + 1) * 64, at] = sum_.astype(BF16)
    for name in ways:
        copy_of(name).wait_send()


def exchange(
    factor,
    block_column,
    tile_count,
    loc_vertical,
    innovation,
    obs_precision,
    perturbations,
    control,
    loc_horizontal,
    obs_weight,
    obs_vertical,
):
    members, levels, columns = control.shape
    slots, block, _ = obs_weight.shape
    smem = pl.BlockSpec(memory_space=pltpu.SMEM)
    vmem = pl.BlockSpec(memory_space=pltpu.VMEM)
    hbm = pl.BlockSpec(memory_space=pl.ANY)

    def blocks(*lead, dtype=BF16):
        return pltpu.VMEM((*lead, levels, block), dtype)

    return pl.pallas_call(
        functools.partial(exchange_kernel, factor),
        out_shape=jax.ShapeDtypeStruct((members * levels, columns), BF16),
        in_specs=[smem] * 2 + [vmem] * 3 + [hbm] * 5,
        out_specs=vmem,
        scratch_shapes=[blocks(8) for _ in range(32)]
        + [
            pltpu.VMEM((members, levels, columns), BF16),
            pltpu.VMEM((members, levels, columns), F32),
            pltpu.VMEM((columns, columns), BF16),
            pltpu.VMEM((members * levels, columns), BF16),
            pltpu.SMEM((slots,), jnp.int32),
            pltpu.SMEM((slots,), jnp.int32),
            pltpu.VMEM((slots, block, block), BF16),
            pltpu.VMEM((slots, block, block), BF16),
            pltpu.VMEM((slots, levels, block), F32),
            blocks(3, 2),
            blocks(3, 2),
            blocks(16),
            blocks(18, dtype=F32),
            blocks(128),
            blocks(128),
            blocks(128),
            blocks(128),
            blocks(32),
            blocks(64),
            blocks(32),
            blocks(24),
            blocks(8, dtype=F32),
            blocks(8),
            blocks(3, 2),
            blocks(8),
            pltpu.SemaphoreType.DMA((2 * LOADS + 3,)),
            pltpu.SemaphoreType.DMA((128,)),
            pltpu.SemaphoreType.DMA((128,)),
        ],
        compiler_params=pltpu.CompilerParams(
            collective_id=0, has_side_effects=True, vmem_limit_bytes=56 * 1024 * 1024
        ),
    )(
        block_column,
        tile_count,
        loc_vertical,
        innovation,
        obs_precision,
        perturbations,
        control,
        loc_horizontal,
        obs_weight,
        obs_vertical,
    )


def on_device(
    perturbations,
    control,
    loc_vertical,
    loc_horizontal,
    obs_weight,
    obs_vertical,
    innovation,
    obs_precision,
    block_column,
    tile_count,
):
    members_dev, levels, columns = control.shape
    ens_total = lax.axis_size("ens")
    factor = 1.0 / math.sqrt(members_dev * ens_total - 1)
    back_vertical = exchange(
        factor,
        block_column,
        tile_count,
        loc_vertical,
        innovation,
        obs_precision,
        perturbations,
        control,
        loc_horizontal,
        obs_weight,
        obs_vertical,
    )
    spread_back = jnp.einsum(
        "rc,dc->rd", back_vertical, loc_horizontal, preferred_element_type=F32
    )
    flat_control = control.reshape(members_dev * levels, columns)
    return (flat_control + factor * spread_back).reshape(control.shape)


def solution(mesh):
    in_specs = (
        P("ens", None, "tile"),
        P("ens", None, "tile"),
        P(),
        P(),
        P(("ens", "tile"), None, None),
        P(("ens", "tile"), None, None),
        P(("ens", "tile"), None),
        P(("ens", "tile"), None),
        P(("ens", "tile")),
        P(("ens", "tile")),
    )
    out_specs = P("ens", None, "tile")
    return jax.shard_map(
        on_device, mesh=mesh, in_specs=in_specs, out_specs=out_specs, check_vma=False
    )
```

```python
import functools
import math

import jax
import jax.numpy as jnp
from jax import lax
from jax.experimental import pallas as pl
from jax.experimental.pallas import tpu as pltpu
from jax.sharding import PartitionSpec as P

MESH = pl.DeviceIdType.MESH
F32 = jnp.float32
BF16 = jnp.bfloat16
SIDE = 4
LOADS = 4


def tile_of(z, x, c):
    return (z * SIDE + x) * 2 + c


ORDER = (
    (0, 0), (0, 1), (0, 3), (3, 0), (1, 0), (0, 2), (3, 1), (1, 1),
    (3, 3), (1, 3), (3, 2), (1, 2), (2, 0), (2, 1), (2, 3), (2, 2),
)
ARRIVE = {
    1: (
        (0, 0, 3), (0, 0, 1), (1, 0, 3), (1, 0, 1),
        (0, 3, 0), (0, 1, 0), (1, 3, 0), (1, 1, 0),
    ),
    3: ((1, 0, 2),),
    5: ((0, 3, 3), (0, 1, 1), (0, 3, 1), (0, 1, 3), (1, 3, 1), (1, 1, 1)),
    7: ((1, 3, 3), (1, 1, 3)),
    8: ((0, 3, 2), (0, 1, 2)),
    9: ((1, 3, 2), (1, 1, 2)),
    10: ((1, 2, 0),),
    12: ((1, 2, 1),),
    13: ((1, 2, 3),),
    14: ((1, 2, 2),),
}
STEP_OF = {place: i for i, place in enumerate(ORDER)}
STEPS = len(ORDER)
LATE = (0, 1, 3, 2)


def exchange_kernel(
    factor,
    block_ref,
    count_ref,
    loc_vertical_ref,
    innov_ref,
    prec_ref,
    pert_hbm,
    control_hbm,
    horizontal_hbm,
    weight_hbm,
    vertical_hbm,
    out_ref,
    *scratch,
):
    rest = list(scratch)
    own = [[rest.pop(0) for _ in range(4)] for _ in range(4)]
    other = [[rest.pop(0) for _ in range(4)] for _ in range(4)]
    (
        pert,
        control,
        horizontal,
        localized,
        prev_ref,
        last_ref,
        weight,
        turned,
        vertical,
        sendy,
        recvy,
        picked,
        chain,
        adj_own,
        adj_other,
        core_in,
        total,
        half_in,
        row_in,
        plane,
        plane_in,
        unit,
        unit_b,
        unit_in,
        final,
        load_sem,
        ssem,
        rsem,
    ) = rest

    e = lax.axis_index("ens")
    t = lax.axis_index("tile")
    c = t % 2
    x = (t // 2) % SIDE
    z = t // (2 * SIDE)

    first_loads = []
    for n, (src, dst) in enumerate(
        ((control_hbm, control), (horizontal_hbm, horizontal), (pert_hbm, pert))
    ):
        copy = pltpu.make_async_copy(src, dst, load_sem.at[2 * LOADS + n])
        copy.start()
        first_loads.append(copy)
    slots = weight.shape[0]
    chunk = slots // LOADS
    loads = []
    for n, (src, dst) in enumerate(((weight_hbm, weight), (vertical_hbm, vertical))):
        for i in range(LOADS):
            at = pl.ds(i * chunk, chunk)
            copy = pltpu.make_async_copy(src.at[at], dst.at[at], load_sem.at[n * LOADS + i])
            copy.start()
            loads.append(copy)

    def beside(zq, xq):
        return tile_of((z + zq) % SIDE, (x + xq) % SIDE, c)

    y_dev = {q: ((e + q) % SIDE, t) for q in (1, 2, 3)}
    hi_dev = {q: (e, jnp.where(c == 0, beside(q, 0), beside(0, q))) for q in (1, 3)}
    lo_dev = {q: (e, jnp.where(c == 0, beside(0, q), beside(q, 0))) for q in (1, 2, 3)}
    core_dev = (e, tile_of(z, x, 1 - c))

    def slot_tile(core, r, rho):
        hi = (jnp.where(core == 0, z, x) + r) % SIDE
        lo = (jnp.where(core == 0, x, z) + rho) % SIDE
        return jnp.where(core == 0, tile_of(hi, lo, 0), tile_of(lo, hi, 1))

    barrier = pltpu.get_barrier_semaphore()
    greet = [*y_dev.values(), *hi_dev.values(), *lo_dev.values(), core_dev]
    for dev in greet:
        pl.semaphore_signal(barrier, inc=1, device_id=dev, device_id_type=MESH)
    ways = {}

    def way(name, src, dst, dev):
        ways[name] = (len(ways), src, dst, dev)

    def copy_of(name):
        n, src, dst, dev = ways[name]
        return pltpu.make_async_remote_copy(
            src_ref=src,
            dst_ref=dst,
            send_sem=ssem.at[n],
            recv_sem=rsem.at[n],
            device_id=dev,
            device_id_type=MESH,
        )

    def go(*names):
        for name in names:
            copy_of(name).start()

    def got(*names):
        for name in names:
            copy_of(name).wait_recv()

    low, high = pl.ds(0, 4), pl.ds(4, 4)
    for i, (r, rho) in enumerate(ORDER):
        at = pl.ds(i * 8, 8)
        way(("D", i), adj_other.at[at], core_in.at[at], core_dev)
    mine = own[0][0].at[pl.ds(2 * e, 2)]
    for q in (1, 2, 3):
        way(("yr", q), sendy.at[q - 1], recvy.at[q - 1], y_dev[q])
        way(("yg", q), mine, mine, y_dev[q])
    for part, at in (("l", low), ("h", high)):
        way(("A", 3, part), own[0][0].at[at], own[0][3].at[at], lo_dev[1])
        way(("A", 1, part), own[0][0].at[at], own[0][1].at[at], lo_dev[3])
    way("A2a", own[0][3].at[low], own[0][2].at[low], lo_dev[1])
    way("A2b", own[0][1].at[high], own[0][2].at[high], lo_dev[3])
    for rho in range(4):
        for part, at in (("l", low), ("h", high)):
            way(("B", 3, rho, part), own[0][rho].at[at], own[3][rho].at[at], hi_dev[1])
            way(("B", 1, rho, part), own[0][rho].at[at], own[1][rho].at[at], hi_dev[3])
        way(("F", 0, rho), own[3][rho].at[low], own[2][rho].at[low], hi_dev[1])
        way(("F", 1, rho), own[1][rho].at[high], own[2][rho].at[high], hi_dev[3])
        for r in range(4):
            way(("C", r, rho), own[r][rho], other[r][rho], core_dev)

    def total_at(r, rho, first, count):
        return total.at[pl.ds(STEP_OF[r, rho] * 8 + first, count)]

    for rho in range(4):
        to_next, to_back = row_in.at[pl.ds(rho * 8, 8)], row_in.at[pl.ds(32 + rho * 8, 8)]
        way(("H", 0, rho), total_at(2, rho, 0, 4), half_in.at[pl.ds(rho * 4, 4)], hi_dev[1])
        way(("H", 1, rho), total_at(2, rho, 4, 4), half_in.at[pl.ds(16 + rho * 4, 4)], hi_dev[3])
        way(("R0u", rho), total_at(1, rho, 4, 4), row_in.at[pl.ds(rho * 8 + 4, 4)], hi_dev[1])
        way(("R0a", rho), total_at(1, rho, 0, 4), row_in.at[pl.ds(rho * 8, 4)], hi_dev[1])
        way(("R1u", rho), total_at(3, rho, 0, 4), row_in.at[pl.ds(32 + rho * 8, 4)], hi_dev[3])
        way(("R1a", rho), total_at(3, rho, 4, 4), row_in.at[pl.ds(32 + rho * 8 + 4, 4)], hi_dev[3])
    for q in range(4):
        at = 2 * ((e + q) % SIDE)
        way(("L2", q), plane.at[pl.ds(16 + at, 2)], plane_in.at[pl.ds(8 + at, 2)], lo_dev[2])
    for rho in (1, 3):
        way(("L", rho), plane.at[pl.ds(rho * 8, 8)], plane_in.at[pl.ds((rho - 1) * 8, 8)], lo_dev[rho])
    done = final.at[pl.ds(2 * e, 2)]
    for q in (1, 2, 3):
        way(("ur", q), unit_b.at[pl.ds(2 * ((e + q) % SIDE), 2)], unit_in.at[q - 1], y_dev[q])
        way(("ug", q), done, done, y_dev[q])

    def turn(first, count):
        def some(i, carry):
            for u in range(8):
                turned[i * 8 + u] = weight[i * 8 + u].T
            return carry

        lax.fori_loop(first // 8, (first + count) // 8, some, 0)

    def tables(j, carry):
        base = j * 8
        columns = [block_ref[base + p] for p in range(8)]
        for p in range(8):
            before = jnp.int32(8)
            for n in range(p):
                before = jnp.where(columns[n] == columns[p], n, before)
            prev_ref[base + p] = before
        for k in range(8):
            latest = jnp.int32(8)
            for n in range(8):
                latest = jnp.where(columns[n] == k, n, latest)
            last_ref[base + k] = latest
        return carry

    lv = loc_vertical_ref[...].astype(BF16)
    first_loads[0].wait()

    def one_member(k, carry):
        sum_ = jnp.dot(lv, control[k].astype(BF16), preferred_element_type=F32)
        localized[pl.ds(pl.multiple_of(k * 64, 64), 64), :] = sum_.astype(BF16)
        return carry

    lax.fori_loop(0, 8, one_member, 0)
    for load in first_loads[1:]:
        load.wait()

    def increment(q):
        at = pl.ds(pl.multiple_of((e + q) % SIDE * 256, 256), 256)
        spread = jnp.dot(localized[...], horizontal[:, at], preferred_element_type=F32)
        sum_ = pert[0, :, at].astype(F32) * spread[:64]
        for k in range(1, 8):
            sum_ = sum_ + pert[k, :, at].astype(F32) * spread[k * 64 : (k + 1) * 64]
        return sum_ * factor

    for n, q in enumerate((2, 1, 3)):
        sum_ = increment(q)
        for h in range(2):
            sendy[q - 1, h] = sum_[:, h * 128 : (h + 1) * 128].astype(BF16)
        if n == 0:
            pl.semaphore_wait(barrier, len(greet))
        go(("yr", q))
    whole = increment(0)
    got(("yr", 1), ("yr", 3), ("yr", 2))
    for h in range(2):
        half = whole[:, h * 128 : (h + 1) * 128]
        for q in range(3):
            half = half + recvy[q, h].astype(F32)
        own[0][0][2 * e + h] = half.astype(BF16)
    go(("yg", 2), ("yg", 1), ("yg", 3))
    lax.fori_loop(0, slots // 8, tables, 0)
    for load in loads[:LOADS]:
        load.wait()
    turn(0, slots // 2)
    got(("yg", 1), ("yg", 3), ("yg", 2))
    go(("A", 3, "l"), ("A", 1, "h"), ("A", 3, "h"), ("A", 1, "l"))
    go(("B", 3, 0, "l"), ("B", 1, 0, "h"), ("C", 0, 0), ("B", 3, 0, "h"), ("B", 1, 0, "l"))
    turn(slots // 2, slots // 2)
    for load in loads[LOADS:]:
        load.wait()
    for f in range(2):
        chain[f * 9 + 8] = jnp.zeros((64, 128), F32)

    def forward(r, rho):
        if r == 0:
            if rho == 3:
                got(("A", 3, "l"))
                go("A2a", ("B", 3, 3, "l"))
            else:
                got(("A", 1, "h"))
                go("A2b", ("B", 1, 1, "h"))
        else:
            got(("B", r, rho, "l" if r == 3 else "h"))
            go(("F", 0 if r == 3 else 1, rho))

    def complete(r, rho):
        if r == 0 and rho == 2:
            got("A2a")
            go(("B", 3, 2, "l"))
            got("A2b")
            go(("B", 1, 2, "h"), ("B", 1, 2, "l"), ("B", 3, 2, "h"))
        elif r == 0 and rho == 3:
            got(("A", 3, "h"))
            go(("B", 1, 3, "h"), ("B", 3, 3, "h"), ("B", 1, 3, "l"))
        elif r == 0:
            got(("A", 1, "l"))
            go(("B", 3, 1, "l"), ("B", 1, 1, "l"), ("B", 3, 1, "h"))
        elif r == 2:
            got(("F", 0, rho), ("F", 1, rho))
        else:
            got(("B", r, rho, "h" if r == 3 else "l"))
        go(("C", r, rho))

    def event(i):
        if i >= 2 and ORDER[i - 2][0] == 2:
            rho = ORDER[i - 2][1]
            go(("H", 0, rho), ("H", 1, rho))
        for whole_tile, r, rho in ARRIVE.get(i, ()):
            (complete if whole_tile else forward)(r, rho)
        if i >= 2 and ORDER[i - 2][0] in (1, 3):
            go(("R0u" if ORDER[i - 2][0] == 1 else "R1u", ORDER[i - 2][1]))
        if i < STEPS:
            r, rho = ORDER[i]
            got(("C", r, rho))
            for f, refs in ((0, own), (1, other)):
                base = slot_tile(c if f == 0 else 1 - c, r, rho) * 8
                for p in range(8):
                    picked[f * 8 + p] = refs[r][rho][block_ref[base + p]]

    def dispatch(i, first, last):
        if last - first == 1:
            event(first)
            return
        middle = (first + last) // 2

        @pl.when(i < middle)
        def _():
            dispatch(i, first, middle)

        @pl.when(i >= middle)
        def _():
            dispatch(i, middle, last)

    def add_core(i):
        pltpu.make_async_remote_copy(
            src_ref=adj_other.at[pl.ds(i * 8, 8)],
            dst_ref=core_in.at[pl.ds(i * 8, 8)],
            send_sem=ssem.at[i],
            recv_sem=rsem.at[i],
            device_id=core_dev,
            device_id_type=MESH,
        ).wait_recv()
        for k in range(8):
            both = adj_own[i * 8 + k].astype(F32) + core_in[i * 8 + k].astype(F32)
            total[i * 8 + k] = both.astype(BF16)

    def step(i, carry):
        @pl.when(i >= 2)
        def _():
            add_core(i - 2)

        dispatch(i, 0, STEPS)
        r, rho = jnp.int32(0), jnp.int32(0)
        for n, (rn, rhon) in enumerate(ORDER):
            r = jnp.where(i == n, rn, r)
            rho = jnp.where(i == n, rhon, rho)
        pairs = []
        for f in range(2):
            tile = slot_tile(c if f == 0 else 1 - c, r, rho)
            pairs.append((f, tile, pl.multiple_of(tile * 8, 8)))
        both = [(f, tile, base, p) for f, tile, base in pairs for p in range(8)]
        innov = [innov_ref[pl.ds(base, 8), :] for _, _, base in pairs]
        prec = [prec_ref[pl.ds(base, 8), :] for _, _, base in pairs]
        projs = [
            jnp.dot(picked[f * 8 + p], turned[base + p], preferred_element_type=F32)
            for f, tile, base, p in both
        ]
        deps = []
        for f, tile, base, p in both:
            model = jnp.sum(vertical[base + p] * projs[f * 8 + p], axis=0, keepdims=True)
            dep = prec[f][p : p + 1] * (model - innov[f][p : p + 1])
            deps.append(jnp.where(p < count_ref[tile], dep, 0.0))
        backs = []
        for f, tile, base, p in both:
            weighted = (vertical[base + p] * deps[f * 8 + p]).astype(BF16)
            backs.append(jnp.dot(weighted, weight[base + p], preferred_element_type=F32))
        for f, tile, base, p in both:
            back = backs[f * 8 + p]
            if p > 0:
                back = back + chain[f * 9 + prev_ref[base + p]]
            chain[f * 9 + p] = back
        for f, tile, base in pairs:
            into = adj_own if f == 0 else adj_other
            for k in range(8):
                into[i * 8 + k] = chain[f * 9 + last_ref[base + k]].astype(BF16)
        pltpu.make_async_remote_copy(
            src_ref=adj_other.at[pl.ds(i * 8, 8)],
            dst_ref=core_in.at[pl.ds(i * 8, 8)],
            send_sem=ssem.at[i],
            recv_sem=rsem.at[i],
            device_id=core_dev,
            device_id_type=MESH,
        ).start()
        return carry

    lax.fori_loop(0, STEPS, step, 0)

    for i in (STEPS, STEPS + 1):
        add_core(i - 2)
        event(i)
    for rho in LATE:
        for d, r, first, name in ((0, 1, 0, "R0a"), (1, 3, 4, "R1a")):
            got(("H", d, rho))
            for b in range(4):
                at = STEP_OF[r, rho] * 8 + first + b
                sum_ = total[at].astype(F32) + half_in[d * 16 + rho * 4 + b].astype(F32)
                total[at] = sum_.astype(BF16)
            go((name, rho))
    for rho in (1, 3, 2, 0):
        got(("R0u", rho), ("R0a", rho), ("R1u", rho), ("R1a", rho))
        for k in range(8):
            sum_ = (
                total[STEP_OF[0, rho] * 8 + k].astype(F32)
                + row_in[rho * 8 + k].astype(F32)
                + row_in[32 + rho * 8 + k].astype(F32)
            )
            if rho == 0:
                unit[k] = sum_
            else:
                plane[rho * 8 + k] = sum_.astype(BF16)
        if rho == 2:
            go(*[("L2", q) for q in (2, 1, 3, 0)])
        elif rho != 0:
            go(("L", rho))
    got(("L", 1), ("L", 3))

    kept = []
    for q in (2, 1, 3, 0):
        got(("L2", q))
        for h in range(2):
            k = 2 * ((e + q) % SIDE) + h
            sum_ = unit[k]
            for n in range(3):
                sum_ = sum_ + plane_in[n * 8 + k].astype(F32)
            if q == 0:
                kept.append(sum_)
            else:
                unit_b[k] = sum_.astype(BF16)
        if q != 0:
            go(("ur", q))
    got(("ur", 1), ("ur", 3), ("ur", 2))
    for h in range(2):
        sum_ = kept[h]
        for q in range(3):
            sum_ = sum_ + unit_in[q, h].astype(F32)
        final[2 * e + h] = sum_.astype(BF16)
    go(("ug", 1), ("ug", 3), ("ug", 2))
    lv_t = loc_vertical_ref[...].T.astype(BF16)
    for q in (0, 1, 3, 2):
        if q > 0:
            got(("ug", (4 - q)))
        chunk_at = (e + q) % SIDE
        at = pl.ds(pl.multiple_of(chunk_at * 256, 256), 256)
        adjoint = jnp.concatenate(
            [final[2 * chunk_at].astype(F32), final[2 * chunk_at + 1].astype(F32)], axis=1
        )
        for k in range(8):
            field = pert[k, :, at].astype(F32) * adjoint
            sum_ = jnp.dot(lv_t, field.astype(BF16), preferred_element_type=F32)
            out_ref[k * 64 : (k + 1) * 64, at] = sum_.astype(BF16)
    for name in ways:
        copy_of(name).wait_send()


def exchange(
    factor,
    block_column,
    tile_count,
    loc_vertical,
    innovation,
    obs_precision,
    perturbations,
    control,
    loc_horizontal,
    obs_weight,
    obs_vertical,
):
    members, levels, columns = control.shape
    slots, block, _ = obs_weight.shape
    smem = pl.BlockSpec(memory_space=pltpu.SMEM)
    vmem = pl.BlockSpec(memory_space=pltpu.VMEM)
    hbm = pl.BlockSpec(memory_space=pl.ANY)

    def blocks(*lead, dtype=BF16):
        return pltpu.VMEM((*lead, levels, block), dtype)

    return pl.pallas_call(
        functools.partial(exchange_kernel, factor),
        out_shape=jax.ShapeDtypeStruct((members * levels, columns), BF16),
        in_specs=[smem] * 2 + [vmem] * 3 + [hbm] * 5,
        out_specs=vmem,
        scratch_shapes=[blocks(8) for _ in range(32)]
        + [
            pltpu.VMEM((members, levels, columns), BF16),
            pltpu.VMEM((members, levels, columns), F32),
            pltpu.VMEM((columns, columns), BF16),
            pltpu.VMEM((members * levels, columns), BF16),
            pltpu.SMEM((slots,), jnp.int32),
            pltpu.SMEM((slots,), jnp.int32),
            pltpu.VMEM((slots, block, block), BF16),
            pltpu.VMEM((slots, block, block), BF16),
            pltpu.VMEM((slots, levels, block), F32),
            blocks(3, 2),
            blocks(3, 2),
            blocks(16),
            blocks(18, dtype=F32),
            blocks(128),
            blocks(128),
            blocks(128),
            blocks(128),
            blocks(32),
            blocks(64),
            blocks(32),
            blocks(24),
            blocks(8, dtype=F32),
            blocks(8),
            blocks(3, 2),
            blocks(8),
            pltpu.SemaphoreType.DMA((2 * LOADS + 3,)),
            pltpu.SemaphoreType.DMA((128,)),
            pltpu.SemaphoreType.DMA((128,)),
        ],
        compiler_params=pltpu.CompilerParams(
            collective_id=0, has_side_effects=True, vmem_limit_bytes=56 * 1024 * 1024
        ),
    )(
        block_column,
        tile_count,
        loc_vertical,
        innovation,
        obs_precision,
        perturbations,
        control,
        loc_horizontal,
        obs_weight,
        obs_vertical,
    )


def on_device(
    perturbations,
    control,
    loc_vertical,
    loc_horizontal,
    obs_weight,
    obs_vertical,
    innovation,
    obs_precision,
    block_column,
    tile_count,
):
    members_dev, levels, columns = control.shape
    ens_total = lax.axis_size("ens")
    factor = 1.0 / math.sqrt(members_dev * ens_total - 1)
    back_vertical = exchange(
        factor,
        block_column,
        tile_count,
        loc_vertical,
        innovation,
        obs_precision,
        perturbations,
        control,
        loc_horizontal,
        obs_weight,
        obs_vertical,
    )
    spread_back = jnp.einsum(
        "rc,dc->rd", back_vertical, loc_horizontal, preferred_element_type=F32
    )
    flat_control = control.reshape(members_dev * levels, columns)
    return (flat_control + factor * spread_back).reshape(control.shape)


def solution(mesh):
    in_specs = (
        P("ens", None, "tile"),
        P("ens", None, "tile"),
        P(),
        P(),
        P(("ens", "tile"), None, None),
        P(("ens", "tile"), None, None),
        P(("ens", "tile"), None),
        P(("ens", "tile"), None),
        P(("ens", "tile")),
        P(("ens", "tile")),
    )
    out_specs = P("ens", None, "tile")
    return jax.shard_map(
        on_device, mesh=mesh, in_specs=in_specs, out_specs=out_specs, check_vma=False
    )
```

```python
import functools
import math

import jax
import jax.numpy as jnp
from jax import lax
from jax.experimental import pallas as pl
from jax.experimental.pallas import tpu as pltpu
from jax.sharding import PartitionSpec as P

MESH = pl.DeviceIdType.MESH
F32 = jnp.float32
BF16 = jnp.bfloat16
SIDE = 4
LOADS = 4


def tile_of(z, x, c):
    return (z * SIDE + x) * 2 + c


ORDER = (
    (0, 0), (0, 1), (0, 3), (3, 0), (1, 0), (0, 2), (3, 1), (1, 1),
    (3, 3), (1, 3), (3, 2), (1, 2), (2, 0), (2, 1), (2, 3), (2, 2),
)
ARRIVE = {
    1: ((0, 0, 3), (0, 0, 1), (1, 0, 3), (1, 0, 1), (0, 3, 0), (0, 1, 0), (1, 3, 0), (1, 1, 0)),
    4: ((1, 0, 2),),
    5: ((0, 3, 3), (0, 1, 1), (0, 3, 1), (0, 1, 3), (1, 3, 1), (1, 1, 1)),
    7: ((1, 3, 3), (1, 1, 3)),
    9: ((0, 3, 2), (0, 1, 2), (1, 3, 2), (1, 1, 2)),
    11: ((1, 2, 0),),
    12: ((1, 2, 1),),
    13: ((1, 2, 3),),
    14: ((1, 2, 2),),
}
STEP_OF = {place: i for i, place in enumerate(ORDER)}
STEPS = len(ORDER)
LATE = (0, 1, 3, 2)


def exchange_kernel(
    factor,
    block_ref,
    count_ref,
    loc_vertical_ref,
    innov_ref,
    prec_ref,
    pert_hbm,
    control_hbm,
    horizontal_hbm,
    weight_hbm,
    vertical_hbm,
    out_ref,
    *scratch,
):
    rest = list(scratch)
    own = [[rest.pop(0) for _ in range(4)] for _ in range(4)]
    other = [[rest.pop(0) for _ in range(4)] for _ in range(4)]
    (
        pert,
        control,
        horizontal,
        localized,
        prev_ref,
        last_ref,
        weight,
        turned,
        vertical,
        sendy,
        recvy,
        picked,
        chain,
        adj_own,
        adj_other,
        core_in,
        total,
        half_in,
        row_in,
        plane,
        plane_in,
        unit,
        unit_b,
        unit_in,
        final,
        load_sem,
        ssem,
        rsem,
    ) = rest

    e = lax.axis_index("ens")
    t = lax.axis_index("tile")
    c = t % 2
    x = (t // 2) % SIDE
    z = t // (2 * SIDE)

    first_loads = []
    for n, (src, dst) in enumerate(
        ((control_hbm, control), (horizontal_hbm, horizontal), (pert_hbm, pert))
    ):
        copy = pltpu.make_async_copy(src, dst, load_sem.at[2 * LOADS + n])
        copy.start()
        first_loads.append(copy)
    slots = weight.shape[0]
    chunk = slots // LOADS
    loads = []
    for n, (src, dst) in enumerate(((weight_hbm, weight), (vertical_hbm, vertical))):
        for i in range(LOADS):
            at = pl.ds(i * chunk, chunk)
            copy = pltpu.make_async_copy(src.at[at], dst.at[at], load_sem.at[n * LOADS + i])
            copy.start()
            loads.append(copy)

    def beside(zq, xq):
        return tile_of((z + zq) % SIDE, (x + xq) % SIDE, c)

    y_dev = {q: ((e + q) % SIDE, t) for q in (1, 2, 3)}
    hi_dev = {q: (e, jnp.where(c == 0, beside(q, 0), beside(0, q))) for q in (1, 3)}
    lo_dev = {q: (e, jnp.where(c == 0, beside(0, q), beside(q, 0))) for q in (1, 2, 3)}
    core_dev = (e, tile_of(z, x, 1 - c))

    def slot_tile(core, r, rho):
        hi = (jnp.where(core == 0, z, x) + r) % SIDE
        lo = (jnp.where(core == 0, x, z) + rho) % SIDE
        return jnp.where(core == 0, tile_of(hi, lo, 0), tile_of(lo, hi, 1))

    barrier = pltpu.get_barrier_semaphore()
    greet = [*y_dev.values(), *hi_dev.values(), *lo_dev.values(), core_dev]
    for dev in greet:
        pl.semaphore_signal(barrier, inc=1, device_id=dev, device_id_type=MESH)
    ways = {}

    def way(name, src, dst, dev):
        ways[name] = (len(ways), src, dst, dev)

    def copy_of(name):
        n, src, dst, dev = ways[name]
        return pltpu.make_async_remote_copy(
            src_ref=src,
            dst_ref=dst,
            send_sem=ssem.at[n],
            recv_sem=rsem.at[n],
            device_id=dev,
            device_id_type=MESH,
        )

    def go(*names):
        for name in names:
            copy_of(name).start()

    def got(*names):
        for name in names:
            copy_of(name).wait_recv()

    low, high = pl.ds(0, 4), pl.ds(4, 4)
    for i, (r, rho) in enumerate(ORDER):
        at = pl.ds(i * 8, 8)
        way(("D", i), adj_other.at[at], core_in.at[at], core_dev)
    mine = own[0][0].at[pl.ds(2 * e, 2)]
    for q in (1, 2, 3):
        way(("yr", q), sendy.at[q - 1], recvy.at[q - 1], y_dev[q])
        way(("yg", q), mine, mine, y_dev[q])
    for part, at in (("l", low), ("h", high)):
        way(("A", 3, part), own[0][0].at[at], own[0][3].at[at], lo_dev[1])
        way(("A", 1, part), own[0][0].at[at], own[0][1].at[at], lo_dev[3])
    way("A2a", own[0][3].at[low], own[0][2].at[low], lo_dev[1])
    way("A2b", own[0][1].at[high], own[0][2].at[high], lo_dev[3])
    for rho in range(4):
        for part, at in (("l", low), ("h", high)):
            way(("B", 3, rho, part), own[0][rho].at[at], own[3][rho].at[at], hi_dev[1])
            way(("B", 1, rho, part), own[0][rho].at[at], own[1][rho].at[at], hi_dev[3])
        way(("F", 0, rho), own[3][rho].at[low], own[2][rho].at[low], hi_dev[1])
        way(("F", 1, rho), own[1][rho].at[high], own[2][rho].at[high], hi_dev[3])
        for r in range(4):
            way(("C", r, rho), own[r][rho], other[r][rho], core_dev)

    def total_at(r, rho, first, count):
        return total.at[pl.ds(STEP_OF[r, rho] * 8 + first, count)]

    for rho in range(4):
        to_next, to_back = row_in.at[pl.ds(rho * 8, 8)], row_in.at[pl.ds(32 + rho * 8, 8)]
        way(("H", 0, rho), total_at(2, rho, 0, 4), half_in.at[pl.ds(rho * 4, 4)], hi_dev[1])
        way(("H", 1, rho), total_at(2, rho, 4, 4), half_in.at[pl.ds(16 + rho * 4, 4)], hi_dev[3])
        way(("R0u", rho), total_at(1, rho, 4, 4), row_in.at[pl.ds(rho * 8 + 4, 4)], hi_dev[1])
        way(("R0a", rho), total_at(1, rho, 0, 4), row_in.at[pl.ds(rho * 8, 4)], hi_dev[1])
        way(("R1u", rho), total_at(3, rho, 0, 4), row_in.at[pl.ds(32 + rho * 8, 4)], hi_dev[3])
        way(("R1a", rho), total_at(3, rho, 4, 4), row_in.at[pl.ds(32 + rho * 8 + 4, 4)], hi_dev[3])
    for q in range(4):
        at = 2 * ((e + q) % SIDE)
        way(("L2", q), plane.at[pl.ds(16 + at, 2)], plane_in.at[pl.ds(8 + at, 2)], lo_dev[2])
    for rho in (1, 3):
        way(("L", rho), plane.at[pl.ds(rho * 8, 8)], plane_in.at[pl.ds((rho - 1) * 8, 8)], lo_dev[rho])
    done = final.at[pl.ds(2 * e, 2)]
    for q in (1, 2, 3):
        way(("ur", q), unit_b.at[pl.ds(2 * ((e + q) % SIDE), 2)], unit_in.at[q - 1], y_dev[q])
        way(("ug", q), done, done, y_dev[q])

    def turn(first, count):
        def some(i, carry):
            for u in range(8):
                turned[i * 8 + u] = weight[i * 8 + u].T
            return carry

        lax.fori_loop(first // 8, (first + count) // 8, some, 0)

    def tables(j, carry):
        base = j * 8
        columns = [block_ref[base + p] for p in range(8)]
        for p in range(8):
            before = jnp.int32(8)
            for n in range(p):
                before = jnp.where(columns[n] == columns[p], n, before)
            prev_ref[base + p] = before
        for k in range(8):
            latest = jnp.int32(8)
            for n in range(8):
                latest = jnp.where(columns[n] == k, n, latest)
            last_ref[base + k] = latest
        return carry

    lv = loc_vertical_ref[...].astype(BF16)
    first_loads[0].wait()

    def one_member(k, carry):
        sum_ = jnp.dot(lv, control[k].astype(BF16), preferred_element_type=F32)
        localized[pl.ds(pl.multiple_of(k * 64, 64), 64), :] = sum_.astype(BF16)
        return carry

    lax.fori_loop(0, 8, one_member, 0)
    for load in first_loads[1:]:
        load.wait()

    def increment(q):
        at = pl.ds(pl.multiple_of((e + q) % SIDE * 256, 256), 256)
        spread = jnp.dot(localized[...], horizontal[:, at], preferred_element_type=F32)
        sum_ = pert[0, :, at].astype(F32) * spread[:64]
        for k in range(1, 8):
            sum_ = sum_ + pert[k, :, at].astype(F32) * spread[k * 64 : (k + 1) * 64]
        return sum_ * factor

    for n, q in enumerate((2, 1, 3)):
        sum_ = increment(q)
        for h in range(2):
            sendy[q - 1, h] = sum_[:, h * 128 : (h + 1) * 128].astype(BF16)
        if n == 0:
            pl.semaphore_wait(barrier, len(greet))
        go(("yr", q))
    whole = increment(0)
    got(("yr", 1), ("yr", 3), ("yr", 2))
    for h in range(2):
        half = whole[:, h * 128 : (h + 1) * 128]
        for q in range(3):
            half = half + recvy[q, h].astype(F32)
        own[0][0][2 * e + h] = half.astype(BF16)
    go(("yg", 2), ("yg", 1), ("yg", 3))
    lax.fori_loop(0, slots // 8, tables, 0)
    for load in loads[:LOADS]:
        load.wait()
    turn(0, slots // 2)
    got(("yg", 1), ("yg", 3), ("yg", 2))
    go(("A", 3, "l"), ("A", 1, "h"), ("A", 3, "h"), ("A", 1, "l"))
    go(("B", 3, 0, "l"), ("B", 1, 0, "h"), ("C", 0, 0), ("B", 3, 0, "h"), ("B", 1, 0, "l"))
    turn(slots // 2, slots // 2)
    for load in loads[LOADS:]:
        load.wait()
    for f in range(2):
        chain[f * 9 + 8] = jnp.zeros((64, 128), F32)

    def forward(r, rho):
        if r == 0:
            if rho == 3:
                got(("A", 3, "l"))
                go("A2a", ("B", 3, 3, "l"))
            else:
                got(("A", 1, "h"))
                go("A2b", ("B", 1, 1, "h"))
        else:
            got(("B", r, rho, "l" if r == 3 else "h"))
            go(("F", 0 if r == 3 else 1, rho))

    def complete(r, rho):
        if r == 0 and rho == 2:
            got("A2a")
            go(("B", 3, 2, "l"))
            got("A2b")
            go(("B", 1, 2, "h"), ("B", 1, 2, "l"), ("B", 3, 2, "h"))
        elif r == 0 and rho == 3:
            got(("A", 3, "h"))
            go(("B", 1, 3, "h"), ("B", 3, 3, "h"), ("B", 1, 3, "l"))
        elif r == 0:
            got(("A", 1, "l"))
            go(("B", 3, 1, "l"), ("B", 1, 1, "l"), ("B", 3, 1, "h"))
        elif r == 2:
            got(("F", 0, rho), ("F", 1, rho))
        else:
            got(("B", r, rho, "h" if r == 3 else "l"))
        go(("C", r, rho))

    def event(i):
        if i >= 2 and ORDER[i - 2][0] == 2:
            rho = ORDER[i - 2][1]
            go(("H", 0, rho), ("H", 1, rho))
        for whole_tile, r, rho in ARRIVE.get(i, ()):
            (complete if whole_tile else forward)(r, rho)
        if i >= 2 and ORDER[i - 2][0] in (1, 3):
            go(("R0u" if ORDER[i - 2][0] == 1 else "R1u", ORDER[i - 2][1]))
        if i < STEPS:
            r, rho = ORDER[i]
            got(("C", r, rho))
            for f, refs in ((0, own), (1, other)):
                base = slot_tile(c if f == 0 else 1 - c, r, rho) * 8
                for p in range(8):
                    picked[f * 8 + p] = refs[r][rho][block_ref[base + p]]

    def dispatch(i, first, last):
        if last - first == 1:
            event(first)
            return
        middle = (first + last) // 2

        @pl.when(i < middle)
        def _():
            dispatch(i, first, middle)

        @pl.when(i >= middle)
        def _():
            dispatch(i, middle, last)

    def add_core(i):
        pltpu.make_async_remote_copy(
            src_ref=adj_other.at[pl.ds(i * 8, 8)],
            dst_ref=core_in.at[pl.ds(i * 8, 8)],
            send_sem=ssem.at[i],
            recv_sem=rsem.at[i],
            device_id=core_dev,
            device_id_type=MESH,
        ).wait_recv()
        for k in range(8):
            both = adj_own[i * 8 + k].astype(F32) + core_in[i * 8 + k].astype(F32)
            total[i * 8 + k] = both.astype(BF16)

    def step(i, carry):
        @pl.when(i >= 2)
        def _():
            add_core(i - 2)

        dispatch(i, 0, STEPS)
        r, rho = jnp.int32(0), jnp.int32(0)
        for n, (rn, rhon) in enumerate(ORDER):
            r = jnp.where(i == n, rn, r)
            rho = jnp.where(i == n, rhon, rho)
        pairs = []
        for f in range(2):
            tile = slot_tile(c if f == 0 else 1 - c, r, rho)
            pairs.append((f, tile, pl.multiple_of(tile * 8, 8)))
        both = [(f, tile, base, p) for f, tile, base in pairs for p in range(8)]
        innov = [innov_ref[pl.ds(base, 8), :] for _, _, base in pairs]
        prec = [prec_ref[pl.ds(base, 8), :] for _, _, base in pairs]
        projs = [
            jnp.dot(picked[f * 8 + p], turned[base + p], preferred_element_type=F32)
            for f, tile, base, p in both
        ]
        deps = []
        for f, tile, base, p in both:
            model = jnp.sum(vertical[base + p] * projs[f * 8 + p], axis=0, keepdims=True)
            dep = prec[f][p : p + 1] * (model - innov[f][p : p + 1])
            deps.append(jnp.where(p < count_ref[tile], dep, 0.0))
        backs = []
        for f, tile, base, p in both:
            weighted = (vertical[base + p] * deps[f * 8 + p]).astype(BF16)
            backs.append(jnp.dot(weighted, weight[base + p], preferred_element_type=F32))
        for f, tile, base, p in both:
            back = backs[f * 8 + p]
            if p > 0:
                back = back + chain[f * 9 + prev_ref[base + p]]
            chain[f * 9 + p] = back
        for f, tile, base in pairs:
            into = adj_own if f == 0 else adj_other
            for k in range(8):
                into[i * 8 + k] = chain[f * 9 + last_ref[base + k]].astype(BF16)
        pltpu.make_async_remote_copy(
            src_ref=adj_other.at[pl.ds(i * 8, 8)],
            dst_ref=core_in.at[pl.ds(i * 8, 8)],
            send_sem=ssem.at[i],
            recv_sem=rsem.at[i],
            device_id=core_dev,
            device_id_type=MESH,
        ).start()
        return carry

    lax.fori_loop(0, STEPS, step, 0)

    for i in (STEPS, STEPS + 1):
        add_core(i - 2)
        event(i)
    for rho in LATE:
        for d, r, first, name in ((0, 1, 0, "R0a"), (1, 3, 4, "R1a")):
            got(("H", d, rho))
            for b in range(4):
                at = STEP_OF[r, rho] * 8 + first + b
                sum_ = total[at].astype(F32) + half_in[d * 16 + rho * 4 + b].astype(F32)
                total[at] = sum_.astype(BF16)
            go((name, rho))
    for rho in (1, 3, 2, 0):
        got(("R0u", rho), ("R0a", rho), ("R1u", rho), ("R1a", rho))
        for k in range(8):
            sum_ = (
                total[STEP_OF[0, rho] * 8 + k].astype(F32)
                + row_in[rho * 8 + k].astype(F32)
                + row_in[32 + rho * 8 + k].astype(F32)
            )
            if rho == 0:
                unit[k] = sum_
            else:
                plane[rho * 8 + k] = sum_.astype(BF16)
        if rho == 2:
            go(*[("L2", q) for q in (2, 1, 3, 0)])
        elif rho != 0:
            go(("L", rho))
    got(("L", 1), ("L", 3))

    kept = []
    for q in (2, 1, 3, 0):
        got(("L2", q))
        for h in range(2):
            k = 2 * ((e + q) % SIDE) + h
            sum_ = unit[k]
            for n in range(3):
                sum_ = sum_ + plane_in[n * 8 + k].astype(F32)
            if q == 0:
                kept.append(sum_)
            else:
                unit_b[k] = sum_.astype(BF16)
        if q != 0:
            go(("ur", q))
    got(("ur", 1), ("ur", 3), ("ur", 2))
    for h in range(2):
        sum_ = kept[h]
        for q in range(3):
            sum_ = sum_ + unit_in[q, h].astype(F32)
        final[2 * e + h] = sum_.astype(BF16)
    go(("ug", 1), ("ug", 3), ("ug", 2))
    lv_t = loc_vertical_ref[...].T.astype(BF16)
    for q in (0, 1, 3, 2):
        if q > 0:
            got(("ug", (4 - q)))
        chunk_at = (e + q) % SIDE
        at = pl.ds(pl.multiple_of(chunk_at * 256, 256), 256)
        adjoint = jnp.concatenate(
            [final[2 * chunk_at].astype(F32), final[2 * chunk_at + 1].astype(F32)], axis=1
        )
        for k in range(8):
            field = pert[k, :, at].astype(F32) * adjoint
            sum_ = jnp.dot(lv_t, field.astype(BF16), preferred_element_type=F32)
            out_ref[k * 64 : (k + 1) * 64, at] = sum_.astype(BF16)
    for name in ways:
        copy_of(name).wait_send()


def exchange(
    factor,
    block_column,
    tile_count,
    loc_vertical,
    innovation,
    obs_precision,
    perturbations,
    control,
    loc_horizontal,
    obs_weight,
    obs_vertical,
):
    members, levels, columns = control.shape
    slots, block, _ = obs_weight.shape
    smem = pl.BlockSpec(memory_space=pltpu.SMEM)
    vmem = pl.BlockSpec(memory_space=pltpu.VMEM)
    hbm = pl.BlockSpec(memory_space=pl.ANY)

    def blocks(*lead, dtype=BF16):
        return pltpu.VMEM((*lead, levels, block), dtype)

    return pl.pallas_call(
        functools.partial(exchange_kernel, factor),
        out_shape=jax.ShapeDtypeStruct((members * levels, columns), BF16),
        in_specs=[smem] * 2 + [vmem] * 3 + [hbm] * 5,
        out_specs=vmem,
        scratch_shapes=[blocks(8) for _ in range(32)]
        + [
            pltpu.VMEM((members, levels, columns), BF16),
            pltpu.VMEM((members, levels, columns), F32),
            pltpu.VMEM((columns, columns), BF16),
            pltpu.VMEM((members * levels, columns), BF16),
            pltpu.SMEM((slots,), jnp.int32),
            pltpu.SMEM((slots,), jnp.int32),
            pltpu.VMEM((slots, block, block), BF16),
            pltpu.VMEM((slots, block, block), BF16),
            pltpu.VMEM((slots, levels, block), F32),
            blocks(3, 2),
            blocks(3, 2),
            blocks(16),
            blocks(18, dtype=F32),
            blocks(128),
            blocks(128),
            blocks(128),
            blocks(128),
            blocks(32),
            blocks(64),
            blocks(32),
            blocks(24),
            blocks(8, dtype=F32),
            blocks(8),
            blocks(3, 2),
            blocks(8),
            pltpu.SemaphoreType.DMA((2 * LOADS + 3,)),
            pltpu.SemaphoreType.DMA((128,)),
            pltpu.SemaphoreType.DMA((128,)),
        ],
        compiler_params=pltpu.CompilerParams(
            collective_id=0, has_side_effects=True, vmem_limit_bytes=56 * 1024 * 1024
        ),
    )(
        block_column,
        tile_count,
        loc_vertical,
        innovation,
        obs_precision,
        perturbations,
        control,
        loc_horizontal,
        obs_weight,
        obs_vertical,
    )


def spread_kernel(factor, control_ref, back_ref, horizontal_ref, out_ref):
    spread = lax.dot_general(
        back_ref[...],
        horizontal_ref[...],
        (((1,), (1,)), ((), ())),
        preferred_element_type=F32,
    )
    for k in range(control_ref.shape[0]):
        out_ref[k] = control_ref[k] + factor * spread[k * 64 : (k + 1) * 64]


def add_spread(factor, control, back_vertical, loc_horizontal):
    members, levels, columns = control.shape
    width = 512
    chunk = pl.BlockSpec((members, levels, width), lambda i: (0, 0, i))
    return pl.pallas_call(
        functools.partial(spread_kernel, factor),
        grid=(columns // width,),
        out_shape=jax.ShapeDtypeStruct(control.shape, F32),
        in_specs=[
            chunk,
            pl.BlockSpec(back_vertical.shape, lambda i: (0, 0)),
            pl.BlockSpec((width, columns), lambda i: (i, 0)),
        ],
        out_specs=chunk,
        compiler_params=pltpu.CompilerParams(vmem_limit_bytes=24 * 1024 * 1024),
    )(control, back_vertical, loc_horizontal)


def on_device(
    perturbations,
    control,
    loc_vertical,
    loc_horizontal,
    obs_weight,
    obs_vertical,
    innovation,
    obs_precision,
    block_column,
    tile_count,
):
    members_dev, levels, columns = control.shape
    ens_total = lax.axis_size("ens")
    factor = 1.0 / math.sqrt(members_dev * ens_total - 1)
    back_vertical = exchange(
        factor,
        block_column,
        tile_count,
        loc_vertical,
        innovation,
        obs_precision,
        perturbations,
        control,
        loc_horizontal,
        obs_weight,
        obs_vertical,
    )
    return add_spread(factor, control, back_vertical, loc_horizontal)


def solution(mesh):
    in_specs = (
        P("ens", None, "tile"),
        P("ens", None, "tile"),
        P(),
        P(),
        P(("ens", "tile"), None, None),
        P(("ens", "tile"), None, None),
        P(("ens", "tile"), None),
        P(("ens", "tile"), None),
        P(("ens", "tile")),
        P(("ens", "tile")),
    )
    out_specs = P("ens", None, "tile")
    return jax.shard_map(
        on_device, mesh=mesh, in_specs=in_specs, out_specs=out_specs, check_vma=False
    )
```
